32 devices in a mesh: ctx: 8 (over z, core), head: 4 (over y, x).
Axes of the slice: x: 2, y: 2, z: 4, core: 2. Of those that a mesh axis runs over, the one named last changes fastest.
Arguments:
- hidden: bfloat16 [2048, 2048], P('ctx'), may hold values from -6 to 6
- w_query: bfloat16 [2048, 2048], P('head'), may hold values from -0.125 to 0.125
- w_key: bfloat16 [2048, 2048], P('head'), may hold values from -0.125 to 0.125
- payload_projection_matrix: bfloat16 [2048, 4096], P('head'), may hold values from -0.125 to 0.125
- conv_weight: bfloat16 [4, 8192], replicated, may hold values from -3 to 3
- log_decay: float32 [32, 2048], P('head', 'ctx'), may hold values from -1.6 to 0
- beta_rate: float32 [32, 2048], P('head', 'ctx'), may hold values from 0 to 1
- norm_gain: float32 [128], replicated, may hold values from 0.25 to 1.75
- head_order: int32 [16], replicated, may hold values from 0 to 15, each once
- block_starts: int32 [8], P('ctx'), may hold values 0 or 1
Outputs:
- mixed: bfloat16 [2048, 4096], P('ctx', 'head')
The draws below stay inside these ranges and needn't reach their ends.
Inputs may be any that keep to these rules, and one draw needn't show every extreme that they name: Index j of the head axis serves serving key head j (logical key head head_order[j * 4]) and serving value heads 2j and 2j + 1.
All inputs are finite; a program needn't handle non-finite values. No bound on the sum of `block_starts` on one device may be relied on, other than what follows from the above.
Results may differ from the reference program's by a relative error of at most 0.0046.
Values may be sent and summed in bfloat16 or wider, within the bound.
No kernel may reach another device: no remote copies, remote signals or barrier semaphores. Data moves between devices by JAX's collectives and lax.ppermute only.
A program may use at most 128 MiB of HBM per device.

```python
import math
import jax
import jax.numpy as jnp
from jax import lax

D = 2048
HK = 16
VH = 32
DK = 128
VALUE_HEAD_SIZE = 128
KCONV = 4
GROUP = 64
TOK_DEV = 256
TOKENS = 2048
BLOCKS = 8


def head_speed(key):
    picks = jax.random.uniform(jax.random.fold_in(key, 101), (VH,), jnp.float32)
    share = 0.5
    return picks < share


def draw_log_decay(key, part):
    fast = head_speed(key)
    keys = jax.random.split(jax.random.fold_in(key, 7), 6)
    quick = jnp.exp(jax.random.uniform(keys[0], (VH,), jnp.float32, math.log(1.0 / 60.0), math.log(1.0 / 15.0)))
    lasting = jnp.exp(jax.random.uniform(keys[1], (VH,), jnp.float32, math.log(0.05), math.log(0.2))) / TOKENS
    base = jnp.where(fast, quick, lasting)
    per_block = jnp.exp(jax.random.uniform(keys[2], (VH, TOKENS // TOK_DEV), jnp.float32, math.log(0.5), math.log(2.0)))
    rough = jax.random.uniform(keys[3], (VH, TOKENS), jnp.float32, 0.5, 1.5)
    delta_writing_strength = base[:, None] * jnp.repeat(per_block, TOK_DEV, axis=1) * rough
    destination_slots = jax.random.randint(keys[4], (VH, 2), 0, TOKENS)
    forgetting_amounts = jax.random.uniform(keys[5], (VH, 2), jnp.float32, 0.2, 0.5)
    attention_lane_sites = jnp.arange(TOKENS)[None, None, :]
    forgetting_spike_multiplier = jnp.sum(jnp.where(attention_lane_sites == destination_slots[:, :, None], jnp.log(1.0 - forgetting_amounts)[:, :, None], 0.0), axis=1)
    return (forgetting_spike_multiplier - delta_writing_strength).astype(jnp.float32)


def draw_beta_rate(key, part):
    fast = head_speed(key)
    keys = jax.random.split(jax.random.fold_in(key, 13), 3)
    quick = jax.random.uniform(keys[0], (VH, TOKENS), jnp.float32, 0.2, 0.9)
    level = jnp.exp(jax.random.uniform(keys[1], (VH,), jnp.float32, math.log(0.2), math.log(0.8))) * DK / TOKENS
    slow = level[:, None] * jax.random.uniform(keys[2], (VH, TOKENS), jnp.float32, 0.5, 1.5)
    return jnp.where(fast[:, None], quick, slow).astype(jnp.float32)


def with_ends(values, own_key, least, largest):
    spot = [jax.random.randint(jax.random.fold_in(own_key, axis), (), 0, length) for axis, length in enumerate(values.shape)]
    longest = values.shape.index(max(values.shape))
    neighbour = spot[:longest] + [(spot[longest] + 1) % values.shape[longest]] + spot[longest + 1:]
    return values.at[tuple(spot)].set(least).at[tuple(neighbour)].set(largest)


def steps_of(key, shape, cuts, least, largest):
    level, own = 1.0, jax.random.fold_in(key, 6)
    for axis_at, blocks in cuts:
        draws = jnp.exp(jax.random.uniform(jax.random.fold_in(own, axis_at), (blocks,), jnp.float32, least / len(cuts), largest / len(cuts)))
        level = level * jnp.repeat(draws, shape[axis_at] // blocks).reshape([-1 if axis == axis_at else 1 for axis in range(len(shape))])
    return level


def normal_values(rng, extent, width, limit, shards=(), kind=jnp.bfloat16):
    drawn = jax.random.normal(rng, extent, jnp.float32) * width
    if len(shards) > 0:
        drawn = steps_of(rng, extent, shards, -0.22, 0.18) * drawn
    return jnp.clip(drawn, min=-limit, max=limit).astype(kind)


def setup_inputs(seed: int = 0) -> dict:
    arg_keys = jax.random.split(jax.random.key(seed), 11)
    return {
        "hidden": normal_values(arg_keys[0], (TOKENS, D), 1.0, 6.0, ((0, 8),)),
        "w_query": normal_values(arg_keys[1], (D, HK * DK), D ** -0.5, 0.125, ((0, 4),)),
        "w_key": normal_values(arg_keys[2], (D, HK * DK), D ** -0.5, 0.125, ((0, 4),)),
        "payload_projection_matrix": normal_values(arg_keys[3], (D, VH * VALUE_HEAD_SIZE), D ** -0.5, 0.125, ((0, 4),)),
        "conv_weight": normal_values(arg_keys[4], (KCONV, 2 * HK * DK + VH * VALUE_HEAD_SIZE), KCONV ** -0.5, 3.0),
        "log_decay": draw_log_decay(jax.random.fold_in(arg_keys[10], 71), 0),
        "beta_rate": draw_beta_rate(jax.random.fold_in(arg_keys[10], 71), 0),
        "norm_gain": jnp.clip(1.0 + 0.15 * jax.random.normal(arg_keys[7], (VALUE_HEAD_SIZE,), jnp.float32), 0.25, 1.75),
        "head_order": jax.random.permutation(arg_keys[8], HK).astype(jnp.int32),
        "block_starts": with_ends((jax.random.randint(arg_keys[9], (BLOCKS,), 0, 8) < 1).astype(jnp.int32), jax.random.fold_in(arg_keys[9], 1), 0, 1),
    }


HIGH_PRECISION = lax.Precision.HIGHEST
eps = 1e-06

def lower_solve(system, right):
    return lax.linalg.triangular_solve(system, right, left_side=True, lower=True, unit_diagonal=True)

def unit_rows(values):
    return values * lax.rsqrt(lax.optimization_barrier(jnp.sum(values * values, axis=-1, keepdims=True)) + eps)

def group_step(running_state, inputs):
    query_vector, key_vec, value, decay, delta_writing_strength, keep = inputs
    running_state = running_state * keep
    size_c = decay.shape[-1]
    cumulative_decay = jnp.cumsum(decay, axis=-1)
    rows = lax.broadcasted_iota(jnp.int32, (size_c, size_c), 0)
    cols = lax.broadcasted_iota(jnp.int32, (size_c, size_c), 1)
    spread = cumulative_decay[:, :, None] - cumulative_decay[:, None, :]
    strict_w = jnp.where(cols < rows, jnp.exp(jnp.where(cols < rows, spread, 0.0)), 0.0)
    incl_w = jnp.where(cols <= rows, jnp.exp(jnp.where(cols <= rows, spread, 0.0)), 0.0)
    key_key = jnp.einsum('htd,hsd->hts', key_vec, key_vec, precision=HIGH_PRECISION)
    system = jnp.eye(size_c, dtype=jnp.float32) + delta_writing_strength[:, :, None] * strict_w * key_key
    decay_growth = jnp.exp(cumulative_decay)
    right = jnp.concatenate([delta_writing_strength[:, :, None] * value, (delta_writing_strength * decay_growth)[:, :, None] * key_vec], axis=-1)
    solved_system = lower_solve(system, right)
    state_update = solved_system[:, :, :VALUE_HEAD_SIZE] - jnp.einsum('dmj,djz->dmz', solved_system[:, :, VALUE_HEAD_SIZE:], running_state, precision=HIGH_PRECISION)
    attend = incl_w * jnp.einsum('htd,hsd->hts', query_vector, key_vec, precision=HIGH_PRECISION)
    state_readout = decay_growth[:, :, None] * jnp.einsum('cwn,cnj->cwj', query_vector, running_state, precision=HIGH_PRECISION)
    state_readout = state_readout + jnp.einsum('hts,hsv->htv', attend, state_update, precision=HIGH_PRECISION)
    trailing_keys = jnp.exp(cumulative_decay[:, -1:] - cumulative_decay)[:, :, None] * key_vec
    running_state = jnp.exp(cumulative_decay[:, -1])[:, None, None] * running_state + jnp.einsum('lpj,lpm->ljm', trailing_keys, state_update, precision=HIGH_PRECISION)
    return (running_state, state_readout)

def reference(hidden, w_query, w_key, payload_projection_matrix, conv_weight, log_decay, beta_rate, norm_gain, head_order, block_starts):
    total = hidden.shape[0]
    attention_lane_sites = jnp.arange(total).astype(jnp.int32)
    starts_tok = block_starts[attention_lane_sites // TOK_DEV]
    first = attention_lane_sites % TOK_DEV
    groups = total // GROUP
    group_first = jnp.arange(groups).astype(jnp.int32) * GROUP
    group_flag = block_starts[group_first // TOK_DEV]
    keeps = jnp.where((group_first % TOK_DEV == 0) & (group_flag == 1), 0.0, 1.0).astype(jnp.float32)

    def one_head(serve):
        logical = head_order[serve]
        key_cols = (logical * DK + jnp.arange(DK)).astype(jnp.int32)
        value_cols = (logical * 2 * VALUE_HEAD_SIZE + jnp.arange(2 * VALUE_HEAD_SIZE)).astype(jnp.int32)
        weights = jnp.concatenate([jnp.take(w_query, key_cols, axis=1), jnp.take(w_key, key_cols, axis=1), jnp.take(payload_projection_matrix, value_cols, axis=1)], axis=1)
        taps = jnp.concatenate([jnp.take(conv_weight, key_cols, axis=1), jnp.take(conv_weight, HK * DK + key_cols, axis=1), jnp.take(conv_weight, 2 * HK * DK + value_cols, axis=1)], axis=1)
        proj = jnp.dot(hidden.astype(jnp.float32), weights.astype(jnp.float32), preferred_element_type=jnp.float32).astype(jnp.bfloat16)
        mixed_in = taps[KCONV - 1].astype(jnp.float32) * proj.astype(jnp.float32)
        for lag in range(1, KCONV):
            moved = jnp.concatenate([jnp.zeros((lag, proj.shape[1]), jnp.bfloat16), proj[:-lag]], axis=0)
            blocked = (first < lag) & (starts_tok == 1)
            moved = jnp.where(blocked[:, None], jnp.zeros_like(moved), moved)
            mixed_in = mixed_in + taps[KCONV - 1 - lag].astype(jnp.float32) * moved.astype(jnp.float32)
        active = jax.nn.silu(mixed_in)
        query_vector = unit_rows(active[:, :DK])
        key_vec = unit_rows(active[:, DK:2 * DK])
        value = active[:, 2 * DK:].reshape(total, 2, VALUE_HEAD_SIZE).transpose(1, 0, 2)
        query_vector = jnp.broadcast_to(query_vector[None], (2, total, DK))
        key_vec = jnp.broadcast_to(key_vec[None], (2, total, DK))
        decay = lax.dynamic_slice_in_dim(log_decay, 2 * serve, 2, axis=0)
        delta_writing_strength = lax.dynamic_slice_in_dim(beta_rate, 2 * serve, 2, axis=0)

        def blocks(values):
            return values.reshape(2, groups, GROUP, values.shape[-1]).transpose(1, 0, 2, 3)
        inputs = (blocks(query_vector), blocks(key_vec), blocks(value), decay.reshape(2, groups, GROUP).transpose(1, 0, 2), delta_writing_strength.reshape(2, groups, GROUP).transpose(1, 0, 2), keeps)
        start = jnp.zeros((2, DK, VALUE_HEAD_SIZE), jnp.float32)
        final, reads = lax.scan(group_step, start, inputs)
        reads = reads.transpose(0, 2, 1, 3).reshape(total, 2, VALUE_HEAD_SIZE)
        scaled = reads * lax.rsqrt(lax.optimization_barrier(jnp.mean(reads * reads, axis=-1, keepdims=True)) + eps) * norm_gain
        return scaled.reshape(total, 2 * VALUE_HEAD_SIZE).astype(jnp.bfloat16)
    outputs = lax.map(one_head, jnp.arange(HK).astype(jnp.int32))
    return outputs.transpose(1, 0, 2).reshape(total, VH * VALUE_HEAD_SIZE)
```

```python
import functools

import jax
import jax.numpy as jnp
from jax import lax
from jax.experimental import pallas as pl
from jax.experimental.pallas import tpu as pltpu
from jax.sharding import PartitionSpec as P

HEAD = 128
TAPS = 4
RIM = 16
EPS = 1e-06
VMEM_BYTES = 40 * 1024 * 1024
F32 = jnp.float32
BF16 = jnp.bfloat16

NN = (((1,), (0,)), ((), ()))
NT = (((1,), (1,)), ((), ()))


def dot1(a, b, dims=NN):
    return lax.dot_general(
        a.astype(BF16), b.astype(BF16), dims, preferred_element_type=F32
    )


def split(a):
    high = a.astype(BF16)
    return high, (a - high.astype(F32)).astype(BF16)


def dot3s(a, b, dims=NN):
    (ah, al), (bh, bl) = a, b
    one = functools.partial(lax.dot_general, dimension_numbers=dims, preferred_element_type=F32)
    return one(ah, bh) + (one(ah, bl) + one(al, bh))


def dot3(a, b, dims=NN):
    return dot3s(split(a), split(b), dims)


def dot_full(a, b, dims=NN):
    return lax.dot_general(
        a, b, dims, precision=lax.Precision.HIGHEST, preferred_element_type=F32
    )


def whole(array):
    zeros = (0,) * array.ndim
    return pl.BlockSpec(array.shape, lambda i, sp: zeros)


def call(body, sp, inputs, specs, outs, scratch=(), flops=10**7):
    return pl.pallas_call(
        body,
        grid_spec=pltpu.PrefetchScalarGridSpec(
            num_scalar_prefetch=1,
            grid=(1,),
            in_specs=specs,
            out_specs=[whole(out) for out in outs],
            scratch_shapes=list(scratch),
        ),
        out_shape=[jax.ShapeDtypeStruct(out.shape, out.dtype) for out in outs],
        compiler_params=pltpu.CompilerParams(vmem_limit_bytes=VMEM_BYTES),
        cost_estimate=pl.CostEstimate(flops=flops, bytes_accessed=2**20, transcendentals=0),
    )(sp, *inputs)


class Plan:
    def __init__(self, ranks, key_heads):
        bits = [1 << i for i in range(ranks.bit_length() - 1)]
        self.orders = (bits, bits[::-1])
        self.stages = len(bits)
        self.key_heads = key_heads

    def offsets(self, route, stage):
        out = [0]
        for bit in self.orders[route][stage + 1 :]:
            out = out + [o ^ bit for o in out]
        return out

    def weight_spec(self, rows, width, unit, head):
        heads = self.key_heads
        return pl.BlockSpec(
            (rows, width), lambda i, sp: (0, sp[2 + (sp[0] ^ unit) * heads + head])
        )

    def tap_spec(self, width, base, head):
        heads = self.key_heads
        return pl.BlockSpec(
            (TAPS, width), lambda i, sp: (0, base + sp[2 + sp[0] * heads + head])
        )


def hidden_spec(hidden, rows):
    return pl.BlockSpec((hidden.shape[0], rows), lambda i, sp: (0, sp[0]))


def send_stage(plan, stage, chunk, hidden, rim, weight, received, sp):
    rows, count = weight.shape[0], hidden.shape[0]
    width = chunk["width"]
    inputs, specs = [hidden, rim], [hidden_spec(hidden, rows), whole(rim)]
    jobs, outs, places = [], [], {}
    for route, heads in enumerate(chunk["heads"]):
        if not heads:
            continue
        offsets = plan.offsets(route, stage)
        for before in range(stage):
            places[route, before] = len(inputs)
            inputs.append(received[route][before])
            specs.append(whole(received[route][before]))
        for slot, offset in enumerate(offsets):
            unit = offset ^ plan.orders[route][stage]
            sources = [
                (places[route, before], plan.offsets(route, before).index(unit))
                for before in range(stage)
            ]
            for at, head in enumerate(heads):
                jobs.append((len(inputs), sources, len(outs), slot, at))
                inputs.append(weight)
                specs.append(plan.weight_spec(rows, width, unit, head))
        outs.append(
            jax.ShapeDtypeStruct((len(offsets), RIM + count, width * len(heads)), BF16)
        )
    total = len(inputs)

    def body(sp_ref, *refs):
        tokens, edge = refs[0][...], refs[1][...]
        for place, sources, out, slot, at in jobs:
            held = refs[place][...]
            cols = slice(at * width, (at + 1) * width)
            for left, span in ((edge, slice(0, RIM)), (tokens, slice(RIM, RIM + count))):
                part = jnp.dot(left, held, preferred_element_type=F32)
                for source, index in sources:
                    part = part + refs[source][index, span, cols].astype(F32)
                refs[total + out][slot, span, cols] = part.astype(BF16)

    sent = call(body, sp, inputs, specs, outs)
    result, at = [], 0
    for heads in chunk["heads"]:
        result.append(sent[at] if heads else None)
        at += 1 if heads else 0
    return result


def exchange(plan, stage, sent):
    ranks = lax.axis_size("head")
    return [
        None
        if part is None
        else lax.ppermute(
            part, "head", [(i, i ^ plan.orders[route][stage]) for i in range(ranks)]
        )
        for route, part in enumerate(sent)
    ]


def gather_specs(plan, chunk, heads, hidden, rim, weight, taps, base, received):
    rows, width = weight.shape[0], chunk["width"]
    inputs, specs = [hidden, rim], [hidden_spec(hidden, rows), whole(rim)]
    places, jobs = {}, []
    for head in heads:
        route = [head in group for group in chunk["heads"]].index(True)
        if route not in places:
            places[route] = []
            for part in received[route]:
                places[route].append(len(inputs))
                inputs.append(part)
                specs.append(pl.BlockSpec((1,) + part.shape[1:], lambda i, sp: (0, 0, 0)))
        at = chunk["heads"][route].index(head)
        jobs.append((len(inputs), places[route], slice(at * width, (at + 1) * width)))
        inputs += [weight, taps]
        specs += [plan.weight_spec(rows, width, 0, head), plan.tap_spec(width, base, head)]
    return inputs, specs, jobs


def activate(refs, job, scratch):
    place, sources, cols = job
    held, taps = refs[place][...], refs[place + 1][...].astype(F32)
    count = refs[0].shape[0]
    for left, span in ((refs[1], slice(0, RIM)), (refs[0], slice(RIM, RIM + count))):
        part = jnp.dot(left[...], held, preferred_element_type=F32)
        for source in sources:
            part = part + refs[source][0, span, cols].astype(F32)
        scratch[span, :] = part
    total = None
    for tap in range(TAPS):
        first = RIM - (TAPS - 1) + tap
        term = taps[tap : tap + 1] * scratch[first : first + count, :]
        total = term if total is None else total + term
    return total / (1.0 + jnp.exp(-total))


def unit_rows(values):
    return values * lax.rsqrt(jnp.sum(values * values, axis=-1, keepdims=True) + EPS)


def iotas(size):
    return (
        lax.broadcasted_iota(jnp.int32, (size, size), 0),
        lax.broadcasted_iota(jnp.int32, (size, size), 1),
    )


def running(decay):
    size = decay.shape[1]
    rows, cols = iotas(size)
    upper = (rows <= cols).astype(F32)
    lower = (cols <= rows).astype(F32)
    return dot_full(decay, upper), dot_full(lower, decay, NT)


def as_columns(values):
    rows, cols = iotas(values.shape[1])
    return dot_full((rows == cols).astype(F32), values, NT)


def inverses(systems):
    size = systems[0].shape[0]
    rows, cols = iotas(size)
    eye = (rows == cols).astype(F32)
    near = [jnp.where((rows >> 3) == (cols >> 3), low, 0.0) for low in systems]
    cut = [split(n) for n in near]
    square = [dot3s(c, c) for c in cut]
    cut2 = [split(s) for s in square]
    cube = [dot3s(c, c2) for c, c2 in zip(cut, cut2)]
    inv = [eye - n + s - c for n, s, c in zip(near, square, cube)]
    fourth = [split(dot3s(c2, c2)) for c2 in cut2]
    inv = [x + dot3s(split(x), f) for x, f in zip(inv, fourth)]
    shift = 3
    while (1 << shift) < size:
        inside = ((rows >> (shift + 1)) == (cols >> (shift + 1))) & (
            (rows >> shift) != (cols >> shift)
        )
        parts = [split(x) for x in inv]
        lower = [split(jnp.where(inside, low, 0.0)) for low in systems]
        middle = [split(dot3s(low, x)) for low, x in zip(lower, parts)]
        inv = [x - dot3s(p, m) for x, p, m in zip(inv, parts, middle)]
        shift += 1
    return inv


def key_phase(plan, chunk, heads, hidden, rim, weight, taps, base, received, decay, beta, sp):
    inputs, specs, jobs = gather_specs(
        plan, chunk, heads, hidden, rim, weight, taps, base, received
    )
    at = len(inputs)
    inputs += [decay, beta]
    specs += [whole(decay), whole(beta)]
    count, number = hidden.shape[0], 2 * len(heads)
    half = count // 2
    first = 2 * heads[0]
    outs = [
        jax.ShapeDtypeStruct((len(heads), count, HEAD), F32),
        jax.ShapeDtypeStruct((len(heads), HEAD, count), F32),
        jax.ShapeDtypeStruct((number, 3, half, half), F32),
        jax.ShapeDtypeStruct((number, count, HEAD), F32),
        jax.ShapeDtypeStruct((number, HEAD, HEAD), F32),
    ]
    total = len(inputs)

    def body(sp_ref, *refs):
        key_ref, turned_ref, solve_ref, write_ref, trans_ref, scratch = refs[total:]
        sums, sums_col = running(refs[at][...])
        beta_col = as_columns(refs[at + 1][...])
        rows, cols = iotas(half)
        keys, systems, crosses = [], [], []
        for i, job in enumerate(jobs):
            key = unit_rows(activate(refs, job, scratch))
            keys.append(key)
            key_ref[i] = key
            turned_ref[i] = key.T
            low, high = split(key[:half]), split(key[half:])
            alike = (dot3s(low, low, NT), dot3s(high, high, NT), dot3s(high, low, NT))
            for r in (first + 2 * i, first + 2 * i + 1):
                row, col, rate = sums[r : r + 1], sums_col[:, r : r + 1], beta_col[:, r : r + 1]
                for b, span in enumerate((slice(0, half), slice(half, count))):
                    fade = jnp.exp(jnp.minimum(col[span] - row[:, span], 0.0))
                    systems.append(jnp.where(cols < rows, rate[span] * fade * alike[b], 0.0))
                fade = jnp.exp(jnp.minimum(col[half:] - row[:, :half], 0.0))
                crosses.append(rate[half:] * fade * alike[2])
        solved = [split(x) for x in inverses(systems)]
        middle = [
            split(dot3s(split(c), solved[2 * j])) for j, c in enumerate(crosses)
        ]
        corner = [-dot3s(solved[2 * j + 1], m) for j, m in enumerate(middle)]
        keep = sp_ref[1].astype(F32)
        eye = (lax.broadcasted_iota(jnp.int32, (HEAD, HEAD), 0)
               == lax.broadcasted_iota(jnp.int32, (HEAD, HEAD), 1)).astype(F32)
        for j in range(number):
            r, key = first + j, keys[j // 2]
            row, col, rate = sums[r : r + 1], sums_col[:, r : r + 1], beta_col[:, r : r + 1]
            top, bottom, side = solved[2 * j], solved[2 * j + 1], split(corner[j])
            for place, part in enumerate((top, bottom, side)):
                solve_ref[j, place] = part[0].astype(F32) + part[1].astype(F32)
            right = (rate * jnp.exp(col)) * key
            right_low, right_high = split(right[:half]), split(right[half:])
            write_low = dot3s(top, right_low)
            write_high = dot3s(side, right_low) + dot3s(bottom, right_high)
            write_ref[j, :half] = write_low
            write_ref[j, half:] = write_high
            tail = jnp.exp(row[:, count - 1 :] - row)
            trailing = turned_ref[j // 2] * tail
            moved = dot3(trailing[:, :half], write_low) + dot3(trailing[:, half:], write_high)
            gone = jnp.exp(row[:, count - 1 :])
            trans_ref[j] = keep * (gone * eye - moved)

    return call(
        body, sp, inputs, specs, outs, [pltpu.VMEM((RIM + count, HEAD), F32)], flops=4 * 10**9
    )


def value_phase(
    plan, chunk, heads, hidden, rim, weight, taps, base, received, decay, beta, turned, solve, sp
):
    inputs, specs, jobs = gather_specs(
        plan, chunk, heads, hidden, rim, weight, taps, base, received
    )
    at = len(inputs)
    inputs += [decay, beta, turned, solve]
    specs += [whole(decay), whole(beta), whole(turned), whole(solve)]
    count, number = hidden.shape[0], 2 * len(heads)
    half = count // 2
    first = 2 * heads[0]
    outs = [
        jax.ShapeDtypeStruct((number, count, HEAD), F32),
        jax.ShapeDtypeStruct((number, HEAD, HEAD), F32),
    ]
    total = len(inputs)

    def body(sp_ref, *refs):
        write_ref, trans_ref, scratch = refs[total:]
        turned_ref, solve_ref = refs[at + 2], refs[at + 3]
        sums, _ = running(refs[at][...])
        beta_col = as_columns(refs[at + 1][...])
        for i, job in enumerate(jobs):
            values = activate(refs, job, scratch)
            for j in (2 * i, 2 * i + 1):
                r = first + j
                row, rate = sums[r : r + 1], beta_col[:, r : r + 1]
                right = rate * values[:, (j % 2) * HEAD : (j % 2 + 1) * HEAD]
                low, high = split(right[:half]), split(right[half:])
                write_low = dot3s(split(solve_ref[j, 0]), low)
                write_high = dot3s(split(solve_ref[j, 2]), low) + dot3s(
                    split(solve_ref[j, 1]), high
                )
                write_ref[j, :half] = write_low
                write_ref[j, half:] = write_high
                trailing = turned_ref[i] * jnp.exp(row[:, count - 1 :] - row)
                trans_ref[j] = dot3(trailing[:, :half], write_low) + dot3(
                    trailing[:, half:], write_high
                )

    return call(
        body, sp, inputs, specs, outs, [pltpu.VMEM((RIM + count, 2 * HEAD), F32)], flops=10**9
    )


def query_phase(
    plan, chunk, heads, hidden, rim, weight, taps, base, received, decay, keys, write_k, write_v, sp
):
    inputs, specs, jobs = gather_specs(
        plan, chunk, heads, hidden, rim, weight, taps, base, received
    )
    at = len(inputs)
    inputs += [decay, keys, write_k, write_v]
    specs += [whole(decay), whole(keys), whole(write_k), whole(write_v)]
    count, number = hidden.shape[0], 2 * len(heads)
    first = 2 * heads[0]
    outs = [
        jax.ShapeDtypeStruct((number, count, HEAD), F32),
        jax.ShapeDtypeStruct((number, count, HEAD), F32),
    ]
    total = len(inputs)

    def body(sp_ref, *refs):
        inner_ref, query_ref, scratch = refs[total:]
        key_ref, write_k_ref, write_v_ref = refs[at + 1 : at + 4]
        sums, sums_col = running(refs[at][...])
        rows, cols = iotas(count)
        for i, job in enumerate(jobs):
            query = unit_rows(activate(refs, job, scratch))
            alike = dot3(query, key_ref[i], NT)
            for j in (2 * i, 2 * i + 1):
                r = first + j
                row, col = sums[r : r + 1], sums_col[:, r : r + 1]
                fade = jnp.exp(jnp.minimum(col - row, 0.0))
                attend = jnp.where(cols <= rows, fade * alike, 0.0)
                attend = split(attend)
                inner_ref[j] = dot3s(attend, split(write_v_ref[j]))
                query_ref[j] = jnp.exp(col) * query - dot3s(attend, split(write_k_ref[j]))

    return call(
        body, sp, inputs, specs, outs, [pltpu.VMEM((RIM + count, HEAD), F32)], flops=10**9
    )


def join_pair(mine_a, mine_b, other_a, other_b, sp, place):
    number = mine_a.shape[0]
    half = number // 2
    inputs = [mine_a, mine_b, other_a, other_b]
    out = jax.ShapeDtypeStruct((2, half, HEAD, HEAD), BF16)

    def body(sp_ref, mine_a_ref, mine_b_ref, other_a_ref, other_b_ref, out_ref):
        core = sp_ref[place]
        for i in range(half):
            h = core * half + i
            pair = [
                (mine_a_ref[h], other_a_ref[h].astype(F32)),
                (mine_b_ref[h], other_b_ref[h].astype(F32)),
            ]
            early_a, early_b = [jnp.where(core == 0, p[0], p[1]) for p in pair]
            late_a, late_b = [jnp.where(core == 0, p[1], p[0]) for p in pair]
            late = split(late_a)
            out_ref[0, i] = dot3s(late, split(early_a)).astype(BF16)
            out_ref[1, i] = (dot3s(late, split(early_b)) + late_b).astype(BF16)

    return call(body, sp, inputs, [whole(a) for a in inputs], [out])[0]


def run_chain(parts, sp):
    half = parts[0].shape[1]
    out = jax.ShapeDtypeStruct((half, HEAD, HEAD), BF16)

    def body(sp_ref, *refs):
        for i in range(half):
            state = refs[0][1, i].astype(F32)
            for part in refs[1:-1]:
                high, low = split(state)
                left = part[0, i]
                state = (
                    jnp.dot(left, high, preferred_element_type=F32)
                    + jnp.dot(left, low, preferred_element_type=F32)
                    + part[1, i].astype(F32)
                )
            refs[-1][i] = state.astype(BF16)

    return call(body, sp, parts, [whole(a) for a in parts], [out])[0]


def shifted(value, steps):
    count = lax.axis_size("ctx")
    return lax.ppermute(value, "ctx", [(i, i + steps) for i in range(count - steps)])


def swapped(value):
    count = lax.axis_size("ctx")
    return lax.ppermute(value, "ctx", [(i, i ^ 1) for i in range(count)])


def enter_chip(joined, sp):
    chips = lax.axis_size("ctx") // 2
    if chips == 1:
        return jnp.zeros(joined.shape[1:], BF16)
    if chips <= 4:
        parts = [shifted(joined, 2 * d) for d in range(chips - 1, 0, -1)]
        return run_chain(parts, sp)
    joined = shifted(joined, 2)
    step = 1
    while step < chips:
        early = shifted(joined, 2 * step).astype(F32)
        late = joined.astype(F32)
        both = jnp.einsum(
            "hij,xhjk->xhik", late[0], early, precision=lax.Precision.HIGHEST
        )
        joined = (both + late * jnp.array([0.0, 1.0], F32)[:, None, None, None]).astype(BF16)
        step *= 2
    return joined[1]


def finish(groups, gain, sp, place, count):
    inputs = [gain]
    for group in groups:
        inputs += list(group)
    heads = sum(group[0].shape[0] for group in groups)
    out = jax.ShapeDtypeStruct((count, heads * HEAD), BF16)

    def body(sp_ref, gain_ref, *refs):
        out_ref = refs[-1]
        core = sp_ref[place]
        keep = sp_ref[1].astype(F32)
        at = 0
        for g in range(len(groups)):
            inner, query, mine, other, early_a, early_b = refs[6 * g : 6 * g + 6]
            number = inner.shape[0]
            half = number // 2
            for j in range(number):
                low_half = j < half
                i = j % half
                own, far = mine[i].astype(F32), other[i].astype(F32)
                state = jnp.where((core == 0) == low_half, own, far)
                stepped = dot3(early_a[j].astype(F32), state) + early_b[j].astype(F32)
                state = keep * jnp.where(core == 0, state, stepped)
                read = inner[j] + dot3(query[j], state)
                scale = lax.rsqrt(jnp.mean(read * read, axis=-1, keepdims=True) + EPS)
                cols = slice(at * HEAD, (at + 1) * HEAD)
                out_ref[:, cols] = (read * scale * gain_ref[...]).astype(BF16)
                at += 1

    return call(body, sp, inputs, [whole(a) for a in inputs], [out], flops=10**8)[0]


def per_device(
    hidden,
    w_query,
    w_key,
    payload_projection_matrix,
    conv_weight,
    log_decay,
    beta_rate,
    norm_gain,
    head_order,
    block_starts,
):
    count = hidden.shape[0]
    ranks = lax.axis_size("head")
    total_heads = head_order.shape[0]
    key_heads = total_heads // ranks
    plan = Plan(ranks, key_heads)
    serve = lax.axis_index("head")
    core = lax.axis_index("ctx") % 2
    rows = w_key.shape[0]
    keep = 1 - block_starts[0]
    place = 2 + total_heads
    sp = jnp.concatenate(
        [jnp.stack([serve, keep]), head_order, jnp.stack([core])]
    ).astype(jnp.int32)

    edge = lax.dynamic_slice(hidden, (count - RIM, serve * rows), (RIM, rows))
    rim = shifted(edge, 1) * keep.astype(BF16)

    cut = (key_heads + 1) // 2
    every = [list(range(cut)), list(range(cut, key_heads))]
    groups = [list(range(i, min(i + 2, key_heads))) for i in range(0, key_heads, 2)]
    narrow = {"width": HEAD, "heads": every}
    wide = [{"width": 2 * HEAD, "heads": [g[:1], g[1:]]} for g in groups]
    chunks = [(narrow, w_key)] + [(w, payload_projection_matrix) for w in wide]
    chunks.append((narrow, w_query))

    arrived = []
    for chunk, weight in chunks:
        received = [[], []]
        for stage in range(plan.stages):
            sent = send_stage(plan, stage, chunk, hidden, rim, weight, received, sp)
            for route, part in enumerate(exchange(plan, stage, sent)):
                if part is not None:
                    received[route].append(part)
        arrived.append(received)

    gain = norm_gain[None, :]
    results = []
    for g, heads in enumerate(groups):
        keys, turned, solve, write_k, trans_a = key_phase(
            plan, narrow, heads, hidden, rim, w_key, conv_weight, total_heads,
            arrived[0], log_decay, beta_rate, sp,
        )
        write_v, trans_b = value_phase(
            plan, wide[g], heads, hidden, rim, payload_projection_matrix, conv_weight,
            total_heads, arrived[1 + g], log_decay, beta_rate, turned, solve, sp,
        )
        other_a, other_b = swapped(trans_a), swapped(trans_b)
        joined = join_pair(trans_a, trans_b, other_a, other_b, sp, place)
        mine = enter_chip(joined, sp)
        other = swapped(mine)
        inner, query = query_phase(
            plan, narrow, heads, hidden, rim, w_query, conv_weight, 0,
            arrived[-1], log_decay, keys, write_k, write_v, sp,
        )
        results.append((inner, query, mine, other, other_a, other_b))
    return finish(results, gain, sp, place, count)


def solution(mesh):
    return jax.shard_map(
        per_device,
        mesh=mesh,
        in_specs=(
            P("ctx", None),
            P("head", None),
            P("head", None),
            P("head", None),
            P(),
            P("head", "ctx"),
            P("head", "ctx"),
            P(),
            P(),
            P("ctx"),
        ),
        out_specs=P("ctx", "head"),
        check_vma=False,
    )
```

```python
import functools

import jax
import jax.numpy as jnp
from jax import lax
from jax.experimental import pallas as pl
from jax.experimental.pallas import tpu as pltpu
from jax.sharding import PartitionSpec as P

HEAD = 128
TAPS = 4
RIM = 16
EPS = 1e-06
VMEM_BYTES = 40 * 1024 * 1024
F32 = jnp.float32
BF16 = jnp.bfloat16

NN = (((1,), (0,)), ((), ()))
NT = (((1,), (1,)), ((), ()))


def dot1(a, b, dims=NN):
    return lax.dot_general(
        a.astype(BF16), b.astype(BF16), dims, preferred_element_type=F32
    )


def split(a):
    high = a.astype(BF16)
    return high, (a - high.astype(F32)).astype(BF16)


def dot3s(a, b, dims=NN):
    (ah, al), (bh, bl) = a, b
    one = functools.partial(lax.dot_general, dimension_numbers=dims, preferred_element_type=F32)
    return one(ah, bh) + (one(ah, bl) + one(al, bh))


def dot3(a, b, dims=NN):
    return dot3s(split(a), split(b), dims)


def packed_left(parts):
    return jnp.concatenate(parts, axis=1)


def packed_right(parts):
    wide = jnp.concatenate(parts, axis=1)
    return jnp.concatenate([wide, wide], axis=0)


def packed_turned(parts):
    tall = jnp.concatenate(parts, axis=0)
    return jnp.concatenate([tall, tall], axis=1)


def fold(left, right, dims=NN):
    both = lax.dot_general(left, right, dims, preferred_element_type=F32)
    width = both.shape[1] // 2
    return both[:, :width] + both[:, width:]


def mul(a, b):
    return fold(packed_left(split(a)), packed_right(split(b)))


def dot_full(a, b, dims=NN):
    return lax.dot_general(
        a, b, dims, precision=lax.Precision.HIGHEST, preferred_element_type=F32
    )


def whole(array):
    zeros = (0,) * array.ndim
    return pl.BlockSpec(array.shape, lambda i, sp: zeros)


def call(body, sp, inputs, specs, outs, scratch=(), flops=10**7, after=()):
    number = len(inputs)
    specs = list(specs) + [pl.BlockSpec(memory_space=pl.ANY) for _ in after]

    def inner(sp_ref, *refs):
        body(sp_ref, *refs[:number], *refs[number + len(after) :])

    return pl.pallas_call(
        inner,
        grid_spec=pltpu.PrefetchScalarGridSpec(
            num_scalar_prefetch=1,
            grid=(1,),
            in_specs=specs,
            out_specs=[whole(out) for out in outs],
            scratch_shapes=list(scratch),
        ),
        out_shape=[jax.ShapeDtypeStruct(out.shape, out.dtype) for out in outs],
        compiler_params=pltpu.CompilerParams(vmem_limit_bytes=VMEM_BYTES),
        cost_estimate=pl.CostEstimate(flops=flops, bytes_accessed=2**20, transcendentals=0),
    )(sp, *inputs, *after)


class Plan:
    def __init__(self, ranks, key_heads):
        bits = [1 << i for i in range(ranks.bit_length() - 1)]
        self.orders = (bits, bits[::-1])
        self.stages = len(bits)
        self.key_heads = key_heads

    def offsets(self, route, stage):
        out = [0]
        for bit in self.orders[route][stage + 1 :]:
            out = out + [o ^ bit for o in out]
        return out

    def weight_spec(self, rows, width, unit, head):
        heads = self.key_heads
        return pl.BlockSpec(
            (rows, width), lambda i, sp: (0, sp[2 + (sp[0] ^ unit) * heads + head])
        )

    def tap_spec(self, width, base, head):
        heads = self.key_heads
        return pl.BlockSpec(
            (TAPS, width), lambda i, sp: (0, base + sp[2 + sp[0] * heads + head])
        )


def hidden_spec(hidden, rows):
    return pl.BlockSpec((hidden.shape[0], rows), lambda i, sp: (0, sp[0]))


def send_stage(plan, stage, chunk, hidden, rim, weight, received, sp, after=()):
    rows, count = weight.shape[0], hidden.shape[0]
    width = chunk["width"]
    inputs, specs = [hidden], [hidden_spec(hidden, rows)]
    lead = 0
    if rim is not None:
        lead = RIM
        inputs, specs = inputs + [rim], specs + [whole(rim)]
    jobs, outs, places = [], [], {}
    for route, heads in enumerate(chunk["heads"]):
        if not heads:
            continue
        offsets = plan.offsets(route, stage)
        for before in range(stage):
            places[route, before] = len(inputs)
            inputs.append(received[route][before])
            specs.append(whole(received[route][before]))
        for slot, offset in enumerate(offsets):
            unit = offset ^ plan.orders[route][stage]
            sources = [
                (places[route, before], plan.offsets(route, before).index(unit))
                for before in range(stage)
            ]
            for at, head in enumerate(heads):
                jobs.append((len(inputs), sources, len(outs), slot, at))
                inputs.append(weight)
                specs.append(plan.weight_spec(rows, width, unit, head))
        outs.append(
            jax.ShapeDtypeStruct((len(offsets), lead + count, width * len(heads)), BF16)
        )
    total = len(inputs)

    def body(sp_ref, *refs):
        lefts = [(refs[0][...], slice(lead, lead + count))]
        if lead:
            lefts.append((refs[1][...], slice(0, lead)))
        for place, sources, out, slot, at in jobs:
            held = refs[place][...]
            cols = slice(at * width, (at + 1) * width)
            for left, span in lefts:
                part = jnp.dot(left, held, preferred_element_type=F32)
                for source, index in sources:
                    part = part + refs[source][index, span, cols].astype(F32)
                refs[total + out][slot, span, cols] = part.astype(BF16)

    sent = call(body, sp, inputs, specs, outs, after=after)
    result, at = [], 0
    for heads in chunk["heads"]:
        result.append(sent[at] if heads else None)
        at += 1 if heads else 0
    return result


def rim_products(plan, rim, weight, ranks, sp, after=()):
    rows, heads = weight.shape[0], plan.key_heads
    number = ranks * heads
    out = jax.ShapeDtypeStruct((ranks, RIM, heads * HEAD), BF16)
    specs = [whole(rim)] + [
        pl.BlockSpec((rows, HEAD), lambda i, sp, s=s: (0, sp[2 + s])) for s in range(number)
    ]

    def body(sp_ref, rim_ref, *refs):
        for s in range(number):
            cols = slice((s % heads) * HEAD, (s % heads + 1) * HEAD)
            part = jnp.dot(rim_ref[...], refs[s][...], preferred_element_type=F32)
            refs[-1][s // heads, :, cols] = part.astype(BF16)

    return call(body, sp, [rim] + [weight] * number, specs, [out], after=after)[0]


def exchange(plan, stage, sent):
    ranks = lax.axis_size("head")
    return [
        None
        if part is None
        else lax.ppermute(
            part, "head", [(i, i ^ plan.orders[route][stage]) for i in range(ranks)]
        )
        for route, part in enumerate(sent)
    ]


def gather_specs(plan, chunk, heads, hidden, rim, weight, taps, base, received, rim_parts=None):
    rows, width = weight.shape[0], chunk["width"]
    inputs, specs = [hidden], [hidden_spec(hidden, rows)]
    edge = rim if rim_parts is None else rim_parts
    inputs, specs = inputs + [edge], specs + [whole(edge)]
    places, jobs = {}, []
    for head in heads:
        route = [head in group for group in chunk["heads"]].index(True)
        if route not in places:
            places[route] = []
            for part in received[route]:
                places[route].append(len(inputs))
                inputs.append(part)
                specs.append(pl.BlockSpec((1,) + part.shape[1:], lambda i, sp: (0, 0, 0)))
        at = chunk["heads"][route].index(head)
        cols = slice(at * width, (at + 1) * width)
        summed = None if rim_parts is None else slice(head * width, (head + 1) * width)
        jobs.append((len(inputs), places[route], cols, summed))
        inputs += [weight, taps]
        specs += [plan.weight_spec(rows, width, 0, head), plan.tap_spec(width, base, head)]
    return inputs, specs, jobs


def activate(refs, job, scratch):
    place, sources, cols, summed = job
    held, taps = refs[place][...], refs[place + 1][...].astype(F32)
    count = refs[0].shape[0]
    lead = 0 if summed is not None else RIM
    lefts = [(refs[0], slice(RIM, RIM + count), slice(lead, lead + count))]
    if summed is None:
        lefts.append((refs[1], slice(0, RIM), slice(0, RIM)))
    else:
        edge = refs[1][0, :, summed].astype(F32)
        for rank in range(1, refs[1].shape[0]):
            edge = edge + refs[1][rank, :, summed].astype(F32)
        scratch[0:RIM, :] = edge
    for left, span, source_span in lefts:
        part = jnp.dot(left[...], held, preferred_element_type=F32)
        for source in sources:
            part = part + refs[source][0, source_span, cols].astype(F32)
        scratch[span, :] = part
    total = None
    for tap in range(TAPS):
        first = RIM - (TAPS - 1) + tap
        term = taps[tap : tap + 1] * scratch[first : first + count, :]
        total = term if total is None else total + term
    return total / (1.0 + jnp.exp(-total))


def unit_rows(values):
    return values * lax.rsqrt(jnp.sum(values * values, axis=-1, keepdims=True) + EPS)


def iotas(size):
    return (
        lax.broadcasted_iota(jnp.int32, (size, size), 0),
        lax.broadcasted_iota(jnp.int32, (size, size), 1),
    )


def prepare(decay, beta, sp, after=()):
    heads, count = decay.shape
    outs = [
        jax.ShapeDtypeStruct((heads, count), F32),
        jax.ShapeDtypeStruct((count, heads), F32),
        jax.ShapeDtypeStruct((count, heads), F32),
    ]

    def body(sp_ref, decay_ref, beta_ref, row_ref, col_ref, rate_ref):
        rows, cols = iotas(count)
        row_ref[...] = dot_full(decay_ref[...], (rows <= cols).astype(F32))
        col_ref[...] = dot_full((cols <= rows).astype(F32), decay_ref[...], NT)
        rate_ref[...] = dot_full((rows == cols).astype(F32), beta_ref[...], NT)

    return call(body, sp, [decay, beta], [whole(decay), whole(beta)], outs, after=after)


def inverses(systems):
    size = systems[0].shape[0]
    rows, cols = iotas(size)
    eye = (rows == cols).astype(F32)
    near = [jnp.where((rows >> 3) == (cols >> 3), low, 0.0) for low in systems]
    cut = [split(n) for n in near]
    left = [packed_left(c) for c in cut]
    square = [fold(l, packed_right(c)) for l, c in zip(left, cut)]
    cut2 = [split(s) for s in square]
    right2 = [packed_right(c) for c in cut2]
    cube = [fold(l, r) for l, r in zip(left, right2)]
    inv = [eye - n + s - c for n, s, c in zip(near, square, cube)]
    fourth = [packed_right(split(fold(packed_left(c), r))) for c, r in zip(cut2, right2)]
    inv = [x + fold(packed_left(split(x)), f) for x, f in zip(inv, fourth)]
    shift = 3
    while (1 << shift) < size:
        inside = ((rows >> (shift + 1)) == (cols >> (shift + 1))) & (
            (rows >> shift) != (cols >> shift)
        )
        parts = [split(x) for x in inv]
        lower = [packed_left(split(jnp.where(inside, low, 0.0))) for low in systems]
        middle = [fold(low, packed_right(p)) for low, p in zip(lower, parts)]
        middle = [packed_right(split(m)) for m in middle]
        inv = [x - fold(packed_left(p), m) for x, p, m in zip(inv, parts, middle)]
        shift += 1
    return inv


def key_phase(
    plan, chunk, heads, hidden, rim_parts, weight, taps, base, received, tables, sp, after=()
):
    inputs, specs, jobs = gather_specs(
        plan, chunk, heads, hidden, None, weight, taps, base, received, rim_parts
    )
    at = len(inputs)
    inputs += tables
    specs += [whole(table) for table in tables]
    count, number = hidden.shape[0], 2 * len(heads)
    half = count // 2
    first = 2 * heads[0]
    outs = [
        jax.ShapeDtypeStruct((len(heads), count, HEAD), F32),
        jax.ShapeDtypeStruct((len(heads), HEAD, count), F32),
        jax.ShapeDtypeStruct((number, 3, half, half), F32),
        jax.ShapeDtypeStruct((number, count, HEAD), F32),
        jax.ShapeDtypeStruct((number, HEAD, HEAD), F32),
    ]
    total = len(inputs)

    def body(sp_ref, *refs):
        key_ref, turned_ref, solve_ref, write_ref, trans_ref, scratch = refs[total:]
        sums, sums_col, beta_col = (ref[...] for ref in refs[at : at + 3])
        rows, cols = iotas(half)
        keys, systems, crosses = [], [], []
        for i, job in enumerate(jobs):
            key = unit_rows(activate(refs, job, scratch))
            keys.append(key)
            key_ref[i] = key
            turned_ref[i] = key.T
            low, high = split(key[:half]), split(key[half:])
            low_left, high_left = packed_left(low), packed_left(high)
            low_right, high_right = packed_turned(low), packed_turned(high)
            alike = (
                fold(low_left, low_right, NT),
                fold(high_left, high_right, NT),
                fold(high_left, low_right, NT),
            )
            for r in (first + 2 * i, first + 2 * i + 1):
                row, col, rate = sums[r : r + 1], sums_col[:, r : r + 1], beta_col[:, r : r + 1]
                for b, span in enumerate((slice(0, half), slice(half, count))):
                    fade = jnp.exp(jnp.minimum(col[span] - row[:, span], 0.0))
                    systems.append(jnp.where(cols < rows, rate[span] * fade * alike[b], 0.0))
                fade = jnp.exp(jnp.minimum(col[half:] - row[:, :half], 0.0))
                crosses.append(rate[half:] * fade * alike[2])
        solved = inverses(systems)
        left = [packed_left(split(x)) for x in solved]
        middle = [
            mul(cross, solved[2 * j]) for j, cross in enumerate(crosses)
        ]
        corner = [
            -fold(left[2 * j + 1], packed_right(split(m))) for j, m in enumerate(middle)
        ]
        keep = sp_ref[1].astype(F32)
        eye = (lax.broadcasted_iota(jnp.int32, (HEAD, HEAD), 0)
               == lax.broadcasted_iota(jnp.int32, (HEAD, HEAD), 1)).astype(F32)
        for j in range(number):
            r, key = first + j, keys[j // 2]
            row, col, rate = sums[r : r + 1], sums_col[:, r : r + 1], beta_col[:, r : r + 1]
            for place, part in enumerate((solved[2 * j], solved[2 * j + 1], corner[j])):
                solve_ref[j, place] = part
            right = (rate * jnp.exp(col)) * key
            right_low = packed_right(split(right[:half]))
            right_high = packed_right(split(right[half:]))
            write_low = fold(left[2 * j], right_low)
            write_high = fold(packed_left(split(corner[j])), right_low) + fold(
                left[2 * j + 1], right_high
            )
            write_ref[j, :half] = write_low
            write_ref[j, half:] = write_high
            tail = jnp.exp(row[:, count - 1 :] - row)
            trailing = turned_ref[j // 2] * tail
            moved = mul(trailing[:, :half], write_low) + mul(trailing[:, half:], write_high)
            gone = jnp.exp(row[:, count - 1 :])
            trans_ref[j] = keep * (gone * eye - moved)

    return call(
        body, sp, inputs, specs, outs, [pltpu.VMEM((RIM + count, HEAD), F32)],
        flops=4 * 10**9, after=after,
    )


def value_phase(
    plan, chunk, heads, hidden, rim, weight, taps, base, received, tables, parts, sp, after=()
):
    inputs, specs, jobs = gather_specs(
        plan, chunk, heads, hidden, rim, weight, taps, base, received
    )
    at = len(inputs)
    inputs += tables
    for turned, solve in parts:
        inputs += [turned, solve]
    specs += [whole(a) for a in inputs[at:]]
    count, number = hidden.shape[0], 2 * len(heads)
    half = count // 2
    outs = [
        jax.ShapeDtypeStruct((number, count, HEAD), F32),
        jax.ShapeDtypeStruct((number, HEAD, HEAD), BF16),
    ]
    total = len(inputs)
    group = parts[0][0].shape[0]

    def body(sp_ref, *refs):
        write_ref, trans_ref, scratch = refs[total:]
        sums, beta_col = refs[at][...], refs[at + 2][...]
        for i, job in enumerate(jobs):
            values = activate(refs, job, scratch)
            turned_ref, solve_ref = refs[at + 3 + 2 * (i // group) : at + 5 + 2 * (i // group)]
            for j in (2 * i, 2 * i + 1):
                row, rate = sums[j : j + 1], beta_col[:, j : j + 1]
                right = rate * values[:, (j % 2) * HEAD : (j % 2 + 1) * HEAD]
                low = packed_right(split(right[:half]))
                high = packed_right(split(right[half:]))
                top, bottom, side = [
                    packed_left(split(solve_ref[j % (2 * group), place])) for place in range(3)
                ]
                write_low = fold(top, low)
                write_high = fold(side, low) + fold(bottom, high)
                write_ref[j, :half] = write_low
                write_ref[j, half:] = write_high
                trailing = turned_ref[i % group] * jnp.exp(row[:, count - 1 :] - row)
                trans_ref[j] = (
                    mul(trailing[:, :half], write_low) + mul(trailing[:, half:], write_high)
                ).astype(BF16)

    return call(
        body, sp, inputs, specs, outs, [pltpu.VMEM((RIM + count, 2 * HEAD), F32)],
        flops=2 * 10**9, after=after,
    )


def query_phase(
    plan, chunk, heads, hidden, rim, weight, taps, base, received, tables, parts, write_v, sp,
    after=(),
):
    inputs, specs, jobs = gather_specs(
        plan, chunk, heads, hidden, rim, weight, taps, base, received
    )
    at = len(inputs)
    inputs += tables + [write_v]
    for key, write_k in parts:
        inputs += [key, write_k]
    specs += [whole(a) for a in inputs[at:]]
    count, number = hidden.shape[0], 2 * len(heads)
    half = count // 2
    outs = [
        jax.ShapeDtypeStruct((number, count, HEAD), F32),
        jax.ShapeDtypeStruct((number, count, HEAD), F32),
    ]
    total = len(inputs)
    group = parts[0][0].shape[0]

    def body(sp_ref, *refs):
        inner_ref, query_ref, scratch = refs[total:]
        sums, sums_col = refs[at][...], refs[at + 1][...]
        write_v_ref = refs[at + 3]
        rows, cols = iotas(half)
        low, high = slice(0, half), slice(half, count)
        for i, job in enumerate(jobs):
            key_ref, write_k_ref = refs[at + 4 + 2 * (i // group) : at + 6 + 2 * (i // group)]
            query = unit_rows(activate(refs, job, scratch))
            key = key_ref[i % group]
            left = [packed_left(split(query[span])) for span in (low, high)]
            right = [packed_turned(split(key[span])) for span in (low, high)]
            alike = {
                (0, 0): fold(left[0], right[0], NT),
                (1, 1): fold(left[1], right[1], NT),
                (1, 0): fold(left[1], right[0], NT),
            }
            for j in (2 * i, 2 * i + 1):
                row, col = sums[j : j + 1], sums_col[:, j : j + 1]
                wrote = [
                    split(
                        jnp.concatenate(
                            [write_v_ref[j, span], write_k_ref[j % (2 * group), span]], axis=1
                        )
                    )
                    for span in (low, high)
                ]
                tall = [jnp.concatenate([w[0], w[0]], axis=0) for w in wrote]
                read = [None, None]
                for (t, s), product in alike.items():
                    fade = jnp.exp(
                        jnp.minimum(col[(low, high)[t]] - row[:, (low, high)[s]], 0.0)
                    )
                    attend = fade * product
                    if t == s:
                        attend = jnp.where(cols <= rows, attend, 0.0)
                    attend = split(attend)
                    part = jnp.dot(
                        packed_left(attend), tall[s], preferred_element_type=F32
                    ) + jnp.dot(attend[0], wrote[s][1], preferred_element_type=F32)
                    read[t] = part if read[t] is None else read[t] + part
                for t, span in enumerate((low, high)):
                    inner_ref[j, span] = read[t][:, :HEAD]
                    query_ref[j, span] = jnp.exp(col[span]) * query[span] - read[t][:, HEAD:]

    return call(
        body, sp, inputs, specs, outs, [pltpu.VMEM((RIM + count, HEAD), F32)],
        flops=2 * 10**9, after=after,
    )


def halves(groups):
    return [(g, i) for g, part in enumerate(groups) for i in range(part.shape[0] // 2)]


def join_transitions(mine, other, sp, place):
    served = halves(mine)
    out = jax.ShapeDtypeStruct((len(served), HEAD, HEAD), BF16)
    inputs, number = [*mine, *other], len(mine)

    def body(sp_ref, *refs):
        core = sp_ref[place]
        for slot, (g, i) in enumerate(served):
            h = core * (refs[g].shape[0] // 2) + i
            pair = (refs[g][h], refs[number + g][h])
            early = jnp.where(core == 0, pair[0], pair[1])
            late = jnp.where(core == 0, pair[1], pair[0])
            refs[-1][slot] = mul(late, early).astype(BF16)

    return call(body, sp, inputs, [whole(a) for a in inputs], [out])[0]


def join_writes(mine_a, other_a, mine, other, sp, place):
    served = halves(mine_a)
    out = jax.ShapeDtypeStruct((len(served), HEAD, HEAD), BF16)
    inputs, number = [*mine_a, *other_a, mine, other], len(mine_a)

    def body(sp_ref, *refs):
        core = sp_ref[place]
        for slot, (g, i) in enumerate(served):
            size = refs[g].shape[0]
            h = core * (size // 2) + i
            pair = (refs[-3][g * size + h].astype(F32), refs[-2][g * size + h].astype(F32))
            early = jnp.where(core == 0, pair[0], pair[1])
            late = jnp.where(core == 0, pair[1], pair[0])
            late_a = jnp.where(core == 0, refs[number + g][h], refs[g][h])
            refs[-1][slot] = (mul(late_a, early) + late).astype(BF16)

    return call(body, sp, inputs, [whole(a) for a in inputs], [out])[0]


def run_chain(trans, writes, sp):
    half = writes[0].shape[0]
    out = jax.ShapeDtypeStruct((half, HEAD, HEAD), BF16)
    inputs = [*trans, *writes]

    def body(sp_ref, *refs):
        for i in range(half):
            state = refs[len(trans)][i].astype(F32)
            for step in range(len(trans)):
                left = refs[step][i]
                state = fold(
                    packed_left((left, jnp.zeros_like(left))), packed_right(split(state))
                ) + refs[len(trans) + 1 + step][i].astype(F32)
            refs[-1][i] = state.astype(BF16)

    return call(body, sp, inputs, [whole(a) for a in inputs], [out])[0]


def shifted(value, steps):
    count = lax.axis_size("ctx")
    return lax.ppermute(value, "ctx", [(i, i + steps) for i in range(count - steps)])


def swapped(value):
    count = lax.axis_size("ctx")
    return lax.ppermute(value, "ctx", [(i, i ^ 1) for i in range(count)])


def enter_far(trans, writes):
    chips = lax.axis_size("ctx") // 2
    trans, writes = shifted(trans, 2), shifted(writes, 2)
    step = 1
    while step < chips:
        early_a, early_b = shifted(trans, 2 * step), shifted(writes, 2 * step)
        late = trans.astype(F32)
        join = functools.partial(
            jnp.einsum, "hij,hjk->hik", late, precision=lax.Precision.HIGHEST
        )
        writes = (join(early_b.astype(F32)) + writes.astype(F32)).astype(BF16)
        trans = join(early_a.astype(F32)).astype(BF16)
        step *= 2
    return writes


def finish(inner, query, mine, other, early_a, early_b, gain, sp, place):
    inputs = [inner, query, mine, other, *early_a, early_b, gain]
    number, count = inner.shape[:2]
    group = early_a[0].shape[0]
    half = group // 2
    out = jax.ShapeDtypeStruct((count, number * HEAD), BF16)

    def body(sp_ref, *refs):
        inner_ref, query_ref, mine_ref, other_ref = refs[:4]
        early_b_ref, gain_ref, out_ref = refs[-3:]
        core = sp_ref[place]
        keep = sp_ref[1].astype(F32)
        for j in range(number):
            slot = (j // group) * half + j % half
            own, far = mine_ref[slot].astype(F32), other_ref[slot].astype(F32)
            state = jnp.where((core == 0) == (j % group < half), own, far)
            stepped = mul(refs[4 + j // group][j % group], state) + early_b_ref[j].astype(F32)
            state = keep * jnp.where(core == 0, state, stepped)
            read = inner_ref[j] + mul(query_ref[j], state)
            scale = lax.rsqrt(jnp.mean(read * read, axis=-1, keepdims=True) + EPS)
            cols = slice(j * HEAD, (j + 1) * HEAD)
            out_ref[:, cols] = (read * scale * gain_ref[...]).astype(BF16)

    return call(body, sp, inputs, [whole(a) for a in inputs], [out], flops=10**8)[0]


def per_device(
    hidden,
    w_query,
    w_key,
    payload_projection_matrix,
    conv_weight,
    log_decay,
    beta_rate,
    norm_gain,
    head_order,
    block_starts,
):
    count = hidden.shape[0]
    ranks = lax.axis_size("head")
    chips = lax.axis_size("ctx") // 2
    total_heads = head_order.shape[0]
    key_heads = total_heads // ranks
    plan = Plan(ranks, key_heads)
    serve = lax.axis_index("head")
    core = lax.axis_index("ctx") % 2
    rows = w_key.shape[0]
    keep = 1 - block_starts[0]
    place = 2 + total_heads
    sp = jnp.concatenate(
        [jnp.stack([serve, keep]), head_order, jnp.stack([core])]
    ).astype(jnp.int32)
    w_value = payload_projection_matrix

    cut = (key_heads + 1) // 2
    routes = [list(range(cut)), list(range(cut, key_heads))]
    everyone = list(range(key_heads))
    groups = [heads for heads in routes if heads]
    narrow = {"width": HEAD, "heads": routes}
    wide = {"width": 2 * HEAD, "heads": routes}

    def send(stage, chunk, rim, weight, received, after=()):
        sent = send_stage(plan, stage, chunk, hidden, rim, weight, received, sp, after)
        for route, part in enumerate(exchange(plan, stage, sent)):
            if part is not None:
                received[route].append(part)
        return [part for part in sent if part is not None]

    got_k, got_v, got_q = [[], []], [[], []], [[], []]
    sent = send(0, narrow, None, w_key, got_k)
    edge = lax.dynamic_slice(hidden, (count - RIM, serve * rows), (RIM, rows))
    rim = shifted(edge, 1) * keep.astype(BF16)
    rim_parts = lax.all_to_all(
        rim_products(plan, rim, w_key, ranks, sp, after=sent), "head", 0, 0, tiled=True
    )
    sent = send(0, wide, rim, w_value, got_v, after=sent)
    tables = list(prepare(log_decay, beta_rate, sp, after=sent))
    for stage in range(1, plan.stages):
        sent = send(stage, narrow, None, w_key, got_k, after=sent)

    keyed = []
    for at, heads in enumerate(groups):
        keyed.append(
            key_phase(
                plan, narrow, heads, hidden, rim_parts, w_key, conv_weight, total_heads,
                got_k, tables, sp, after=sent,
            )
        )
        if at == 0:
            for stage in range(1, plan.stages):
                sent = send(stage, wide, rim, w_value, got_v, after=[keyed[0][4]])
            sent = send(0, narrow, rim, w_query, got_q, after=sent)
    for stage in range(1, plan.stages):
        send(stage, narrow, rim, w_query, got_q, after=[keyed[-1][4]])

    trans = [group[4] for group in keyed]
    other_trans = [swapped(part) for part in trans]
    joined_a = join_transitions(trans, other_trans, sp, place)
    write_v, trans_b = value_phase(
        plan, wide, everyone, hidden, rim, w_value, conv_weight, total_heads, got_v, tables,
        [(group[1], group[2]) for group in keyed], sp,
    )
    other_b = swapped(trans_b)
    joined_b = join_writes(trans, other_trans, trans_b, other_b, sp, place)
    if chips <= 4:
        far_a = [shifted(joined_a, 2 * d) for d in range(chips - 2, 0, -1)]
        far_b = [shifted(joined_b, 2 * d) for d in range(chips - 1, 0, -1)]
        mine = run_chain(far_a, far_b, sp)
    else:
        mine = enter_far(joined_a, joined_b)
    other = swapped(mine)
    inner, query = query_phase(
        plan, narrow, everyone, hidden, rim, w_query, conv_weight, 0, got_q, tables,
        [(group[0], group[3]) for group in keyed], write_v, sp,
    )
    return finish(
        inner, query, mine, other, other_trans, other_b, norm_gain[None, :], sp, place
    )


def solution(mesh):
    return jax.shard_map(
        per_device,
        mesh=mesh,
        in_specs=(
            P("ctx", None),
            P("head", None),
            P("head", None),
            P("head", None),
            P(),
            P("head", "ctx"),
            P("head", "ctx"),
            P(),
            P(),
            P("ctx"),
        ),
        out_specs=P("ctx", "head"),
        check_vma=False,
    )
```

```python
import functools

import jax
import jax.numpy as jnp
from jax import lax
from jax.experimental import pallas as pl
from jax.experimental.pallas import tpu as pltpu
from jax.sharding import PartitionSpec as P

HEAD = 128
TAPS = 4
RIM = 16
EPS = 1e-06
VMEM_BYTES = 20 * 1024 * 1024
F32 = jnp.float32
BF16 = jnp.bfloat16

NN = (((1,), (0,)), ((), ()))
NT = (((1,), (1,)), ((), ()))


def dot1(a, b, dims=NN):
    return lax.dot_general(
        a.astype(BF16), b.astype(BF16), dims, preferred_element_type=F32
    )


def split(a):
    high = a.astype(BF16)
    return high, (a - high.astype(F32)).astype(BF16)


def dot3s(a, b, dims=NN):
    (ah, al), (bh, bl) = a, b
    one = functools.partial(lax.dot_general, dimension_numbers=dims, preferred_element_type=F32)
    return one(ah, bh) + (one(ah, bl) + one(al, bh))


def dot3(a, b, dims=NN):
    return dot3s(split(a), split(b), dims)


def packed_left(parts):
    return jnp.concatenate(parts, axis=1)


def packed_right(parts):
    wide = jnp.concatenate(parts, axis=1)
    return jnp.concatenate([wide, wide], axis=0)


def packed_turned(parts):
    tall = jnp.concatenate(parts, axis=0)
    return jnp.concatenate([tall, tall], axis=1)


def fold(left, right, dims=NN):
    both = lax.dot_general(left, right, dims, preferred_element_type=F32)
    width = both.shape[1] // 2
    return both[:, :width] + both[:, width:]


def mul(a, b):
    return fold(packed_left(split(a)), packed_right(split(b)))


def dot_full(a, b, dims=NN):
    return lax.dot_general(
        a, b, dims, precision=lax.Precision.HIGHEST, preferred_element_type=F32
    )


def whole(array):
    zeros = (0,) * array.ndim
    return pl.BlockSpec(array.shape, lambda i, sp: zeros)


def call(body, sp, inputs, specs, outs, scratch=(), after=()):
    number = len(inputs)
    specs = list(specs) + [pl.BlockSpec(memory_space=pl.ANY) for _ in after]

    def inner(sp_ref, *refs):
        body(sp_ref, *refs[:number], *refs[number + len(after) :])

    return pl.pallas_call(
        inner,
        grid_spec=pltpu.PrefetchScalarGridSpec(
            num_scalar_prefetch=1,
            grid=(1,),
            in_specs=specs,
            out_specs=[whole(out) for out in outs],
            scratch_shapes=list(scratch),
        ),
        out_shape=[jax.ShapeDtypeStruct(out.shape, out.dtype) for out in outs],
        compiler_params=pltpu.CompilerParams(vmem_limit_bytes=VMEM_BYTES),
        cost_estimate=pl.CostEstimate(flops=1000, bytes_accessed=1000, transcendentals=0),
    )(sp, *inputs, *after)


def weight_spec(key_heads, rows, width, unit, head):
    return pl.BlockSpec(
        (rows, width), lambda i, sp: (0, sp[2 + (sp[0] ^ unit) * key_heads + head])
    )


def tap_spec(key_heads, width, base, head):
    return pl.BlockSpec(
        (TAPS, width), lambda i, sp: (0, base + sp[2 + sp[0] * key_heads + head])
    )


def hidden_spec(hidden, rows):
    return pl.BlockSpec((hidden.shape[0], rows), lambda i, sp: (0, sp[0]))


def partial_sums(key_heads, ranks, heads, width, hidden, rim, weight, sp, after=()):
    rows, count = weight.shape[0], hidden.shape[0]
    inputs, specs = [hidden, rim], [hidden_spec(hidden, rows), hidden_spec(rim, rows)]
    for unit in range(1, ranks):
        for head in heads:
            inputs.append(weight)
            specs.append(weight_spec(key_heads, rows, width, unit, head))
    outs = [jax.ShapeDtypeStruct((RIM + count, width * len(heads)), BF16)] * (ranks - 1)

    def body(sp_ref, hidden_ref, rim_ref, *refs):
        for unit in range(ranks - 1):
            out = refs[(ranks - 1) * len(heads) + unit]
            for at in range(len(heads)):
                held = refs[unit * len(heads) + at][...]
                cols = slice(at * width, (at + 1) * width)
                out[RIM:, cols] = plain(hidden_ref[...], held).astype(BF16)
                out[:RIM, cols] = plain(rim_ref[...], held).astype(BF16)

    return call(body, sp, inputs, specs, outs, after=after)


def exchange(parts):
    ranks = len(parts) + 1
    return [
        lax.ppermute(part, "head", [(i, i ^ (unit + 1)) for i in range(ranks)])
        for unit, part in enumerate(parts)
    ]


def gather_specs(key_heads, heads, width, hidden, rim, weight, taps, base, received):
    rows = weight.shape[0]
    inputs = [hidden, rim]
    specs = [hidden_spec(hidden, rows), hidden_spec(rim, rows)]
    jobs = []
    for head, at in heads:
        jobs.append(len(inputs))
        inputs += [weight, taps]
        specs += [
            weight_spec(key_heads, rows, width, 0, head), tap_spec(key_heads, width, base, head)
        ]
        for part in received:
            inputs.append(part)
            specs.append(pl.BlockSpec((part.shape[0], width), lambda i, sp, at=at: (0, at)))
    return inputs, specs, jobs


def activate(refs, job, number, scratch):
    held, taps = refs[job][...], refs[job + 1][...].astype(F32)
    count = refs[0].shape[0]
    for left, span in ((refs[0], slice(RIM, RIM + count)), (refs[1], slice(0, RIM))):
        part = plain(left[...], held)
        for source in range(job + 2, job + 2 + number):
            part = part + refs[source][span, :].astype(F32)
        scratch[span, :] = part
    total = None
    for tap in range(TAPS):
        first = RIM - (TAPS - 1) + tap
        term = taps[tap : tap + 1] * scratch[first : first + count, :]
        total = term if total is None else total + term
    return total / (1.0 + jnp.exp(-total))


def plain(a, b):
    return jnp.dot(a, b, preferred_element_type=F32)


def unit_rows(values):
    return values * lax.rsqrt(jnp.sum(values * values, axis=-1, keepdims=True) + EPS)


def iotas(size):
    return (
        lax.broadcasted_iota(jnp.int32, (size, size), 0),
        lax.broadcasted_iota(jnp.int32, (size, size), 1),
    )


def prepare(decay, beta, sp, after=()):
    heads, count = decay.shape
    outs = [
        jax.ShapeDtypeStruct((heads, count), F32),
        jax.ShapeDtypeStruct((count, heads), F32),
        jax.ShapeDtypeStruct((count, heads), F32),
    ]

    def body(sp_ref, decay_ref, beta_ref, row_ref, col_ref, rate_ref):
        rows, cols = iotas(count)
        row_ref[...] = dot_full(decay_ref[...], (rows <= cols).astype(F32))
        col_ref[...] = dot_full((cols <= rows).astype(F32), decay_ref[...], NT)
        rate_ref[...] = dot_full((rows == cols).astype(F32), beta_ref[...], NT)

    return call(body, sp, [decay, beta], [whole(decay), whole(beta)], outs, after=after)


def inverses(systems):
    size = systems[0].shape[0]
    rows, cols = iotas(size)
    eye = (rows == cols).astype(F32)
    cut = [split(low) for low in systems]
    mask = ((rows >> 2) == (cols >> 2)).astype(F32).astype(BF16)
    near = [c[0] * mask for c in cut]
    square = [plain(n, n) for n in near]
    cube = [plain(n, s.astype(BF16)) for n, s in zip(near, square)]
    inv = [
        (eye - n.astype(F32) + s - c).astype(BF16) for n, s, c in zip(near, square, cube)
    ]
    shift = 2
    while (1 << shift) < size:
        inside = ((rows >> (shift + 1)) == (cols >> (shift + 1))) & (
            (rows >> shift) != (cols >> shift)
        )
        mask = inside.astype(F32).astype(BF16)
        middle = [plain(c[0] * mask, x).astype(BF16) for c, x in zip(cut, inv)]
        inv = [x - plain(x, m).astype(BF16) for x, m in zip(inv, middle)]
        shift += 1
    rest = [
        eye - x.astype(F32) - plain(packed_left(c), jnp.concatenate([x, x], axis=0))
        for c, x in zip(cut, inv)
    ]
    return [x.astype(F32) + plain(x, r.astype(BF16)) for x, r in zip(inv, rest)]


def key_phase(gathered, first, number, count, tables, sp, after=()):
    inputs, specs, jobs = gathered
    received = (len(inputs) - 2) // len(jobs) - 2
    at = len(inputs)
    inputs = inputs + tables
    specs = specs + [whole(table) for table in tables]
    half = count // 2
    heads = range(number // 2)
    outs = [
        jax.ShapeDtypeStruct((len(heads), count, HEAD), F32),
        jax.ShapeDtypeStruct((len(heads), HEAD, count), F32),
        jax.ShapeDtypeStruct((number, 3, half, half), F32),
        jax.ShapeDtypeStruct((number, count, HEAD), F32),
        jax.ShapeDtypeStruct((number, HEAD, HEAD), F32),
    ]
    total = len(inputs)

    def body(sp_ref, *refs):
        key_ref, turned_ref, solve_ref, write_ref, trans_ref, scratch = refs[total:]
        sums, sums_col, beta_col = (ref[...] for ref in refs[at : at + 3])
        rows, cols = iotas(half)
        keys, systems, crosses = [], [], []
        for i, job in enumerate(jobs):
            key = unit_rows(activate(refs, job, received, scratch))
            keys.append(key)
            key_ref[i] = key
            turned_ref[i] = key.T
            low, high = split(key[:half]), split(key[half:])
            low_left, high_left = packed_left(low), packed_left(high)
            low_right, high_right = packed_turned(low), packed_turned(high)
            alike = (
                fold(low_left, low_right, NT),
                fold(high_left, high_right, NT),
                fold(high_left, low_right, NT),
            )
            for r in (first + 2 * i, first + 2 * i + 1):
                row, col, rate = sums[r : r + 1], sums_col[:, r : r + 1], beta_col[:, r : r + 1]
                for b, span in enumerate((slice(0, half), slice(half, count))):
                    fade = jnp.exp(jnp.minimum(col[span] - row[:, span], 0.0))
                    systems.append(jnp.where(cols < rows, rate[span] * fade * alike[b], 0.0))
                fade = jnp.exp(jnp.minimum(col[half:] - row[:, :half], 0.0))
                crosses.append(rate[half:] * fade * alike[2])
        solved = inverses(systems)
        left = [packed_left(split(x)) for x in solved]
        middle = [
            mul(cross, solved[2 * j]) for j, cross in enumerate(crosses)
        ]
        corner = [
            -fold(left[2 * j + 1], packed_right(split(m))) for j, m in enumerate(middle)
        ]
        keep = sp_ref[1].astype(F32)
        eye = (lax.broadcasted_iota(jnp.int32, (HEAD, HEAD), 0)
               == lax.broadcasted_iota(jnp.int32, (HEAD, HEAD), 1)).astype(F32)
        for j in range(number):
            r, key = first + j, keys[j // 2]
            row, col, rate = sums[r : r + 1], sums_col[:, r : r + 1], beta_col[:, r : r + 1]
            for which, part in enumerate((solved[2 * j], solved[2 * j + 1], corner[j])):
                solve_ref[j, which] = part
            right = (rate * jnp.exp(col)) * key
            right_low = packed_right(split(right[:half]))
            right_high = packed_right(split(right[half:]))
            write_low = fold(left[2 * j], right_low)
            write_high = fold(packed_left(split(corner[j])), right_low) + fold(
                left[2 * j + 1], right_high
            )
            write_ref[j, :half] = write_low
            write_ref[j, half:] = write_high
            tail = jnp.exp(row[:, count - 1 :] - row)
            trailing = turned_ref[j // 2] * tail
            moved = mul(trailing[:, :half], write_low) + mul(trailing[:, half:], write_high)
            gone = jnp.exp(row[:, count - 1 :])
            trans_ref[j] = keep * (gone * eye - moved)

    return call(
        body, sp, inputs, specs, outs, [pltpu.VMEM((RIM + count, HEAD), F32)], after=after,
    )


def value_phase(gathered, first, number, count, tables, turned, solve, sp, after=()):
    inputs, specs, jobs = gathered
    received = (len(inputs) - 2) // len(jobs) - 2
    at = len(inputs)
    inputs = inputs + tables + [turned, solve]
    specs = specs + [whole(a) for a in inputs[at:]]
    half = count // 2
    outs = [
        jax.ShapeDtypeStruct((number, count, HEAD), F32),
        jax.ShapeDtypeStruct((number, HEAD, HEAD), BF16),
    ]
    total = len(inputs)

    def body(sp_ref, *refs):
        write_ref, trans_ref, scratch = refs[total:]
        sums, beta_col = refs[at][...], refs[at + 2][...]
        turned_ref, solve_ref = refs[at + 3 : at + 5]
        for i, job in enumerate(jobs):
            values = activate(refs, job, received, scratch)
            for j in (2 * i, 2 * i + 1):
                r = first + j
                row, rate = sums[r : r + 1], beta_col[:, r : r + 1]
                right = rate * values[:, (j % 2) * HEAD : (j % 2 + 1) * HEAD]
                low = packed_right(split(right[:half]))
                high = packed_right(split(right[half:]))
                top, bottom, side = [
                    packed_left(split(solve_ref[j, which])) for which in range(3)
                ]
                write_low = fold(top, low)
                write_high = fold(side, low) + fold(bottom, high)
                write_ref[j, :half] = write_low
                write_ref[j, half:] = write_high
                trailing = turned_ref[i] * jnp.exp(row[:, count - 1 :] - row)
                trans_ref[j] = (
                    mul(trailing[:, :half], write_low) + mul(trailing[:, half:], write_high)
                ).astype(BF16)

    return call(
        body, sp, inputs, specs, outs, [pltpu.VMEM((RIM + count, 2 * HEAD), F32)], after=after,
    )


def query_phase(gathered, number, count, tables, parts, sp, after=()):
    inputs, specs, jobs = gathered
    received = (len(inputs) - 2) // len(jobs) - 2
    at = len(inputs)
    inputs = inputs + tables
    for part in parts:
        inputs = inputs + list(part)
    specs = specs + [whole(a) for a in inputs[at:]]
    half = count // 2
    outs = [
        jax.ShapeDtypeStruct((number, count, HEAD), F32),
        jax.ShapeDtypeStruct((number, count, HEAD), F32),
    ]
    total = len(inputs)
    group = parts[0][0].shape[0]

    def body(sp_ref, *refs):
        inner_ref, query_ref, scratch = refs[total:]
        sums, sums_col = refs[at][...], refs[at + 1][...]
        rows, cols = iotas(half)
        low, high = slice(0, half), slice(half, count)
        for i, job in enumerate(jobs):
            place = at + 3 + 3 * (i // group)
            key_ref, write_k_ref, write_v_ref = refs[place : place + 3]
            query = unit_rows(activate(refs, job, received, scratch))
            key = key_ref[i % group]
            left = [packed_left(split(query[span])) for span in (low, high)]
            right = [packed_turned(split(key[span])) for span in (low, high)]
            alike = {
                (0, 0): fold(left[0], right[0], NT),
                (1, 1): fold(left[1], right[1], NT),
                (1, 0): fold(left[1], right[0], NT),
            }
            for j in (2 * i, 2 * i + 1):
                row, col = sums[j : j + 1], sums_col[:, j : j + 1]
                wrote = [
                    split(
                        jnp.concatenate(
                            [part[j % (2 * group), span] for part in (write_v_ref, write_k_ref)],
                            axis=1,
                        )
                    )
                    for span in (low, high)
                ]
                tall = [jnp.concatenate([w[0], w[0]], axis=0) for w in wrote]
                read = [None, None]
                for (t, s), product in alike.items():
                    fade = jnp.exp(
                        jnp.minimum(col[(low, high)[t]] - row[:, (low, high)[s]], 0.0)
                    )
                    attend = fade * product
                    if t == s:
                        attend = jnp.where(cols <= rows, attend, 0.0)
                    attend = split(attend)
                    part = jnp.dot(
                        packed_left(attend), tall[s], preferred_element_type=F32
                    ) + jnp.dot(attend[0], wrote[s][1], preferred_element_type=F32)
                    read[t] = part if read[t] is None else read[t] + part
                for t, span in enumerate((low, high)):
                    inner_ref[j, span] = read[t][:, :HEAD]
                    query_ref[j, span] = jnp.exp(col[span]) * query[span] - read[t][:, HEAD:]

    return call(
        body, sp, inputs, specs, outs, [pltpu.VMEM((RIM + count, HEAD), F32)], after=after,
    )


def join_cores(mine_a, other_a, mine_b, other_b, sp, place, after=()):
    half = mine_a.shape[0] // 2
    inputs = [mine_a, other_a, mine_b, other_b]
    outs = [
        jax.ShapeDtypeStruct((2, half, HEAD, HEAD), BF16),
        jax.ShapeDtypeStruct((half, HEAD, HEAD), BF16),
    ]

    def body(sp_ref, *refs):
        core = sp_ref[place]
        for i in range(half):
            h = core * half + i
            held = [ref[h].astype(F32) for ref in refs[:4]]
            early_a, early_b = [jnp.where(core == 0, held[k], held[k + 1]) for k in (0, 2)]
            late_a, late_b = [jnp.where(core == 0, held[k + 1], held[k]) for k in (0, 2)]
            late = packed_left(split(late_a))
            write = (fold(late, packed_right(split(early_b))) + late_b).astype(BF16)
            refs[4][0, i] = fold(late, packed_right(split(early_a))).astype(BF16)
            refs[4][1, i] = write
            refs[5][i] = write

    return call(body, sp, inputs, [whole(a) for a in inputs], outs, after=after)


def run_chain(parts, sp, after=()):
    half = parts[0].shape[0]
    out = jax.ShapeDtypeStruct((half, HEAD, HEAD), BF16)

    def body(sp_ref, *refs):
        for i in range(half):
            state = refs[0][i].astype(F32)
            for ref in refs[1:-1]:
                left = ref[0, i]
                state = fold(
                    packed_left((left, jnp.zeros_like(left))), packed_right(split(state))
                ) + ref[1, i].astype(F32)
            refs[-1][i] = state.astype(BF16)

    return call(body, sp, parts, [whole(a) for a in parts], [out], after=after)[0]


def shifted(value, steps):
    count = lax.axis_size("ctx")
    return lax.ppermute(value, "ctx", [(i, i + steps) for i in range(count - steps)])


def swapped(value):
    count = lax.axis_size("ctx")
    return lax.ppermute(value, "ctx", [(i, i ^ 1) for i in range(count)])


def enter_far(joined):
    chips = lax.axis_size("ctx") // 2
    joined = shifted(joined, 2)
    step = 1
    while step < chips:
        early = shifted(joined, 2 * step).astype(F32)
        late = joined.astype(F32)
        both = jnp.einsum("hij,xhjk->xhik", late[0], early, precision=lax.Precision.HIGHEST)
        joined = (both + late * jnp.array([0.0, 1.0], F32)[:, None, None, None]).astype(BF16)
        step *= 2
    return joined[1]


def finish(inner, query, groups, gain, sp, place):
    inputs = [inner, query, gain]
    for part in groups:
        inputs += list(part)
    number, count = inner.shape[:2]
    group = groups[0][2].shape[0]
    half = group // 2
    out = jax.ShapeDtypeStruct((count, number * HEAD), BF16)

    def body(sp_ref, inner_ref, query_ref, gain_ref, *refs):
        core = sp_ref[place]
        keep = sp_ref[1].astype(F32)
        for j in range(number):
            at, h = 4 * (j // group), j % group
            mine, other, early_a, early_b = refs[at : at + 4]
            own, far = mine[h % half].astype(F32), other[h % half].astype(F32)
            state = jnp.where((core == 0) == (h < half), own, far)
            stepped = mul(early_a[h], state) + early_b[h].astype(F32)
            state = keep * jnp.where(core == 0, state, stepped)
            read = inner_ref[j] + mul(query_ref[j], state)
            scale = lax.rsqrt(jnp.mean(read * read, axis=-1, keepdims=True) + EPS)
            cols = slice(j * HEAD, (j + 1) * HEAD)
            refs[-1][:, cols] = (read * scale * gain_ref[...]).astype(BF16)

    return call(body, sp, inputs, [whole(a) for a in inputs], [out])[0]


def per_device(
    hidden,
    w_query,
    w_key,
    payload_projection_matrix,
    conv_weight,
    log_decay,
    beta_rate,
    norm_gain,
    head_order,
    block_starts,
):
    count = hidden.shape[0]
    ranks = lax.axis_size("head")
    chips = lax.axis_size("ctx") // 2
    total_heads = head_order.shape[0]
    key_heads = total_heads // ranks
    serve = lax.axis_index("head")
    core = lax.axis_index("ctx") % 2
    keep = 1 - block_starts[0]
    place = 2 + total_heads
    w_value = payload_projection_matrix

    rim = shifted(hidden[count - RIM :], 1) * keep.astype(BF16)
    sp = jnp.concatenate(
        [jnp.stack([serve, keep]), head_order, jnp.stack([core])]
    ).astype(jnp.int32)

    size = max(1, key_heads // 2)
    groups = [list(range(g, g + size)) for g in range(0, key_heads, size)]
    everyone = list(range(key_heads))

    def send(heads, width, weight, after=()):
        return partial_sums(key_heads, ranks, heads, width, hidden, rim, weight, sp, after)

    def gathered(heads, width, weight, base, received):
        return gather_specs(
            key_heads, heads, width, hidden, rim, weight, conv_weight, base, received
        )

    part_k = send(everyone, HEAD, w_key)
    got_k = exchange(part_k)
    tables = list(prepare(log_decay, beta_rate, sp, after=part_k[:1]))
    part_v = [send(groups[0], 2 * HEAD, w_value, after=tables[:1])]
    last = part_v[0][:1]
    keyed = []
    for g, heads in enumerate(groups):
        keyed.append(
            key_phase(
                gathered([(h, h) for h in heads], HEAD, w_key, total_heads, got_k),
                2 * heads[0], 2 * size, count, tables, sp, after=last,
            )
        )
        last = keyed[-1][4:]
        if g + 1 < len(groups):
            part_v.append(send(groups[g + 1], 2 * HEAD, w_value, after=last))
            last = part_v[-1][:1]
    got_v = [exchange(part) for part in part_v]
    other_a = [swapped(group[4]) for group in keyed]

    entered, wrote = [], []
    part_q = None
    for g, heads in enumerate(groups):
        write_v, trans_b = value_phase(
            gathered([(h, i) for i, h in enumerate(heads)], 2 * HEAD, w_value, total_heads, got_v[g]),
            2 * heads[0], 2 * size, count, tables, keyed[g][1], keyed[g][2], sp, after=last,
        )
        wrote.append((keyed[g][0], keyed[g][3], write_v))
        other_b = swapped(trans_b)
        last = [trans_b]
        if part_q is None:
            part_q = send(everyone, HEAD, w_query, after=last)
            got_q = exchange(part_q)
            last = part_q[:1]
        joined, joined_b = join_cores(
            keyed[g][4], other_a[g], trans_b, other_b, sp, place, after=last
        )
        last = [joined_b]
        entered.append([joined, joined_b, other_b])
    inner, query = query_phase(
        gathered([(h, h) for h in everyone], HEAD, w_query, 0, got_q),
        2 * key_heads, count, tables, wrote, sp, after=last,
    )
    last = [query]
    ends = []
    for g, (joined, joined_b, other_b) in enumerate(entered):
        if chips <= 4:
            far = [shifted(joined_b, 2 * (chips - 1))]
            far += [shifted(joined, 2 * d) for d in range(chips - 2, 0, -1)]
            mine = run_chain(far, sp, after=last)
            last = [mine]
        else:
            mine = enter_far(joined)
        ends.append((mine, swapped(mine), other_a[g], other_b))
    return finish(inner, query, ends, norm_gain[None, :], sp, place)


def solution(mesh):
    return jax.shard_map(
        per_device,
        mesh=mesh,
        in_specs=(
            P("ctx", None),
            P("head", None),
            P("head", None),
            P("head", None),
            P(),
            P("head", "ctx"),
            P("head", "ctx"),
            P(),
            P(),
            P("ctx"),
        ),
        out_specs=P("ctx", "head"),
        check_vma=False,
    )
```

```python
import functools

import jax
import jax.numpy as jnp
from jax import lax
from jax.experimental import pallas as pl
from jax.experimental.pallas import tpu as pltpu
from jax.sharding import PartitionSpec as P

HEAD = 128
TAPS = 4
RIM = 16
EPS = 1e-06
VMEM_BYTES = 20 * 1024 * 1024
F32 = jnp.float32
BF16 = jnp.bfloat16

NN = (((1,), (0,)), ((), ()))
NT = (((1,), (1,)), ((), ()))


def dot1(a, b, dims=NN):
    return lax.dot_general(
        a.astype(BF16), b.astype(BF16), dims, preferred_element_type=F32
    )


def split(a):
    high = a.astype(BF16)
    return high, (a - high.astype(F32)).astype(BF16)


def dot3s(a, b, dims=NN):
    (ah, al), (bh, bl) = a, b
    one = functools.partial(lax.dot_general, dimension_numbers=dims, preferred_element_type=F32)
    return one(ah, bh) + (one(ah, bl) + one(al, bh))


def dot3(a, b, dims=NN):
    return dot3s(split(a), split(b), dims)


def packed_left(parts):
    return jnp.concatenate(parts, axis=1)


def packed_right(parts):
    wide = jnp.concatenate(parts, axis=1)
    return jnp.concatenate([wide, wide], axis=0)


def packed_turned(parts):
    tall = jnp.concatenate(parts, axis=0)
    return jnp.concatenate([tall, tall], axis=1)


def fold(left, right, dims=NN):
    both = lax.dot_general(left, right, dims, preferred_element_type=F32)
    width = both.shape[1] // 2
    return both[:, :width] + both[:, width:]


def mul(a, b):
    return fold(packed_left(split(a)), packed_right(split(b)))


def dot_full(a, b, dims=NN):
    return lax.dot_general(
        a, b, dims, precision=lax.Precision.HIGHEST, preferred_element_type=F32
    )


def whole(array):
    zeros = (0,) * array.ndim
    return pl.BlockSpec(array.shape, lambda i, sp: zeros)


def call(
    body, sp, inputs, specs, outs, micros, scratch=(), after=()
):
    number = len(inputs)
    specs = list(specs) + [pl.BlockSpec(memory_space=pl.ANY) for _ in after]

    def inner(sp_ref, *refs):
        body(sp_ref, *refs[:number], *refs[number + len(after) :])

    return pl.pallas_call(
        inner,
        grid_spec=pltpu.PrefetchScalarGridSpec(
            num_scalar_prefetch=1,
            grid=(1,),
            in_specs=specs,
            out_specs=[whole(out) for out in outs],
            scratch_shapes=list(scratch),
        ),
        out_shape=[jax.ShapeDtypeStruct(out.shape, out.dtype) for out in outs],
        compiler_params=pltpu.CompilerParams(vmem_limit_bytes=VMEM_BYTES),
        cost_estimate=pl.CostEstimate(
            flops=int(micros * 10**9), bytes_accessed=1000, transcendentals=0
        ),
    )(sp, *inputs, *after)


def weight_spec(key_heads, rows, width, unit, head):
    return pl.BlockSpec(
        (rows, width), lambda i, sp: (0, sp[2 + (sp[0] ^ unit) * key_heads + head])
    )


def tap_spec(key_heads, width, base, head):
    return pl.BlockSpec(
        (TAPS, width), lambda i, sp: (0, base + sp[2 + sp[0] * key_heads + head])
    )


def hidden_spec(hidden, rows):
    return pl.BlockSpec((hidden.shape[0], rows), lambda i, sp: (0, sp[0]))


def partial_sums(key_heads, ranks, heads, width, hidden, rim, weight, sp, after=()):
    rows, count = weight.shape[0], hidden.shape[0]
    inputs, specs = [hidden, rim], [hidden_spec(hidden, rows), hidden_spec(rim, rows)]
    for unit in range(1, ranks):
        for head in heads:
            inputs.append(weight)
            specs.append(weight_spec(key_heads, rows, width, unit, head))
    outs = [jax.ShapeDtypeStruct((RIM + count, width * len(heads)), BF16)] * (ranks - 1)
    step = 2 if width == HEAD and len(heads) % 2 == 0 else 1

    def body(sp_ref, hidden_ref, rim_ref, *refs):
        for unit in range(ranks - 1):
            out = refs[(ranks - 1) * len(heads) + unit]
            for at in range(0, len(heads), step):
                place = unit * len(heads) + at
                held = [refs[place + i][...] for i in range(step)]
                held = held[0] if step == 1 else jnp.concatenate(held, axis=1)
                cols = slice(at * width, (at + step) * width)
                out[RIM:, cols] = plain(hidden_ref[...], held).astype(BF16)
                out[:RIM, cols] = plain(rim_ref[...], held).astype(BF16)

    return call(body, sp, inputs, specs, outs, 1.3, after=after)


def exchange(parts):
    ranks = len(parts) + 1
    return [
        lax.ppermute(part, "head", [(i, i ^ (unit + 1)) for i in range(ranks)])
        for unit, part in enumerate(parts)
    ]


class Halving:
    def __init__(self, ranks, heads):
        bits = [1 << i for i in range(ranks.bit_length() - 1)]
        cut = (len(heads) + 1) // 2
        self.ranks, self.stages = ranks, len(bits)
        self.routes = [
            (order, part) for order, part in ((bits, heads[:cut]), (bits[::-1], heads[cut:])) if part
        ]

    def offsets(self, route, stage):
        out = [0]
        for bit in self.routes[route][0][stage + 1 :]:
            out = out + [o ^ bit for o in out]
        return out

    def send(self, stage, key_heads, width, hidden, rim, weight, received, sp, after=()):
        rows, count = weight.shape[0], hidden.shape[0]
        inputs, specs = [hidden, rim], [hidden_spec(hidden, rows), hidden_spec(rim, rows)]
        jobs, outs = [], []
        for route, (order, heads) in enumerate(self.routes):
            first = len(inputs)
            inputs += received[route]
            specs += [whole(part) for part in received[route]]
            offsets = self.offsets(route, stage)
            for slot, offset in enumerate(offsets):
                unit = offset ^ order[stage]
                sources = [
                    (first + before, self.offsets(route, before).index(unit))
                    for before in range(stage)
                ]
                for at, head in enumerate(heads):
                    jobs.append((len(inputs), sources, route, slot, at))
                    inputs.append(weight)
                    specs.append(weight_spec(key_heads, rows, width, unit, head))
            shape = (len(offsets), RIM + count, width * len(heads))
            outs.append(jax.ShapeDtypeStruct(shape, BF16))
        total = len(inputs)

        def body(sp_ref, *refs):
            for place, sources, route, slot, at in jobs:
                held = refs[place][...]
                cols = slice(at * width, (at + 1) * width)
                for left, span in ((refs[0], slice(RIM, RIM + count)), (refs[1], slice(0, RIM))):
                    part = plain(left[...], held)
                    for source, index in sources:
                        part = part + refs[source][index, span, cols].astype(F32)
                    refs[total + route][slot, span, cols] = part.astype(BF16)

        return call(body, sp, inputs, specs, outs, 1.3, after=after)

    def exchange(self, stage, sent, received):
        for route, part in enumerate(sent):
            bit = self.routes[route][0][stage]
            pairs = [(i, i ^ bit) for i in range(self.ranks)]
            received[route].append(lax.ppermute(part, "head", pairs))

    def parts(self, head, width, received):
        route = [head in heads for _, heads in self.routes].index(True)
        at = self.routes[route][1].index(head)
        return [
            (part, pl.BlockSpec((None, part.shape[1], width), lambda i, sp: (0, 0, at)))
            for part in received[route]
        ]


def direct_parts(head, width, received):
    return [
        (part, pl.BlockSpec((part.shape[0], width), lambda i, sp: (0, head))) for part in received
    ]


def gather_specs(key_heads, width, hidden, rim, weight, taps, base, parts):
    rows = weight.shape[0]
    inputs = [hidden, rim]
    specs = [hidden_spec(hidden, rows), hidden_spec(rim, rows)]
    jobs = []
    for head, received in enumerate(parts):
        jobs.append(len(inputs))
        inputs += [weight, taps]
        specs += [
            weight_spec(key_heads, rows, width, 0, head), tap_spec(key_heads, width, base, head)
        ]
        for part, spec in received:
            inputs.append(part)
            specs.append(spec)
    return inputs, specs, jobs


def activate(refs, job, number, scratch):
    held, taps = refs[job][...], refs[job + 1][...].astype(F32)
    count = refs[0].shape[0]
    for left, span in ((refs[0], slice(RIM, RIM + count)), (refs[1], slice(0, RIM))):
        part = plain(left[...], held)
        for source in range(job + 2, job + 2 + number):
            part = part + refs[source][span, :].astype(F32)
        scratch[span, :] = part
    total = None
    for tap in range(TAPS):
        first = RIM - (TAPS - 1) + tap
        term = taps[tap : tap + 1] * scratch[first : first + count, :]
        total = term if total is None else total + term
    return total / (1.0 + jnp.exp(-total))


def plain(a, b):
    return jnp.dot(a, b, preferred_element_type=F32)


def unit_rows(values):
    return values * lax.rsqrt(jnp.sum(values * values, axis=-1, keepdims=True) + EPS)


def iotas(size):
    return (
        lax.broadcasted_iota(jnp.int32, (size, size), 0),
        lax.broadcasted_iota(jnp.int32, (size, size), 1),
    )


def prepare(decay, beta, sp, after=()):
    heads, count = decay.shape
    outs = [
        jax.ShapeDtypeStruct((heads, count), F32),
        jax.ShapeDtypeStruct((count, heads), F32),
        jax.ShapeDtypeStruct((count, heads), F32),
    ]

    def body(sp_ref, decay_ref, beta_ref, row_ref, col_ref, rate_ref):
        rows, cols = iotas(count)
        row_ref[...] = dot_full(decay_ref[...], (rows <= cols).astype(F32))
        col_ref[...] = dot_full((cols <= rows).astype(F32), decay_ref[...], NT)
        rate_ref[...] = dot_full((rows == cols).astype(F32), beta_ref[...], NT)

    return call(body, sp, [decay, beta], [whole(decay), whole(beta)], outs, 1.2, after=after)


def inverses(systems):
    size = systems[0].shape[0]
    rows, cols = iotas(size)
    eye = (rows == cols).astype(F32)
    cut = [split(low) for low in systems]
    mask = ((rows >> 2) == (cols >> 2)).astype(F32).astype(BF16)
    near = [c[0] * mask for c in cut]
    square = [plain(n, n) for n in near]
    cube = [plain(n, s.astype(BF16)) for n, s in zip(near, square)]
    inv = [
        (eye - n.astype(F32) + s - c).astype(BF16) for n, s, c in zip(near, square, cube)
    ]
    shift = 2
    while (1 << shift) < size:
        inside = ((rows >> (shift + 1)) == (cols >> (shift + 1))) & (
            (rows >> shift) != (cols >> shift)
        )
        mask = inside.astype(F32).astype(BF16)
        middle = [plain(c[0] * mask, x).astype(BF16) for c, x in zip(cut, inv)]
        inv = [x - plain(x, m).astype(BF16) for x, m in zip(inv, middle)]
        shift += 1
    rest = [
        eye - x.astype(F32) - plain(packed_left(c), jnp.concatenate([x, x], axis=0))
        for c, x in zip(cut, inv)
    ]
    return [x.astype(F32) + plain(x, r.astype(BF16)) for x, r in zip(inv, rest)]


def key_phase(gathered, number, count, tables, sp, after=()):
    inputs, specs, jobs = gathered
    received = (len(inputs) - 2) // len(jobs) - 2
    at = len(inputs)
    inputs = inputs + tables
    specs = specs + [whole(table) for table in tables]
    half = count // 2
    heads = range(number // 2)
    outs = [
        jax.ShapeDtypeStruct((len(heads), count, HEAD), F32),
        jax.ShapeDtypeStruct((number, 3, half, 2 * half), BF16),
        jax.ShapeDtypeStruct((number, 2, HEAD, 2 * half), BF16),
        jax.ShapeDtypeStruct((number, HEAD, HEAD), F32),
    ]
    total = len(inputs)

    def body(sp_ref, *refs):
        key_ref, solve_ref, gather_ref, trans_ref, scratch = refs[total:]
        sums, sums_col, beta_col = (ref[...] for ref in refs[at : at + 3])
        rows, cols = iotas(half)
        keys, turned, systems, crosses = [], [], [], []
        for i, job in enumerate(jobs):
            key = unit_rows(activate(refs, job, received, scratch))
            keys.append(key)
            key_ref[i] = key
            turned.append(key.T)
            low, high = split(key[:half]), split(key[half:])
            low_left, high_left = packed_left(low), packed_left(high)
            low_right, high_right = packed_turned(low), packed_turned(high)
            alike = (
                fold(low_left, low_right, NT),
                fold(high_left, high_right, NT),
                fold(high_left, low_right, NT),
            )
            for r in (2 * i, 2 * i + 1):
                row, col, rate = sums[r : r + 1], sums_col[:, r : r + 1], beta_col[:, r : r + 1]
                for b, span in enumerate((slice(0, half), slice(half, count))):
                    fade = jnp.exp(jnp.minimum(col[span] - row[:, span], 0.0))
                    systems.append(jnp.where(cols < rows, rate[span] * fade * alike[b], 0.0))
                fade = jnp.exp(jnp.minimum(col[half:] - row[:, :half], 0.0))
                crosses.append(rate[half:] * fade * alike[2])
        solved = inverses(systems)
        left = [packed_left(split(x)) for x in solved]
        middle = [
            mul(cross, solved[2 * j]) for j, cross in enumerate(crosses)
        ]
        corner = [
            -fold(left[2 * j + 1], packed_right(split(m))) for j, m in enumerate(middle)
        ]
        keep = sp_ref[1].astype(F32)
        eye = (lax.broadcasted_iota(jnp.int32, (HEAD, HEAD), 0)
               == lax.broadcasted_iota(jnp.int32, (HEAD, HEAD), 1)).astype(F32)
        for j in range(number):
            key = keys[j // 2]
            row, col, rate = sums[j : j + 1], sums_col[:, j : j + 1], beta_col[:, j : j + 1]
            side = split(corner[j])
            for which, part in enumerate((left[2 * j], left[2 * j + 1], packed_left(side))):
                solve_ref[j, which] = part
            trailing = turned[j // 2] * jnp.exp(row[:, count - 1 :] - row)
            low, high = [packed_left(split(t)) for t in (trailing[:, :half], trailing[:, half:])]
            taken = (
                fold(low, packed_right(split(solved[2 * j]))) + fold(high, packed_right(side)),
                fold(high, packed_right(split(solved[2 * j + 1]))),
            )
            right = (rate * jnp.exp(col)) * key
            moved = None
            for part, span in zip(taken, (slice(0, half), slice(half, count))):
                part = packed_left(split(part))
                gather_ref[j, 0 if span.start == 0 else 1] = part
                term = fold(part, packed_right(split(right[span])))
                moved = term if moved is None else moved + term
            gone = jnp.exp(row[:, count - 1 :])
            trans_ref[j] = keep * (gone * eye - moved)

    return call(
        body, sp, inputs, specs, outs, 5.0, [pltpu.VMEM((RIM + count, HEAD), F32)], after=after,
    )


def value_phase(gathered, number, count, tables, gathers, trans, sp, place, after=()):
    inputs, specs, jobs = gathered
    received = (len(inputs) - 2) // len(jobs) - 2
    at = len(inputs)
    inputs = inputs + tables + [gathers, trans]
    specs = specs + [whole(a) for a in inputs[at:]]
    half = count // 2
    outs = [
        jax.ShapeDtypeStruct((number, count, HEAD), F32),
        jax.ShapeDtypeStruct((2, number // 2, HEAD, HEAD), BF16),
        jax.ShapeDtypeStruct((2, number // 2, HEAD, HEAD), BF16),
    ]
    total = len(inputs)

    def body(sp_ref, *refs):
        write_ref, keep_ref, give_ref, scratch = refs[total:]
        beta_col = refs[at + 2][...]
        gather_ref, moved_ref = refs[at + 3 : at + 5]
        made = []
        for i, job in enumerate(jobs):
            values = activate(refs, job, received, scratch)
            for j in (2 * i, 2 * i + 1):
                right = beta_col[:, j : j + 1] * values[:, (j % 2) * HEAD : (j % 2 + 1) * HEAD]
                write_ref[j] = right
                made.append(
                    fold(gather_ref[j, 0], packed_right(split(right[:half])))
                    + fold(gather_ref[j, 1], packed_right(split(right[half:])))
                )
        first = sp_ref[place] == 0
        for i in range(number // 2):
            k = i + number // 2
            for ref, mine in ((keep_ref, first), (give_ref, jnp.logical_not(first))):
                ref[0, i] = jnp.where(mine, moved_ref[i], moved_ref[k]).astype(BF16)
                ref[1, i] = jnp.where(mine, made[i], made[k]).astype(BF16)

    return call(
        body, sp, inputs, specs, outs, 0.05, [pltpu.VMEM((RIM + count, 2 * HEAD), F32)], after=after,
    )


def write_phase(right, keys, tables, solve, sp, after=()):
    number, count = right.shape[:2]
    half = count // 2
    inputs = [right, keys, *tables, solve]
    out = jax.ShapeDtypeStruct((number, count, 2 * HEAD), F32)

    def body(sp_ref, right_ref, key_ref, _, col_ref, rate_ref, solve_ref, out_ref):
        for j in range(number):
            col, rate = col_ref[:, j : j + 1], rate_ref[:, j : j + 1]
            both = jnp.concatenate([right_ref[j], (rate * jnp.exp(col)) * key_ref[j // 2]], axis=1)
            parts = []
            for span in (slice(0, half), slice(half, count)):
                high, low = split(both[span])
                parts.append((jnp.concatenate([high, high], axis=0), low))

            def solved(which, part):
                left = solve_ref[j, which]
                return plain(left, part[0]) + plain(left[:, :half], part[1])

            out_ref[j, :half] = solved(0, parts[0])
            out_ref[j, half:] = solved(2, parts[0]) + solved(1, parts[1])

    return call(body, sp, inputs, [whole(a) for a in inputs], [out], 0.05, after=after)[0]


def query_phase(gathered, number, count, tables, keys, writes, sp, after=()):
    inputs, specs, jobs = gathered
    received = (len(inputs) - 2) // len(jobs) - 2
    at = len(inputs)
    inputs = inputs + tables + [keys, writes]
    specs = specs + [whole(a) for a in inputs[at:]]
    half = count // 2
    outs = [
        jax.ShapeDtypeStruct((number, count, HEAD), F32),
        jax.ShapeDtypeStruct((number, count, HEAD), BF16),
    ]
    total = len(inputs)

    def body(sp_ref, *refs):
        inner_ref, query_ref, scratch = refs[total:]
        sums, sums_col = refs[at][...], refs[at + 1][...]
        rows, cols = iotas(half)
        low, high = slice(0, half), slice(half, count)
        for i, job in enumerate(jobs):
            key_ref, write_ref = refs[at + 3 : at + 5]
            query = unit_rows(activate(refs, job, received, scratch))
            key = key_ref[i]
            left = [packed_left(split(query[span])) for span in (low, high)]
            right = [packed_turned(split(key[span])) for span in (low, high)]
            alike = {
                (0, 0): fold(left[0], right[0], NT),
                (1, 1): fold(left[1], right[1], NT),
                (1, 0): fold(left[1], right[0], NT),
            }
            for j in (2 * i, 2 * i + 1):
                row, col = sums[j : j + 1], sums_col[:, j : j + 1]
                wrote = [split(write_ref[j, span]) for span in (low, high)]
                tall = [jnp.concatenate([w[0], w[0]], axis=0) for w in wrote]
                read = [None, None]
                for (t, s), product in alike.items():
                    fade = jnp.exp(
                        jnp.minimum(col[(low, high)[t]] - row[:, (low, high)[s]], 0.0)
                    )
                    attend = fade * product
                    if t == s:
                        attend = jnp.where(cols <= rows, attend, 0.0)
                    attend = split(attend)
                    part = jnp.dot(
                        packed_left(attend), tall[s], preferred_element_type=F32
                    ) + jnp.dot(attend[0], wrote[s][1], preferred_element_type=F32)
                    read[t] = part if read[t] is None else read[t] + part
                for t, span in enumerate((low, high)):
                    inner_ref[j, span] = read[t][:, :HEAD]
                    read_in = jnp.exp(col[span]) * query[span] - read[t][:, HEAD:]
                    query_ref[j, span] = read_in.astype(BF16)

    return call(
        body, sp, inputs, specs, outs, 3.7, [pltpu.VMEM((RIM + count, HEAD), F32)], after=after,
    )


def join_cores(mine, other, sp, place, after=()):
    half = mine.shape[1]
    outs = [
        jax.ShapeDtypeStruct((2, half, HEAD, HEAD), BF16),
        jax.ShapeDtypeStruct((half, HEAD, HEAD), BF16),
    ]

    def body(sp_ref, mine_ref, other_ref, both_ref, write_ref):
        first = sp_ref[place] == 0
        for i in range(half):
            held = [(mine_ref[k, i].astype(F32), other_ref[k, i].astype(F32)) for k in (0, 1)]
            early = [jnp.where(first, pair[0], pair[1]) for pair in held]
            late = [jnp.where(first, pair[1], pair[0]) for pair in held]
            left = late[0].astype(BF16)
            write = plain(left, early[1].astype(BF16)) + late[1]
            both_ref[0, i] = plain(left, early[0].astype(BF16)).astype(BF16)
            both_ref[1, i] = write.astype(BF16)
            write_ref[i] = write.astype(BF16)

    inputs = [mine, other]
    return call(body, sp, inputs, [whole(a) for a in inputs], outs, 0.05, after=after)


def pass_chip(joined, states, sp, after=()):
    half = states[0].shape[0]
    outs = [jax.ShapeDtypeStruct((half, HEAD, HEAD), BF16)] * 2
    inputs = [joined, *states]

    def body(sp_ref, joined_ref, *refs):
        for i in range(half):
            state = sum(ref[i].astype(F32) for ref in refs[:-2]).astype(BF16)
            stepped = plain(joined_ref[0, i], state)
            refs[-2][i] = (stepped + joined_ref[1, i].astype(F32)).astype(BF16)
            refs[-1][i] = state

    return call(body, sp, inputs, [whole(a) for a in inputs], outs, 0.05, after=after)


def shifted(value, steps):
    count = lax.axis_size("ctx")
    return lax.ppermute(value, "ctx", [(i, i + steps) for i in range(count - steps)])


def swapped(value):
    count = lax.axis_size("ctx")
    return lax.ppermute(value, "ctx", [(i, i ^ 1) for i in range(count)])


def enter_far(joined):
    chips = lax.axis_size("ctx") // 2
    joined = shifted(joined, 2)
    step = 1
    while step < chips:
        early = shifted(joined, 2 * step).astype(F32)
        late = joined.astype(F32)
        both = jnp.einsum("hij,xhjk->xhik", late[0], early, precision=lax.Precision.HIGHEST)
        joined = (both + late * jnp.array([0.0, 1.0], F32)[:, None, None, None]).astype(BF16)
        step *= 2
    return joined[1]


def finish(inner, query, mine, others, early, gain, sp, place):
    inputs = [inner, query, *early, gain, *mine, *others]
    number, count = inner.shape[:2]
    half = number // 2
    out = jax.ShapeDtypeStruct((count, number * HEAD), BF16)

    def body(sp_ref, inner_ref, query_ref, low_ref, high_ref, gain_ref, *refs):
        core = sp_ref[place]
        keep = sp_ref[1].astype(F32)
        for j in range(number):
            i, early_ref = j % half, (low_ref, high_ref)[j // half]
            own, far = [
                sum(ref[i].astype(F32) for ref in part)
                for part in (refs[: len(mine)], refs[len(mine) : 2 * len(mine)])
            ]
            state = jnp.where((core == 0) == (j < half), own, far)
            stepped = plain(early_ref[0, i], state.astype(BF16)) + early_ref[1, i].astype(F32)
            state = keep * jnp.where(core == 0, state, stepped)
            read = inner_ref[j] + plain(query_ref[j], state.astype(BF16))
            scale = lax.rsqrt(jnp.mean(read * read, axis=-1, keepdims=True) + EPS)
            cols = slice(j * HEAD, (j + 1) * HEAD)
            refs[-1][:, cols] = (read * scale * gain_ref[...]).astype(BF16)

    return call(body, sp, inputs, [whole(a) for a in inputs], [out], 2.7)[0]


def per_device(
    hidden,
    w_query,
    w_key,
    payload_projection_matrix,
    conv_weight,
    log_decay,
    beta_rate,
    norm_gain,
    head_order,
    block_starts,
):
    count = hidden.shape[0]
    ranks = lax.axis_size("head")
    chips = lax.axis_size("ctx") // 2
    total_heads = head_order.shape[0]
    key_heads = total_heads // ranks
    number = 2 * key_heads
    serve, spot = lax.axis_index("head"), lax.axis_index("ctx")
    keep = 1 - block_starts[0]
    place = 2 + total_heads
    w_value = payload_projection_matrix

    rim = shifted(hidden[count - RIM :], 1) * keep.astype(BF16)
    sp = jnp.concatenate(
        [jnp.stack([serve, keep]), head_order, jnp.stack([spot % 2])]
    ).astype(jnp.int32)

    everyone = list(range(key_heads))
    halving = Halving(ranks, everyone)

    def gathered(width, weight, base, parts):
        return gather_specs(key_heads, width, hidden, rim, weight, conv_weight, base, parts)

    part_k = partial_sums(key_heads, ranks, everyone, HEAD, hidden, rim, w_key, sp)
    got_k = exchange(part_k)
    tables = list(prepare(log_decay, beta_rate, sp, after=part_k[:1]))
    got_v = [[] for _ in halving.routes]
    part_v = halving.send(
        0, key_heads, 2 * HEAD, hidden, rim, w_value, got_v, sp, after=tables[:1]
    )
    halving.exchange(0, part_v, got_v)
    part_q = partial_sums(
        key_heads, ranks, everyone, HEAD, hidden, rim, w_query, sp, after=part_v[:1]
    )
    keys, solve, gathers, trans_a = key_phase(
        gathered(HEAD, w_key, total_heads, [direct_parts(h, HEAD, got_k) for h in everyone]),
        number, count, tables, sp, after=part_q[:1],
    )
    ordered = [trans_a]
    for stage in range(1, halving.stages):
        part_v = halving.send(
            stage, key_heads, 2 * HEAD, hidden, rim, w_value, got_v, sp, after=ordered
        )
        halving.exchange(stage, part_v, got_v)
        ordered = part_v[:1]
    part_q, _ = lax.optimization_barrier((part_q, ordered[0]))
    got_q = exchange(part_q)
    right, own, given = value_phase(
        gathered(
            2 * HEAD, w_value, total_heads,
            [halving.parts(h, 2 * HEAD, got_v) for h in everyone],
        ),
        number, count, tables, gathers, trans_a, sp, place, after=ordered,
    )
    taken = swapped(given)
    joined, joined_b = join_cores(own, taken, sp, place)
    early = swapped(own)
    states, last, writes = [], joined_b, None
    if chips <= 4:
        for chip in range(chips - 1):
            if chip:
                after = [] if writes is None else [writes, early]
                last, so_far = pass_chip(joined, states, sp, after)
                states = [so_far]
            hop = [(2 * chip + c, 2 * chip + 2 + c) for c in range(2)]
            states.append(lax.ppermute(last, "ctx", hop))
            if writes is None and chip + 1 >= min(2, chips - 1):
                writes = write_phase(right, keys, tables, solve, sp, after=[last])
    else:
        states = [enter_far(joined)]
    if writes is None:
        writes = write_phase(right, keys, tables, solve, sp, after=[last])
    inner, query = query_phase(
        gathered(HEAD, w_query, 0, [direct_parts(h, HEAD, got_q) for h in everyone]),
        number, count, tables, keys, writes, sp, after=[last],
    )
    others = [swapped(state) for state in states[:-1]]
    final, _ = lax.optimization_barrier((states[-1], inner))
    return finish(
        inner, query, [*states[:-1], final], [*others, swapped(final)], (early, taken),
        norm_gain[None, :], sp, place,
    )


def solution(mesh):
    return jax.shard_map(
        per_device,
        mesh=mesh,
        in_specs=(
            P("ctx", None),
            P("head", None),
            P("head", None),
            P("head", None),
            P(),
            P("head", "ctx"),
            P("head", "ctx"),
            P(),
            P(),
            P("ctx"),
        ),
        out_specs=P("ctx", "head"),
        check_vma=False,
    )
```

```python
import functools

import jax
import jax.numpy as jnp
from jax import lax
from jax.experimental import pallas as pl
from jax.experimental.pallas import tpu as pltpu
from jax.sharding import PartitionSpec as P

HEAD = 128
TAPS = 4
RIM = 16
EPS = 1e-06
VMEM_BYTES = 20 * 1024 * 1024
F32 = jnp.float32
BF16 = jnp.bfloat16

NN = (((1,), (0,)), ((), ()))
NT = (((1,), (1,)), ((), ()))


def dot1(a, b, dims=NN):
    return lax.dot_general(
        a.astype(BF16), b.astype(BF16), dims, preferred_element_type=F32
    )


def split(a):
    high = a.astype(BF16)
    return high, (a - high.astype(F32)).astype(BF16)


def dot3s(a, b, dims=NN):
    (ah, al), (bh, bl) = a, b
    one = functools.partial(lax.dot_general, dimension_numbers=dims, preferred_element_type=F32)
    return one(ah, bh) + (one(ah, bl) + one(al, bh))


def dot3(a, b, dims=NN):
    return dot3s(split(a), split(b), dims)


def packed_left(parts):
    return jnp.concatenate(parts, axis=1)


def packed_right(parts):
    wide = jnp.concatenate(parts, axis=1)
    return jnp.concatenate([wide, wide], axis=0)


def packed_turned(parts):
    tall = jnp.concatenate(parts, axis=0)
    return jnp.concatenate([tall, tall], axis=1)


def fold(left, right, dims=NN):
    both = lax.dot_general(left, right, dims, preferred_element_type=F32)
    width = both.shape[1] // 2
    return both[:, :width] + both[:, width:]


def mul(a, b):
    return fold(packed_left(split(a)), packed_right(split(b)))


def dot_full(a, b, dims=NN):
    return lax.dot_general(
        a, b, dims, precision=lax.Precision.HIGHEST, preferred_element_type=F32
    )


def whole(array):
    zeros = (0,) * array.ndim
    return pl.BlockSpec(array.shape, lambda i, sp: zeros)


def call(
    body, sp, inputs, specs, outs, micros, scratch=(), after=()
):
    number = len(inputs)
    specs = list(specs) + [pl.BlockSpec(memory_space=pl.ANY) for _ in after]

    def inner(sp_ref, *refs):
        body(sp_ref, *refs[:number], *refs[number + len(after) :])

    return pl.pallas_call(
        inner,
        grid_spec=pltpu.PrefetchScalarGridSpec(
            num_scalar_prefetch=1,
            grid=(1,),
            in_specs=specs,
            out_specs=[whole(out) for out in outs],
            scratch_shapes=list(scratch),
        ),
        out_shape=[jax.ShapeDtypeStruct(out.shape, out.dtype) for out in outs],
        compiler_params=pltpu.CompilerParams(vmem_limit_bytes=VMEM_BYTES),
        cost_estimate=pl.CostEstimate(
            flops=int(micros * 10**9), bytes_accessed=1000, transcendentals=0
        ),
    )(sp, *inputs, *after)


def weight_spec(key_heads, rows, width, unit, head):
    return pl.BlockSpec(
        (rows, width), lambda i, sp: (0, sp[2 + (sp[0] ^ unit) * key_heads + head])
    )


def tap_spec(key_heads, width, base, head):
    return pl.BlockSpec(
        (TAPS, width), lambda i, sp: (0, base + sp[2 + sp[0] * key_heads + head])
    )


def hidden_spec(hidden, rows):
    return whole(hidden)


def partial_sums(key_heads, ranks, heads, width, hidden, rim, weight, sp, after=()):
    rows, count = weight.shape[0], hidden.shape[0]
    inputs, specs = [hidden, rim], [hidden_spec(hidden, rows), hidden_spec(rim, rows)]
    for unit in range(1, ranks):
        for head in heads:
            inputs.append(weight)
            specs.append(weight_spec(key_heads, rows, width, unit, head))
    outs = [jax.ShapeDtypeStruct((RIM + count, width * len(heads)), BF16)] * (ranks - 1)
    step = 2 if width == HEAD and len(heads) % 2 == 0 else 1

    def body(sp_ref, hidden_ref, rim_ref, *refs):
        for unit in range(ranks - 1):
            out = refs[(ranks - 1) * len(heads) + unit]
            for at in range(0, len(heads), step):
                place = unit * len(heads) + at
                held = [refs[place + i][...] for i in range(step)]
                held = held[0] if step == 1 else jnp.concatenate(held, axis=1)
                cols = slice(at * width, (at + step) * width)
                out[RIM:, cols] = plain(hidden_ref[...], held).astype(BF16)
                out[:RIM, cols] = plain(rim_ref[...], held).astype(BF16)

    return call(body, sp, inputs, specs, outs, 1.3, after=after)


def exchange(parts):
    ranks = len(parts) + 1
    return [
        lax.ppermute(part, "head", [(i, i ^ (unit + 1)) for i in range(ranks)])
        for unit, part in enumerate(parts)
    ]


class Halving:
    def __init__(self, ranks, heads):
        bits = [1 << i for i in range(ranks.bit_length() - 1)]
        cut = (len(heads) + 1) // 2
        self.ranks, self.stages = ranks, len(bits)
        self.routes = [
            (order, part) for order, part in ((bits, heads[:cut]), (bits[::-1], heads[cut:])) if part
        ]

    def offsets(self, route, stage):
        out = [0]
        for bit in self.routes[route][0][stage + 1 :]:
            out = out + [o ^ bit for o in out]
        return out

    def send(self, stage, key_heads, width, hidden, rim, weight, received, sp, after=()):
        rows, count = weight.shape[0], hidden.shape[0]
        inputs, specs = [hidden, rim], [hidden_spec(hidden, rows), hidden_spec(rim, rows)]
        jobs, outs = [], []
        for route, (order, heads) in enumerate(self.routes):
            first = len(inputs)
            inputs += received[route]
            specs += [whole(part) for part in received[route]]
            offsets = self.offsets(route, stage)
            for slot, offset in enumerate(offsets):
                unit = offset ^ order[stage]
                sources = [
                    (first + before, self.offsets(route, before).index(unit))
                    for before in range(stage)
                ]
                for at, head in enumerate(heads):
                    jobs.append((len(inputs), sources, route, slot, at))
                    inputs.append(weight)
                    specs.append(weight_spec(key_heads, rows, width, unit, head))
            shape = (len(offsets), RIM + count, width * len(heads))
            outs.append(jax.ShapeDtypeStruct(shape, BF16))
        total = len(inputs)

        def body(sp_ref, *refs):
            for place, sources, route, slot, at in jobs:
                held = refs[place][...]
                cols = slice(at * width, (at + 1) * width)
                for left, span in ((refs[0], slice(RIM, RIM + count)), (refs[1], slice(0, RIM))):
                    part = plain(left[...], held)
                    for source, index in sources:
                        part = part + refs[source][index, span, cols].astype(F32)
                    refs[total + route][slot, span, cols] = part.astype(BF16)

        return call(body, sp, inputs, specs, outs, 1.3, after=after)

    def exchange(self, stage, sent, received):
        for route, part in enumerate(sent):
            bit = self.routes[route][0][stage]
            pairs = [(i, i ^ bit) for i in range(self.ranks)]
            received[route].append(lax.ppermute(part, "head", pairs))

    def parts(self, head, width, received):
        route = [head in heads for _, heads in self.routes].index(True)
        at = self.routes[route][1].index(head)
        return [
            (part, pl.BlockSpec((None, part.shape[1], width), lambda i, sp: (0, 0, at)))
            for part in received[route]
        ]


def direct_parts(head, width, received):
    return [
        (part, pl.BlockSpec((part.shape[0], width), lambda i, sp: (0, head))) for part in received
    ]


def gather_specs(key_heads, width, hidden, rim, weight, taps, base, parts):
    rows = weight.shape[0]
    inputs = [hidden, rim]
    specs = [hidden_spec(hidden, rows), hidden_spec(rim, rows)]
    jobs = []
    for head, received in enumerate(parts):
        jobs.append(len(inputs))
        inputs += [weight, taps]
        specs += [
            weight_spec(key_heads, rows, width, 0, head), tap_spec(key_heads, width, base, head)
        ]
        for part, spec in received:
            inputs.append(part)
            specs.append(spec)
    return inputs, specs, jobs


def activate(refs, job, number, scratch):
    held, taps = refs[job][...], refs[job + 1][...].astype(F32)
    count = refs[0].shape[0]
    for left, span in ((refs[0], slice(RIM, RIM + count)), (refs[1], slice(0, RIM))):
        part = plain(left[...], held)
        for source in range(job + 2, job + 2 + number):
            part = part + refs[source][span, :].astype(F32)
        scratch[span, :] = part
    total = None
    for tap in range(TAPS):
        first = RIM - (TAPS - 1) + tap
        term = taps[tap : tap + 1] * scratch[first : first + count, :]
        total = term if total is None else total + term
    return total / (1.0 + jnp.exp(-total))


def plain(a, b):
    return jnp.dot(a, b, preferred_element_type=F32)


def unit_rows(values):
    return values * lax.rsqrt(jnp.sum(values * values, axis=-1, keepdims=True) + EPS)


def iotas(size):
    return (
        lax.broadcasted_iota(jnp.int32, (size, size), 0),
        lax.broadcasted_iota(jnp.int32, (size, size), 1),
    )


def prepare(decay, beta, sp, after=()):
    heads, count = decay.shape
    outs = [
        jax.ShapeDtypeStruct((heads, count), F32),
        jax.ShapeDtypeStruct((count, heads), F32),
        jax.ShapeDtypeStruct((count, heads), F32),
    ]

    def body(sp_ref, decay_ref, beta_ref, row_ref, col_ref, rate_ref):
        rows, cols = iotas(count)
        row_ref[...] = dot_full(decay_ref[...], (rows <= cols).astype(F32))
        col_ref[...] = dot_full((cols <= rows).astype(F32), decay_ref[...], NT)
        rate_ref[...] = dot_full((rows == cols).astype(F32), beta_ref[...], NT)

    return call(body, sp, [decay, beta], [whole(decay), whole(beta)], outs, 1.2, after=after)


def inverses(systems):
    size = systems[0].shape[0]
    rows, cols = iotas(size)
    eye = (rows == cols).astype(F32)
    cut = [split(low) for low in systems]
    mask = ((rows >> 2) == (cols >> 2)).astype(F32).astype(BF16)
    near = [c[0] * mask for c in cut]
    square = [plain(n, n) for n in near]
    cube = [plain(n, s.astype(BF16)) for n, s in zip(near, square)]
    inv = [
        (eye - n.astype(F32) + s - c).astype(BF16) for n, s, c in zip(near, square, cube)
    ]
    shift = 2
    while (1 << shift) < size:
        inside = ((rows >> (shift + 1)) == (cols >> (shift + 1))) & (
            (rows >> shift) != (cols >> shift)
        )
        mask = inside.astype(F32).astype(BF16)
        middle = [plain(c[0] * mask, x).astype(BF16) for c, x in zip(cut, inv)]
        inv = [x - plain(x, m).astype(BF16) for x, m in zip(inv, middle)]
        shift += 1
    rest = [
        eye - x.astype(F32) - plain(packed_left(c), jnp.concatenate([x, x], axis=0))
        for c, x in zip(cut, inv)
    ]
    return [x.astype(F32) + plain(x, r.astype(BF16)) for x, r in zip(inv, rest)]


def key_phase(gathered, number, count, tables, sp, after=()):
    inputs, specs, jobs = gathered
    received = (len(inputs) - 2) // len(jobs) - 2
    at = len(inputs)
    inputs = inputs + tables
    specs = specs + [whole(table) for table in tables]
    half = count // 2
    heads = range(number // 2)
    outs = [
        jax.ShapeDtypeStruct((len(heads), count, HEAD), F32),
        jax.ShapeDtypeStruct((number, 3, half, 2 * half), BF16),
        jax.ShapeDtypeStruct((number, 2, HEAD, 2 * half), BF16),
        jax.ShapeDtypeStruct((number, HEAD, HEAD), F32),
    ]
    total = len(inputs)

    def body(sp_ref, *refs):
        key_ref, solve_ref, gather_ref, trans_ref, scratch = refs[total:]
        sums, sums_col, beta_col = (ref[...] for ref in refs[at : at + 3])
        rows, cols = iotas(half)
        keys, turned, systems, crosses = [], [], [], []
        for i, job in enumerate(jobs):
            key = unit_rows(activate(refs, job, received, scratch))
            keys.append(key)
            key_ref[i] = key
            turned.append(key.T)
            low, high = split(key[:half]), split(key[half:])
            low_left, high_left = packed_left(low), packed_left(high)
            low_right, high_right = packed_turned(low), packed_turned(high)
            alike = (
                fold(low_left, low_right, NT),
                fold(high_left, high_right, NT),
                fold(high_left, low_right, NT),
            )
            for r in (2 * i, 2 * i + 1):
                row, col, rate = sums[r : r + 1], sums_col[:, r : r + 1], beta_col[:, r : r + 1]
                for b, span in enumerate((slice(0, half), slice(half, count))):
                    fade = jnp.exp(jnp.minimum(col[span] - row[:, span], 0.0))
                    systems.append(jnp.where(cols < rows, rate[span] * fade * alike[b], 0.0))
                fade = jnp.exp(jnp.minimum(col[half:] - row[:, :half], 0.0))
                crosses.append(rate[half:] * fade * alike[2])
        solved = inverses(systems)
        left = [packed_left(split(x)) for x in solved]
        middle = [
            mul(cross, solved[2 * j]) for j, cross in enumerate(crosses)
        ]
        corner = [
            -fold(left[2 * j + 1], packed_right(split(m))) for j, m in enumerate(middle)
        ]
        keep = sp_ref[1].astype(F32)
        eye = (lax.broadcasted_iota(jnp.int32, (HEAD, HEAD), 0)
               == lax.broadcasted_iota(jnp.int32, (HEAD, HEAD), 1)).astype(F32)
        for j in range(number):
            key = keys[j // 2]
            row, col, rate = sums[j : j + 1], sums_col[:, j : j + 1], beta_col[:, j : j + 1]
            side = split(corner[j])
            for which, part in enumerate((left[2 * j], left[2 * j + 1], packed_left(side))):
                solve_ref[j, which] = part
            trailing = turned[j // 2] * jnp.exp(row[:, count - 1 :] - row)
            low, high = [packed_left(split(t)) for t in (trailing[:, :half], trailing[:, half:])]
            taken = (
                fold(low, packed_right(split(solved[2 * j]))) + fold(high, packed_right(side)),
                fold(high, packed_right(split(solved[2 * j + 1]))),
            )
            right = (rate * jnp.exp(col)) * key
            moved = None
            for part, span in zip(taken, (slice(0, half), slice(half, count))):
                part = packed_left(split(part))
                gather_ref[j, 0 if span.start == 0 else 1] = part
                term = fold(part, packed_right(split(right[span])))
                moved = term if moved is None else moved + term
            gone = jnp.exp(row[:, count - 1 :])
            trans_ref[j] = keep * (gone * eye - moved)

    return call(
        body, sp, inputs, specs, outs, 5.0, [pltpu.VMEM((RIM + count, HEAD), F32)], after=after,
    )


def value_phase(gathered, number, count, tables, gathers, trans, sp, place, after=()):
    inputs, specs, jobs = gathered
    received = (len(inputs) - 2) // len(jobs) - 2
    at = len(inputs)
    inputs = inputs + tables + [gathers, trans]
    specs = specs + [whole(a) for a in inputs[at:]]
    half = count // 2
    outs = [
        jax.ShapeDtypeStruct((number, count, HEAD), F32),
        jax.ShapeDtypeStruct((2, number // 2, HEAD, HEAD), BF16),
        jax.ShapeDtypeStruct((2, number // 2, HEAD, HEAD), BF16),
    ]
    total = len(inputs)

    def body(sp_ref, *refs):
        write_ref, keep_ref, give_ref, scratch = refs[total:]
        beta_col = refs[at + 2][...]
        gather_ref, moved_ref = refs[at + 3 : at + 5]
        made = []
        for i, job in enumerate(jobs):
            values = activate(refs, job, received, scratch)
            for j in (2 * i, 2 * i + 1):
                right = beta_col[:, j : j + 1] * values[:, (j % 2) * HEAD : (j % 2 + 1) * HEAD]
                write_ref[j] = right
                made.append(
                    fold(gather_ref[j, 0], packed_right(split(right[:half])))
                    + fold(gather_ref[j, 1], packed_right(split(right[half:])))
                )
        first = sp_ref[place] == 0
        for i in range(number // 2):
            k = i + number // 2
            for ref, mine in ((keep_ref, first), (give_ref, jnp.logical_not(first))):
                ref[0, i] = jnp.where(mine, moved_ref[i], moved_ref[k]).astype(BF16)
                ref[1, i] = jnp.where(mine, made[i], made[k]).astype(BF16)

    return call(
        body, sp, inputs, specs, outs, 0.05, [pltpu.VMEM((RIM + count, 2 * HEAD), F32)], after=after,
    )


def write_phase(right, keys, tables, solve, sp, after=()):
    number, count = right.shape[:2]
    half = count // 2
    inputs = [right, keys, *tables, solve]
    out = jax.ShapeDtypeStruct((number, count, 2 * HEAD), F32)

    def body(sp_ref, right_ref, key_ref, _, col_ref, rate_ref, solve_ref, out_ref):
        for j in range(number):
            col, rate = col_ref[:, j : j + 1], rate_ref[:, j : j + 1]
            both = jnp.concatenate([right_ref[j], (rate * jnp.exp(col)) * key_ref[j // 2]], axis=1)
            parts = []
            for span in (slice(0, half), slice(half, count)):
                high, low = split(both[span])
                parts.append((jnp.concatenate([high, high], axis=0), low))

            def solved(which, part):
                left = solve_ref[j, which]
                return plain(left, part[0]) + plain(left[:, :half], part[1])

            out_ref[j, :half] = solved(0, parts[0])
            out_ref[j, half:] = solved(2, parts[0]) + solved(1, parts[1])

    return call(body, sp, inputs, [whole(a) for a in inputs], [out], 0.05, after=after)[0]


def query_phase(gathered, number, count, tables, keys, writes, sp, after=()):
    inputs, specs, jobs = gathered
    received = (len(inputs) - 2) // len(jobs) - 2
    at = len(inputs)
    inputs = inputs + tables + [keys, writes]
    specs = specs + [whole(a) for a in inputs[at:]]
    half = count // 2
    outs = [
        jax.ShapeDtypeStruct((number, count, HEAD), F32),
        jax.ShapeDtypeStruct((number, count, HEAD), BF16),
    ]
    total = len(inputs)

    def body(sp_ref, *refs):
        inner_ref, query_ref, scratch = refs[total:]
        sums, sums_col = refs[at][...], refs[at + 1][...]
        rows, cols = iotas(half)
        low, high = slice(0, half), slice(half, count)
        for i, job in enumerate(jobs):
            key_ref, write_ref = refs[at + 3 : at + 5]
            query = unit_rows(activate(refs, job, received, scratch))
            key = key_ref[i]
            left = [packed_left(split(query[span])) for span in (low, high)]
            right = [packed_turned(split(key[span])) for span in (low, high)]
            alike = {
                (0, 0): fold(left[0], right[0], NT),
                (1, 1): fold(left[1], right[1], NT),
                (1, 0): fold(left[1], right[0], NT),
            }
            for j in (2 * i, 2 * i + 1):
                row, col = sums[j : j + 1], sums_col[:, j : j + 1]
                wrote = [split(write_ref[j, span]) for span in (low, high)]
                tall = [jnp.concatenate([w[0], w[0]], axis=0) for w in wrote]
                read = [None, None]
                for (t, s), product in alike.items():
                    fade = jnp.exp(
                        jnp.minimum(col[(low, high)[t]] - row[:, (low, high)[s]], 0.0)
                    )
                    attend = fade * product
                    if t == s:
                        attend = jnp.where(cols <= rows, attend, 0.0)
                    attend = split(attend)
                    part = jnp.dot(
                        packed_left(attend), tall[s], preferred_element_type=F32
                    ) + jnp.dot(attend[0], wrote[s][1], preferred_element_type=F32)
                    read[t] = part if read[t] is None else read[t] + part
                for t, span in enumerate((low, high)):
                    inner_ref[j, span] = read[t][:, :HEAD]
                    read_in = jnp.exp(col[span]) * query[span] - read[t][:, HEAD:]
                    query_ref[j, span] = read_in.astype(BF16)

    return call(
        body, sp, inputs, specs, outs, 3.7, [pltpu.VMEM((RIM + count, HEAD), F32)], after=after,
    )


def join_cores(mine, other, sp, place, after=()):
    half = mine.shape[1]
    outs = [
        jax.ShapeDtypeStruct((2, half, HEAD, HEAD), BF16),
        jax.ShapeDtypeStruct((half, HEAD, HEAD), BF16),
    ]

    def body(sp_ref, mine_ref, other_ref, both_ref, write_ref):
        first = sp_ref[place] == 0
        for i in range(half):
            held = [(mine_ref[k, i].astype(F32), other_ref[k, i].astype(F32)) for k in (0, 1)]
            early = [jnp.where(first, pair[0], pair[1]) for pair in held]
            late = [jnp.where(first, pair[1], pair[0]) for pair in held]
            left = late[0].astype(BF16)
            write = plain(left, early[1].astype(BF16)) + late[1]
            both_ref[0, i] = plain(left, early[0].astype(BF16)).astype(BF16)
            both_ref[1, i] = write.astype(BF16)
            write_ref[i] = write.astype(BF16)

    inputs = [mine, other]
    return call(body, sp, inputs, [whole(a) for a in inputs], outs, 0.05, after=after)


def pass_chip(joined, states, sp, after=()):
    half = states[0].shape[0]
    outs = [jax.ShapeDtypeStruct((half, HEAD, HEAD), BF16)] * 2
    inputs = [joined, *states]

    def body(sp_ref, joined_ref, *refs):
        for i in range(half):
            state = sum(ref[i].astype(F32) for ref in refs[:-2]).astype(BF16)
            stepped = plain(joined_ref[0, i], state)
            refs[-2][i] = (stepped + joined_ref[1, i].astype(F32)).astype(BF16)
            refs[-1][i] = state

    return call(body, sp, inputs, [whole(a) for a in inputs], outs, 0.05, after=after)


def shifted(value, steps):
    count = lax.axis_size("ctx")
    return lax.ppermute(value, "ctx", [(i, i + steps) for i in range(count - steps)])


def swapped(value):
    count = lax.axis_size("ctx")
    return lax.ppermute(value, "ctx", [(i, i ^ 1) for i in range(count)])


def enter_far(joined):
    chips = lax.axis_size("ctx") // 2
    joined = shifted(joined, 2)
    step = 1
    while step < chips:
        early = shifted(joined, 2 * step).astype(F32)
        late = joined.astype(F32)
        both = jnp.einsum("hij,xhjk->xhik", late[0], early, precision=lax.Precision.HIGHEST)
        joined = (both + late * jnp.array([0.0, 1.0], F32)[:, None, None, None]).astype(BF16)
        step *= 2
    return joined[1]


def finish(inner, query, mine, others, early, gain, sp, place):
    inputs = [inner, query, *early, gain, *mine, *others]
    number, count = inner.shape[:2]
    half = number // 2
    out = jax.ShapeDtypeStruct((count, number * HEAD), BF16)

    def body(sp_ref, inner_ref, query_ref, low_ref, high_ref, gain_ref, *refs):
        core = sp_ref[place]
        keep = sp_ref[1].astype(F32)
        for j in range(number):
            i, early_ref = j % half, (low_ref, high_ref)[j // half]
            own, far = [
                sum(ref[i].astype(F32) for ref in part)
                for part in (refs[: len(mine)], refs[len(mine) : 2 * len(mine)])
            ]
            state = jnp.where((core == 0) == (j < half), own, far)
            stepped = plain(early_ref[0, i], state.astype(BF16)) + early_ref[1, i].astype(F32)
            state = keep * jnp.where(core == 0, state, stepped)
            read = inner_ref[j] + plain(query_ref[j], state.astype(BF16))
            scale = lax.rsqrt(jnp.mean(read * read, axis=-1, keepdims=True) + EPS)
            cols = slice(j * HEAD, (j + 1) * HEAD)
            refs[-1][:, cols] = (read * scale * gain_ref[...]).astype(BF16)

    return call(body, sp, inputs, [whole(a) for a in inputs], [out], 2.7)[0]


def per_device(
    hidden,
    w_query,
    w_key,
    payload_projection_matrix,
    conv_weight,
    log_decay,
    beta_rate,
    norm_gain,
    head_order,
    block_starts,
):
    count = hidden.shape[0]
    ranks = lax.axis_size("head")
    chips = lax.axis_size("ctx") // 2
    total_heads = head_order.shape[0]
    key_heads = total_heads // ranks
    number = 2 * key_heads
    serve, spot = lax.axis_index("head"), lax.axis_index("ctx")
    keep = 1 - block_starts[0]
    place = 2 + total_heads
    w_value = payload_projection_matrix

    rows = w_key.shape[0]
    edge = lax.dynamic_slice(hidden, (count - RIM, serve * rows), (RIM, rows))
    rim = shifted(edge, 1) * keep.astype(BF16)
    hidden = lax.dynamic_slice(hidden, (0, serve * rows), (count, rows))
    sp = jnp.concatenate(
        [jnp.stack([serve, keep]), head_order, jnp.stack([spot % 2])]
    ).astype(jnp.int32)

    everyone = list(range(key_heads))
    halving = Halving(ranks, everyone)

    def gathered(width, weight, base, parts):
        return gather_specs(key_heads, width, hidden, rim, weight, conv_weight, base, parts)

    got_k = [[] for _ in halving.routes]
    part_k = halving.send(0, key_heads, HEAD, hidden, rim, w_key, got_k, sp)
    halving.exchange(0, part_k, got_k)
    tables = list(prepare(log_decay, beta_rate, sp, after=part_k[:1]))
    got_v = [[] for _ in halving.routes]
    part_v = halving.send(
        0, key_heads, 2 * HEAD, hidden, rim, w_value, got_v, sp, after=tables[:1]
    )
    halving.exchange(0, part_v, got_v)
    part_q = partial_sums(
        key_heads, ranks, everyone, HEAD, hidden, rim, w_query, sp, after=part_v[:1]
    )
    for stage in range(1, halving.stages):
        part_k = halving.send(
            stage, key_heads, HEAD, hidden, rim, w_key, got_k, sp, after=part_q[:1]
        )
        halving.exchange(stage, part_k, got_k)
    keys, solve, gathers, trans_a = key_phase(
        gathered(HEAD, w_key, total_heads, [halving.parts(h, HEAD, got_k) for h in everyone]),
        number, count, tables, sp, after=part_k[:1],
    )
    ordered = [trans_a]
    for stage in range(1, halving.stages):
        part_v = halving.send(
            stage, key_heads, 2 * HEAD, hidden, rim, w_value, got_v, sp, after=ordered
        )
        halving.exchange(stage, part_v, got_v)
        ordered = part_v[:1]
    part_q, _ = lax.optimization_barrier((part_q, ordered[0]))
    got_q = exchange(part_q)
    right, own, given = value_phase(
        gathered(
            2 * HEAD, w_value, total_heads,
            [halving.parts(h, 2 * HEAD, got_v) for h in everyone],
        ),
        number, count, tables, gathers, trans_a, sp, place, after=ordered,
    )
    taken = swapped(given)
    joined, joined_b = join_cores(own, taken, sp, place)
    states, last, writes = [], joined_b, None
    if chips <= 4:
        for chip in range(chips - 1):
            if chip:
                after = [] if writes is None else [writes]
                last, so_far = pass_chip(joined, states, sp, after)
                states = [so_far]
            hop = [(2 * chip + c, 2 * chip + 2 + c) for c in range(2)]
            states.append(lax.ppermute(last, "ctx", hop))
            if writes is None and chip + 1 >= min(2, chips - 1):
                writes = write_phase(right, keys, tables, solve, sp, after=[last])
    else:
        states = [enter_far(joined)]
    if writes is None:
        writes = write_phase(right, keys, tables, solve, sp, after=[last])
    inner, query = query_phase(
        gathered(HEAD, w_query, 0, [direct_parts(h, HEAD, got_q) for h in everyone]),
        number, count, tables, keys, writes, sp, after=[last],
    )
    own, _ = lax.optimization_barrier((own, writes))
    early = swapped(own)
    others = [swapped(state) for state in states[:-1]]
    final, _ = lax.optimization_barrier((states[-1], inner))
    return finish(
        inner, query, [*states[:-1], final], [*others, swapped(final)], (early, taken),
        norm_gain[None, :], sp, place,
    )


def solution(mesh):
    return jax.shard_map(
        per_device,
        mesh=mesh,
        in_specs=(
            P("ctx", None),
            P("head", None),
            P("head", None),
            P("head", None),
            P(),
            P("head", "ctx"),
            P("head", "ctx"),
            P(),
            P(),
            P("ctx"),
        ),
        out_specs=P("ctx", "head"),
        check_vma=False,
    )
```

```python
import functools

import jax
import jax.numpy as jnp
from jax import lax
from jax.experimental import pallas as pl
from jax.experimental.pallas import tpu as pltpu
from jax.sharding import PartitionSpec as P

HEAD = 128
TAPS = 4
RIM = 16
EPS = 1e-06
VMEM_BYTES = 20 * 1024 * 1024
F32 = jnp.float32
BF16 = jnp.bfloat16

NN = (((1,), (0,)), ((), ()))
NT = (((1,), (1,)), ((), ()))


def dot1(a, b, dims=NN):
    return lax.dot_general(
        a.astype(BF16), b.astype(BF16), dims, preferred_element_type=F32
    )


def split(a):
    high = a.astype(BF16)
    return high, (a - high.astype(F32)).astype(BF16)


def dot3s(a, b, dims=NN):
    (ah, al), (bh, bl) = a, b
    one = functools.partial(lax.dot_general, dimension_numbers=dims, preferred_element_type=F32)
    return one(ah, bh) + (one(ah, bl) + one(al, bh))


def dot3(a, b, dims=NN):
    return dot3s(split(a), split(b), dims)


def packed_left(parts):
    return jnp.concatenate(parts, axis=1)


def packed_right(parts):
    wide = jnp.concatenate(parts, axis=1)
    return jnp.concatenate([wide, wide], axis=0)


def packed_turned(parts):
    tall = jnp.concatenate(parts, axis=0)
    return jnp.concatenate([tall, tall], axis=1)


def fold(left, right, dims=NN):
    both = lax.dot_general(left, right, dims, preferred_element_type=F32)
    width = both.shape[1] // 2
    return both[:, :width] + both[:, width:]


def mul(a, b):
    return fold(packed_left(split(a)), packed_right(split(b)))


def dot_full(a, b, dims=NN):
    return lax.dot_general(
        a, b, dims, precision=lax.Precision.HIGHEST, preferred_element_type=F32
    )


def whole(array):
    zeros = (0,) * array.ndim
    return pl.BlockSpec(array.shape, lambda i, sp: zeros)


def call(
    body, sp, inputs, specs, outs, micros, scratch=(), after=()
):
    number = len(inputs)
    specs = list(specs) + [pl.BlockSpec(memory_space=pl.ANY) for _ in after]

    def inner(sp_ref, *refs):
        body(sp_ref, *refs[:number], *refs[number + len(after) :])

    return pl.pallas_call(
        inner,
        grid_spec=pltpu.PrefetchScalarGridSpec(
            num_scalar_prefetch=1,
            grid=(1,),
            in_specs=specs,
            out_specs=[whole(out) for out in outs],
            scratch_shapes=list(scratch),
        ),
        out_shape=[jax.ShapeDtypeStruct(out.shape, out.dtype) for out in outs],
        compiler_params=pltpu.CompilerParams(vmem_limit_bytes=VMEM_BYTES),
        cost_estimate=pl.CostEstimate(
            flops=int(micros * 10**9), bytes_accessed=1000, transcendentals=0
        ),
    )(sp, *inputs, *after)


def weight_spec(key_heads, rows, width, unit, head):
    return pl.BlockSpec(
        (rows, width), lambda i, sp: (0, sp[2 + (sp[0] ^ unit) * key_heads + head])
    )


def tap_spec(key_heads, width, base, head):
    return pl.BlockSpec(
        (TAPS, width), lambda i, sp: (0, base + sp[2 + sp[0] * key_heads + head])
    )


def hidden_spec(hidden, rows):
    return whole(hidden)


def partial_sums(key_heads, ranks, heads, width, hidden, rim, weight, sp, after=()):
    rows, count = weight.shape[0], hidden.shape[0]
    inputs, specs = [hidden, rim], [hidden_spec(hidden, rows), hidden_spec(rim, rows)]
    for unit in range(1, ranks):
        for head in heads:
            inputs.append(weight)
            specs.append(weight_spec(key_heads, rows, width, unit, head))
    outs = [jax.ShapeDtypeStruct((RIM + count, width * len(heads)), BF16)] * (ranks - 1)
    step = 2 if width == HEAD and len(heads) % 2 == 0 else 1

    def body(sp_ref, hidden_ref, rim_ref, *refs):
        for unit in range(ranks - 1):
            out = refs[(ranks - 1) * len(heads) + unit]
            for at in range(0, len(heads), step):
                place = unit * len(heads) + at
                held = [refs[place + i][...] for i in range(step)]
                held = held[0] if step == 1 else jnp.concatenate(held, axis=1)
                cols = slice(at * width, (at + step) * width)
                out[RIM:, cols] = plain(hidden_ref[...], held).astype(BF16)
                out[:RIM, cols] = plain(rim_ref[...], held).astype(BF16)

    return call(body, sp, inputs, specs, outs, 1.3, after=after)


def exchange(parts):
    ranks = len(parts) + 1
    return [
        lax.ppermute(part, "head", [(i, i ^ (unit + 1)) for i in range(ranks)])
        for unit, part in enumerate(parts)
    ]


class Halving:
    def __init__(self, ranks, heads):
        bits = [1 << i for i in range(ranks.bit_length() - 1)]
        cut = (len(heads) + 1) // 2
        self.ranks, self.stages = ranks, len(bits)
        self.routes = [
            (order, part) for order, part in ((bits, heads[:cut]), (bits[::-1], heads[cut:])) if part
        ]

    def offsets(self, route, stage):
        out = [0]
        for bit in self.routes[route][0][stage + 1 :]:
            out = out + [o ^ bit for o in out]
        return out

    def send(self, stage, key_heads, width, hidden, rim, weight, received, sp, after=()):
        rows, count = weight.shape[0], hidden.shape[0]
        inputs, specs = [hidden, rim], [hidden_spec(hidden, rows), hidden_spec(rim, rows)]
        jobs, outs = [], []
        for route, (order, heads) in enumerate(self.routes):
            first = len(inputs)
            inputs += received[route]
            specs += [whole(part) for part in received[route]]
            offsets = self.offsets(route, stage)
            for slot, offset in enumerate(offsets):
                unit = offset ^ order[stage]
                sources = [
                    (first + before, self.offsets(route, before).index(unit))
                    for before in range(stage)
                ]
                for at, head in enumerate(heads):
                    jobs.append((len(inputs), sources, route, slot, at))
                    inputs.append(weight)
                    specs.append(weight_spec(key_heads, rows, width, unit, head))
            shape = (len(offsets), RIM + count, width * len(heads))
            outs.append(jax.ShapeDtypeStruct(shape, BF16))
        total = len(inputs)

        def body(sp_ref, *refs):
            for place, sources, route, slot, at in jobs:
                held = refs[place][...]
                cols = slice(at * width, (at + 1) * width)
                for left, span in ((refs[0], slice(RIM, RIM + count)), (refs[1], slice(0, RIM))):
                    part = plain(left[...], held)
                    for source, index in sources:
                        part = part + refs[source][index, span, cols].astype(F32)
                    refs[total + route][slot, span, cols] = part.astype(BF16)

        return call(body, sp, inputs, specs, outs, 1.3, after=after)

    def exchange(self, stage, sent, received):
        for route, part in enumerate(sent):
            bit = self.routes[route][0][stage]
            pairs = [(i, i ^ bit) for i in range(self.ranks)]
            received[route].append(lax.ppermute(part, "head", pairs))

    def parts(self, head, width, received):
        route = [head in heads for _, heads in self.routes].index(True)
        at = self.routes[route][1].index(head)
        return [
            (part, pl.BlockSpec((None, part.shape[1], width), lambda i, sp: (0, 0, at)))
            for part in received[route]
        ]


def direct_parts(head, width, received):
    return [
        (part, pl.BlockSpec((part.shape[0], width), lambda i, sp: (0, head))) for part in received
    ]


def gather_specs(key_heads, width, hidden, rim, weight, taps, base, parts):
    rows = weight.shape[0]
    inputs = [hidden, rim]
    specs = [hidden_spec(hidden, rows), hidden_spec(rim, rows)]
    jobs = []
    for head, received in enumerate(parts):
        jobs.append(len(inputs))
        inputs += [weight, taps]
        specs += [
            weight_spec(key_heads, rows, width, 0, head), tap_spec(key_heads, width, base, head)
        ]
        for part, spec in received:
            inputs.append(part)
            specs.append(spec)
    return inputs, specs, jobs


def activate(refs, job, number, scratch):
    held, taps = refs[job][...], refs[job + 1][...].astype(F32)
    count = refs[0].shape[0]
    for left, span in ((refs[0], slice(RIM, RIM + count)), (refs[1], slice(0, RIM))):
        part = plain(left[...], held)
        for source in range(job + 2, job + 2 + number):
            part = part + refs[source][span, :].astype(F32)
        scratch[span, :] = part
    total = None
    for tap in range(TAPS):
        first = RIM - (TAPS - 1) + tap
        term = taps[tap : tap + 1] * scratch[first : first + count, :]
        total = term if total is None else total + term
    return total / (1.0 + jnp.exp(-total))


def plain(a, b):
    return jnp.dot(a, b, preferred_element_type=F32)


def unit_rows(values):
    return values * lax.rsqrt(jnp.sum(values * values, axis=-1, keepdims=True) + EPS)


def iotas(size):
    return (
        lax.broadcasted_iota(jnp.int32, (size, size), 0),
        lax.broadcasted_iota(jnp.int32, (size, size), 1),
    )


def prepare(decay, beta, sp, after=()):
    heads, count = decay.shape
    outs = [
        jax.ShapeDtypeStruct((heads, count), F32),
        jax.ShapeDtypeStruct((count, heads), F32),
        jax.ShapeDtypeStruct((count, heads), F32),
    ]

    def body(sp_ref, decay_ref, beta_ref, row_ref, col_ref, rate_ref):
        rows, cols = iotas(count)
        row_ref[...] = dot_full(decay_ref[...], (rows <= cols).astype(F32))
        col_ref[...] = dot_full((cols <= rows).astype(F32), decay_ref[...], NT)
        rate_ref[...] = dot_full((rows == cols).astype(F32), beta_ref[...], NT)

    return call(body, sp, [decay, beta], [whole(decay), whole(beta)], outs, 1.2, after=after)


def inverses(systems):
    size = systems[0].shape[0]
    rows, cols = iotas(size)
    eye = (rows == cols).astype(F32)
    cut = [split(low) for low in systems]
    mask = ((rows >> 2) == (cols >> 2)).astype(F32).astype(BF16)
    near = [c[0] * mask for c in cut]
    square = [plain(n, n) for n in near]
    cube = [plain(n, s.astype(BF16)) for n, s in zip(near, square)]
    inv = [
        (eye - n.astype(F32) + s - c).astype(BF16) for n, s, c in zip(near, square, cube)
    ]
    shift = 2
    while (1 << shift) < size:
        inside = ((rows >> (shift + 1)) == (cols >> (shift + 1))) & (
            (rows >> shift) != (cols >> shift)
        )
        mask = inside.astype(F32).astype(BF16)
        middle = [plain(c[0] * mask, x).astype(BF16) for c, x in zip(cut, inv)]
        inv = [x - plain(x, m).astype(BF16) for x, m in zip(inv, middle)]
        shift += 1
    rest = [
        eye - x.astype(F32) - plain(packed_left(c), jnp.concatenate([x, x], axis=0))
        for c, x in zip(cut, inv)
    ]
    return [x.astype(F32) + plain(x, r.astype(BF16)) for x, r in zip(inv, rest)]


def key_phase(gathered, number, count, tables, sp, after=()):
    inputs, specs, jobs = gathered
    received = (len(inputs) - 2) // len(jobs) - 2
    at = len(inputs)
    inputs = inputs + tables
    specs = specs + [whole(table) for table in tables]
    half = count // 2
    heads = range(number // 2)
    outs = [
        jax.ShapeDtypeStruct((len(heads), count, HEAD), F32),
        jax.ShapeDtypeStruct((number, 3, half, 2 * half), BF16),
        jax.ShapeDtypeStruct((number, 2, HEAD, 2 * half), BF16),
        jax.ShapeDtypeStruct((number, HEAD, HEAD), F32),
    ]
    total = len(inputs)

    def body(sp_ref, *refs):
        key_ref, solve_ref, gather_ref, trans_ref, scratch = refs[total:]
        sums, sums_col, beta_col = (ref[...] for ref in refs[at : at + 3])
        rows, cols = iotas(half)
        keys, turned, systems, crosses = [], [], [], []
        for i, job in enumerate(jobs):
            key = unit_rows(activate(refs, job, received, scratch))
            keys.append(key)
            key_ref[i] = key
            turned.append(key.T)
            low, high = split(key[:half]), split(key[half:])
            low_left, high_left = packed_left(low), packed_left(high)
            low_right, high_right = packed_turned(low), packed_turned(high)
            alike = (
                fold(low_left, low_right, NT),
                fold(high_left, high_right, NT),
                fold(high_left, low_right, NT),
            )
            for r in (2 * i, 2 * i + 1):
                row, col, rate = sums[r : r + 1], sums_col[:, r : r + 1], beta_col[:, r : r + 1]
                for b, span in enumerate((slice(0, half), slice(half, count))):
                    fade = jnp.exp(jnp.minimum(col[span] - row[:, span], 0.0))
                    systems.append(jnp.where(cols < rows, rate[span] * fade * alike[b], 0.0))
                fade = jnp.exp(jnp.minimum(col[half:] - row[:, :half], 0.0))
                crosses.append(rate[half:] * fade * alike[2])
        solved = inverses(systems)
        left = [packed_left(split(x)) for x in solved]
        middle = [
            mul(cross, solved[2 * j]) for j, cross in enumerate(crosses)
        ]
        corner = [
            -fold(left[2 * j + 1], packed_right(split(m))) for j, m in enumerate(middle)
        ]
        keep = sp_ref[1].astype(F32)
        eye = (lax.broadcasted_iota(jnp.int32, (HEAD, HEAD), 0)
               == lax.broadcasted_iota(jnp.int32, (HEAD, HEAD), 1)).astype(F32)
        for j in range(number):
            key = keys[j // 2]
            row, col, rate = sums[j : j + 1], sums_col[:, j : j + 1], beta_col[:, j : j + 1]
            side = split(corner[j])
            for which, part in enumerate((left[2 * j], left[2 * j + 1], packed_left(side))):
                solve_ref[j, which] = part
            trailing = turned[j // 2] * jnp.exp(row[:, count - 1 :] - row)
            low, high = [packed_left(split(t)) for t in (trailing[:, :half], trailing[:, half:])]
            taken = (
                fold(low, packed_right(split(solved[2 * j]))) + fold(high, packed_right(side)),
                fold(high, packed_right(split(solved[2 * j + 1]))),
            )
            right = (rate * jnp.exp(col)) * key
            moved = None
            for part, span in zip(taken, (slice(0, half), slice(half, count))):
                part = packed_left(split(part))
                gather_ref[j, 0 if span.start == 0 else 1] = part
                term = fold(part, packed_right(split(right[span])))
                moved = term if moved is None else moved + term
            gone = jnp.exp(row[:, count - 1 :])
            trans_ref[j] = keep * (gone * eye - moved)

    return call(
        body, sp, inputs, specs, outs, 5.0, [pltpu.VMEM((RIM + count, HEAD), F32)], after=after,
    )


def value_phase(gathered, number, count, tables, gathers, trans, sp, place, after=()):
    inputs, specs, jobs = gathered
    received = (len(inputs) - 2) // len(jobs) - 2
    at = len(inputs)
    inputs = inputs + tables + [gathers, trans]
    specs = specs + [whole(a) for a in inputs[at:]]
    half = count // 2
    outs = [
        jax.ShapeDtypeStruct((number, count, HEAD), F32),
        jax.ShapeDtypeStruct((2, number // 2, HEAD, HEAD), BF16),
        jax.ShapeDtypeStruct((2, number // 2, HEAD, HEAD), BF16),
    ]
    total = len(inputs)

    def body(sp_ref, *refs):
        write_ref, keep_ref, give_ref, scratch = refs[total:]
        beta_col = refs[at + 2][...]
        gather_ref, moved_ref = refs[at + 3 : at + 5]
        made = []
        for i, job in enumerate(jobs):
            values = activate(refs, job, received, scratch)
            for j in (2 * i, 2 * i + 1):
                right = beta_col[:, j : j + 1] * values[:, (j % 2) * HEAD : (j % 2 + 1) * HEAD]
                write_ref[j] = right
                low, high = [right[span].astype(BF16) for span in (slice(0, half), slice(half, count))]
                made.append(
                    plain(gather_ref[j, 0], jnp.concatenate([low, low], axis=0))
                    + plain(gather_ref[j, 1], jnp.concatenate([high, high], axis=0))
                )
        first = sp_ref[place] == 0
        for i in range(number // 2):
            k = i + number // 2
            for ref, mine in ((keep_ref, first), (give_ref, jnp.logical_not(first))):
                ref[0, i] = jnp.where(mine, moved_ref[i], moved_ref[k]).astype(BF16)
                ref[1, i] = jnp.where(mine, made[i], made[k]).astype(BF16)

    return call(
        body, sp, inputs, specs, outs, 0.05, [pltpu.VMEM((RIM + count, 2 * HEAD), F32)], after=after,
    )


def write_phase(right, keys, tables, solve, sp, after=()):
    number, count = right.shape[:2]
    half = count // 2
    inputs = [right, keys, *tables, solve]
    out = jax.ShapeDtypeStruct((number, count, 2 * HEAD), F32)

    def body(sp_ref, right_ref, key_ref, _, col_ref, rate_ref, solve_ref, out_ref):
        for j in range(number):
            col, rate = col_ref[:, j : j + 1], rate_ref[:, j : j + 1]
            both = jnp.concatenate([right_ref[j], (rate * jnp.exp(col)) * key_ref[j // 2]], axis=1)
            parts = []
            for span in (slice(0, half), slice(half, count)):
                high, low = split(both[span])
                parts.append((jnp.concatenate([high, high], axis=0), low))

            def solved(which, part):
                left = solve_ref[j, which]
                return plain(left, part[0]) + plain(left[:, :half], part[1])

            out_ref[j, :half] = solved(0, parts[0])
            out_ref[j, half:] = solved(2, parts[0]) + solved(1, parts[1])

    return call(body, sp, inputs, [whole(a) for a in inputs], [out], 0.05, after=after)[0]


def query_phase(gathered, number, count, tables, keys, writes, sp, after=()):
    inputs, specs, jobs = gathered
    received = (len(inputs) - 2) // len(jobs) - 2
    at = len(inputs)
    inputs = inputs + tables + [keys, writes]
    specs = specs + [whole(a) for a in inputs[at:]]
    half = count // 2
    outs = [
        jax.ShapeDtypeStruct((number, count, HEAD), F32),
        jax.ShapeDtypeStruct((number, count, HEAD), BF16),
    ]
    total = len(inputs)

    def body(sp_ref, *refs):
        inner_ref, query_ref, scratch = refs[total:]
        sums, sums_col = refs[at][...], refs[at + 1][...]
        rows, cols = iotas(half)
        low, high = slice(0, half), slice(half, count)
        for i, job in enumerate(jobs):
            key_ref, write_ref = refs[at + 3 : at + 5]
            query = unit_rows(activate(refs, job, received, scratch))
            key = key_ref[i]
            left = [packed_left(split(query[span])) for span in (low, high)]
            right = [packed_turned(split(key[span])) for span in (low, high)]
            alike = {
                (0, 0): fold(left[0], right[0], NT),
                (1, 1): fold(left[1], right[1], NT),
                (1, 0): fold(left[1], right[0], NT),
            }
            for j in (2 * i, 2 * i + 1):
                row, col = sums[j : j + 1], sums_col[:, j : j + 1]
                wrote = [split(write_ref[j, span]) for span in (low, high)]
                tall = [jnp.concatenate([w[0], w[0]], axis=0) for w in wrote]
                read = [None, None]
                for (t, s), product in alike.items():
                    fade = jnp.exp(
                        jnp.minimum(col[(low, high)[t]] - row[:, (low, high)[s]], 0.0)
                    )
                    attend = fade * product
                    if t == s:
                        attend = jnp.where(cols <= rows, attend, 0.0)
                    attend = split(attend)
                    part = jnp.dot(
                        packed_left(attend), tall[s], preferred_element_type=F32
                    ) + jnp.dot(attend[0], wrote[s][1], preferred_element_type=F32)
                    read[t] = part if read[t] is None else read[t] + part
                for t, span in enumerate((low, high)):
                    inner_ref[j, span] = read[t][:, :HEAD]
                    read_in = jnp.exp(col[span]) * query[span] - read[t][:, HEAD:]
                    query_ref[j, span] = read_in.astype(BF16)

    return call(
        body, sp, inputs, specs, outs, 3.7, [pltpu.VMEM((RIM + count, HEAD), F32)], after=after,
    )


def join_cores(mine, other, sp, place, after=()):
    half = mine.shape[1]
    outs = [
        jax.ShapeDtypeStruct((2, half, HEAD, HEAD), BF16),
        jax.ShapeDtypeStruct((half, HEAD, HEAD), BF16),
    ]

    def body(sp_ref, mine_ref, other_ref, both_ref, write_ref):
        first = sp_ref[place] == 0
        for i in range(half):
            held = [(mine_ref[k, i].astype(F32), other_ref[k, i].astype(F32)) for k in (0, 1)]
            early = [jnp.where(first, pair[0], pair[1]) for pair in held]
            late = [jnp.where(first, pair[1], pair[0]) for pair in held]
            left = late[0].astype(BF16)
            write = plain(left, early[1].astype(BF16)) + late[1]
            both_ref[0, i] = plain(left, early[0].astype(BF16)).astype(BF16)
            both_ref[1, i] = write.astype(BF16)
            write_ref[i] = write.astype(BF16)

    inputs = [mine, other]
    return call(body, sp, inputs, [whole(a) for a in inputs], outs, 0.05, after=after)


def pass_chip(joined, states, sp, after=()):
    half = states[0].shape[0]
    outs = [jax.ShapeDtypeStruct((half, HEAD, HEAD), BF16)] * 2
    inputs = [joined, *states]

    def body(sp_ref, joined_ref, *refs):
        for i in range(half):
            state = sum(ref[i].astype(F32) for ref in refs[:-2]).astype(BF16)
            stepped = plain(joined_ref[0, i], state)
            refs[-2][i] = (stepped + joined_ref[1, i].astype(F32)).astype(BF16)
            refs[-1][i] = state

    return call(body, sp, inputs, [whole(a) for a in inputs], outs, 0.05, after=after)


def shifted(value, steps):
    count = lax.axis_size("ctx")
    return lax.ppermute(value, "ctx", [(i, i + steps) for i in range(count - steps)])


def swapped(value):
    count = lax.axis_size("ctx")
    return lax.ppermute(value, "ctx", [(i, i ^ 1) for i in range(count)])


def enter_far(joined):
    chips = lax.axis_size("ctx") // 2
    joined = shifted(joined, 2)
    step = 1
    while step < chips:
        early = shifted(joined, 2 * step).astype(F32)
        late = joined.astype(F32)
        both = jnp.einsum("hij,xhjk->xhik", late[0], early, precision=lax.Precision.HIGHEST)
        joined = (both + late * jnp.array([0.0, 1.0], F32)[:, None, None, None]).astype(BF16)
        step *= 2
    return joined[1]


def finish(inner, query, mine, others, early, gain, sp, place):
    inputs = [inner, query, *early, gain, *mine, *others]
    number, count = inner.shape[:2]
    half = number // 2
    out = jax.ShapeDtypeStruct((count, number * HEAD), BF16)

    def body(sp_ref, inner_ref, query_ref, low_ref, high_ref, gain_ref, *refs):
        core = sp_ref[place]
        keep = sp_ref[1].astype(F32)
        for j in range(number):
            i, early_ref = j % half, (low_ref, high_ref)[j // half]
            own, far = [
                sum(ref[i].astype(F32) for ref in part)
                for part in (refs[: len(mine)], refs[len(mine) : 2 * len(mine)])
            ]
            state = jnp.where((core == 0) == (j < half), own, far)
            stepped = plain(early_ref[0, i], state.astype(BF16)) + early_ref[1, i].astype(F32)
            state = keep * jnp.where(core == 0, state, stepped)
            read = inner_ref[j] + plain(query_ref[j], state.astype(BF16))
            scale = lax.rsqrt(jnp.mean(read * read, axis=-1, keepdims=True) + EPS)
            cols = slice(j * HEAD, (j + 1) * HEAD)
            refs[-1][:, cols] = (read * scale * gain_ref[...]).astype(BF16)

    return call(body, sp, inputs, [whole(a) for a in inputs], [out], 2.7)[0]


def per_device(
    hidden,
    w_query,
    w_key,
    payload_projection_matrix,
    conv_weight,
    log_decay,
    beta_rate,
    norm_gain,
    head_order,
    block_starts,
):
    count = hidden.shape[0]
    ranks = lax.axis_size("head")
    chips = lax.axis_size("ctx") // 2
    total_heads = head_order.shape[0]
    key_heads = total_heads // ranks
    number = 2 * key_heads
    serve, spot = lax.axis_index("head"), lax.axis_index("ctx")
    keep = 1 - block_starts[0]
    place = 2 + total_heads
    w_value = payload_projection_matrix

    rows = w_key.shape[0]
    edge = lax.dynamic_slice(hidden, (count - RIM, serve * rows), (RIM, rows))
    rim = shifted(edge, 1) * keep.astype(BF16)
    hidden = lax.dynamic_slice(hidden, (0, serve * rows), (count, rows))
    sp = jnp.concatenate(
        [jnp.stack([serve, keep]), head_order, jnp.stack([spot % 2])]
    ).astype(jnp.int32)

    everyone = list(range(key_heads))
    halving = Halving(ranks, everyone)

    def gathered(width, weight, base, parts):
        return gather_specs(key_heads, width, hidden, rim, weight, conv_weight, base, parts)

    got_k = [[] for _ in halving.routes]
    part_k = halving.send(0, key_heads, HEAD, hidden, rim, w_key, got_k, sp)
    halving.exchange(0, part_k, got_k)
    tables = list(prepare(log_decay, beta_rate, sp, after=part_k[:1]))
    got_v = [[] for _ in halving.routes]
    part_v = halving.send(
        0, key_heads, 2 * HEAD, hidden, rim, w_value, got_v, sp, after=tables[:1]
    )
    halving.exchange(0, part_v, got_v)
    part_q = partial_sums(
        key_heads, ranks, everyone, HEAD, hidden, rim, w_query, sp, after=part_v[:1]
    )
    for stage in range(1, halving.stages):
        part_k = halving.send(
            stage, key_heads, HEAD, hidden, rim, w_key, got_k, sp, after=part_q[:1]
        )
        halving.exchange(stage, part_k, got_k)
    keys, solve, gathers, trans_a = key_phase(
        gathered(HEAD, w_key, total_heads, [halving.parts(h, HEAD, got_k) for h in everyone]),
        number, count, tables, sp, after=part_k[:1],
    )
    ordered = [trans_a]
    for stage in range(1, halving.stages):
        part_v = halving.send(
            stage, key_heads, 2 * HEAD, hidden, rim, w_value, got_v, sp, after=ordered
        )
        halving.exchange(stage, part_v, got_v)
        ordered = part_v[:1]
    part_q, _ = lax.optimization_barrier((part_q, ordered[0]))
    got_q = exchange(part_q)
    right, own, given = value_phase(
        gathered(
            2 * HEAD, w_value, total_heads,
            [halving.parts(h, 2 * HEAD, got_v) for h in everyone],
        ),
        number, count, tables, gathers, trans_a, sp, place, after=ordered,
    )
    taken = swapped(given)
    joined, joined_b = join_cores(own, taken, sp, place)
    states, last, writes = [], joined_b, None
    if chips <= 4:
        for chip in range(chips - 1):
            if chip:
                after = [] if writes is None else [writes]
                last, so_far = pass_chip(joined, states, sp, after)
                states = [so_far]
            hop = [(2 * chip + c, 2 * chip + 2 + c) for c in range(2)]
            states.append(lax.ppermute(last, "ctx", hop))
            if writes is None and chip + 1 >= min(2, chips - 1):
                writes = write_phase(right, keys, tables, solve, sp, after=[last])
    else:
        states = [enter_far(joined)]
    if writes is None:
        writes = write_phase(right, keys, tables, solve, sp, after=[last])
    inner, query = query_phase(
        gathered(HEAD, w_query, 0, [direct_parts(h, HEAD, got_q) for h in everyone]),
        number, count, tables, keys, writes, sp, after=[last],
    )
    own, _ = lax.optimization_barrier((own, joined))
    early = swapped(own)
    others = [swapped(state) for state in states[:-1]]
    final, _ = lax.optimization_barrier((states[-1], inner))
    return finish(
        inner, query, [*states[:-1], final], [*others, swapped(final)], (early, taken),
        norm_gain[None, :], sp, place,
    )


def solution(mesh):
    return jax.shard_map(
        per_device,
        mesh=mesh,
        in_specs=(
            P("ctx", None),
            P("head", None),
            P("head", None),
            P("head", None),
            P(),
            P("head", "ctx"),
            P("head", "ctx"),
            P(),
            P(),
            P("ctx"),
        ),
        out_specs=P("ctx", "head"),
        check_vma=False,
    )
```

```python
import functools

import jax
import jax.numpy as jnp
from jax import lax
from jax.experimental import pallas as pl
from jax.experimental.pallas import tpu as pltpu
from jax.sharding import PartitionSpec as P

HEAD = 128
TAPS = 4
RIM = 16
EPS = 1e-06
VMEM_BYTES = 20 * 1024 * 1024
F32 = jnp.float32
BF16 = jnp.bfloat16

NN = (((1,), (0,)), ((), ()))
NT = (((1,), (1,)), ((), ()))


def dot1(a, b, dims=NN):
    return lax.dot_general(
        a.astype(BF16), b.astype(BF16), dims, preferred_element_type=F32
    )


def split(a):
    high = a.astype(BF16)
    return high, (a - high.astype(F32)).astype(BF16)


def dot3s(a, b, dims=NN):
    (ah, al), (bh, bl) = a, b
    one = functools.partial(lax.dot_general, dimension_numbers=dims, preferred_element_type=F32)
    return one(ah, bh) + (one(ah, bl) + one(al, bh))


def dot3(a, b, dims=NN):
    return dot3s(split(a), split(b), dims)


def packed_left(parts):
    return jnp.concatenate(parts, axis=1)


def packed_right(parts):
    wide = jnp.concatenate(parts, axis=1)
    return jnp.concatenate([wide, wide], axis=0)


def packed_turned(parts):
    tall = jnp.concatenate(parts, axis=0)
    return jnp.concatenate([tall, tall], axis=1)


def fold(left, right, dims=NN):
    both = lax.dot_general(left, right, dims, preferred_element_type=F32)
    width = both.shape[1] // 2
    return both[:, :width] + both[:, width:]


def mul(a, b):
    return fold(packed_left(split(a)), packed_right(split(b)))


def dot_full(a, b, dims=NN):
    return lax.dot_general(
        a, b, dims, precision=lax.Precision.HIGHEST, preferred_element_type=F32
    )


def whole(array):
    zeros = (0,) * array.ndim
    return pl.BlockSpec(array.shape, lambda i, sp: zeros)


def call(
    body, sp, inputs, specs, outs, micros, scratch=(), after=()
):
    number = len(inputs)
    specs = list(specs) + [pl.BlockSpec(memory_space=pl.ANY) for _ in after]

    def inner(sp_ref, *refs):
        body(sp_ref, *refs[:number], *refs[number + len(after) :])

    return pl.pallas_call(
        inner,
        grid_spec=pltpu.PrefetchScalarGridSpec(
            num_scalar_prefetch=1,
            grid=(1,),
            in_specs=specs,
            out_specs=[whole(out) for out in outs],
            scratch_shapes=list(scratch),
        ),
        out_shape=[jax.ShapeDtypeStruct(out.shape, out.dtype) for out in outs],
        compiler_params=pltpu.CompilerParams(vmem_limit_bytes=VMEM_BYTES),
        cost_estimate=pl.CostEstimate(
            flops=int(micros * 10**9), bytes_accessed=1000, transcendentals=0
        ),
    )(sp, *inputs, *after)


def weight_spec(key_heads, rows, width, unit, head):
    return pl.BlockSpec(
        (rows, width), lambda i, sp: (0, sp[2 + (sp[0] ^ unit) * key_heads + head])
    )


def tap_spec(key_heads, width, base, head):
    return pl.BlockSpec(
        (TAPS, width), lambda i, sp: (0, base + sp[2 + sp[0] * key_heads + head])
    )


def hidden_spec(hidden, rows):
    return whole(hidden)


def partial_sums(key_heads, ranks, heads, width, hidden, rim, weight, sp, after=()):
    rows, count = weight.shape[0], hidden.shape[0]
    inputs, specs = [hidden, rim], [hidden_spec(hidden, rows), hidden_spec(rim, rows)]
    for unit in range(1, ranks):
        for head in heads:
            inputs.append(weight)
            specs.append(weight_spec(key_heads, rows, width, unit, head))
    outs = [jax.ShapeDtypeStruct((RIM + count, width * len(heads)), BF16)] * (ranks - 1)
    step = 2 if width == HEAD and len(heads) % 2 == 0 else 1

    def body(sp_ref, hidden_ref, rim_ref, *refs):
        for unit in range(ranks - 1):
            out = refs[(ranks - 1) * len(heads) + unit]
            for at in range(0, len(heads), step):
                place = unit * len(heads) + at
                held = [refs[place + i][...] for i in range(step)]
                held = held[0] if step == 1 else jnp.concatenate(held, axis=1)
                cols = slice(at * width, (at + step) * width)
                out[RIM:, cols] = plain(hidden_ref[...], held).astype(BF16)
                out[:RIM, cols] = plain(rim_ref[...], held).astype(BF16)

    return call(body, sp, inputs, specs, outs, 1.3, after=after)


def exchange(parts):
    ranks = len(parts) + 1
    return [
        lax.ppermute(part, "head", [(i, i ^ (unit + 1)) for i in range(ranks)])
        for unit, part in enumerate(parts)
    ]


class Halving:
    def __init__(self, ranks, heads):
        bits = [1 << i for i in range(ranks.bit_length() - 1)]
        cut = (len(heads) + 1) // 2
        self.ranks, self.stages = ranks, len(bits)
        self.routes = [
            (order, part) for order, part in ((bits, heads[:cut]), (bits[::-1], heads[cut:])) if part
        ]

    def offsets(self, route, stage):
        out = [0]
        for bit in self.routes[route][0][stage + 1 :]:
            out = out + [o ^ bit for o in out]
        return out

    def send(self, stage, key_heads, width, hidden, rim, weight, received, sp, after=()):
        rows, count = weight.shape[0], hidden.shape[0]
        inputs, specs = [hidden, rim], [hidden_spec(hidden, rows), hidden_spec(rim, rows)]
        jobs, outs = [], []
        for route, (order, heads) in enumerate(self.routes):
            first = len(inputs)
            inputs += received[route]
            specs += [whole(part) for part in received[route]]
            offsets = self.offsets(route, stage)
            for slot, offset in enumerate(offsets):
                unit = offset ^ order[stage]
                sources = [
                    (first + before, self.offsets(route, before).index(unit))
                    for before in range(stage)
                ]
                for at, head in enumerate(heads):
                    jobs.append((len(inputs), sources, route, slot, at))
                    inputs.append(weight)
                    specs.append(weight_spec(key_heads, rows, width, unit, head))
            shape = (len(offsets), RIM + count, width * len(heads))
            outs.append(jax.ShapeDtypeStruct(shape, BF16))
        total = len(inputs)

        def body(sp_ref, *refs):
            for place, sources, route, slot, at in jobs:
                held = refs[place][...]
                cols = slice(at * width, (at + 1) * width)
                for left, span in ((refs[0], slice(RIM, RIM + count)), (refs[1], slice(0, RIM))):
                    part = plain(left[...], held)
                    for source, index in sources:
                        part = part + refs[source][index, span, cols].astype(F32)
                    refs[total + route][slot, span, cols] = part.astype(BF16)

        return call(body, sp, inputs, specs, outs, 1.3, after=after)

    def exchange(self, stage, sent, received):
        for route, part in enumerate(sent):
            bit = self.routes[route][0][stage]
            pairs = [(i, i ^ bit) for i in range(self.ranks)]
            received[route].append(lax.ppermute(part, "head", pairs))

    def parts(self, head, width, received):
        route = [head in heads for _, heads in self.routes].index(True)
        at = self.routes[route][1].index(head)
        return [
            (part, pl.BlockSpec((None, part.shape[1], width), lambda i, sp: (0, 0, at)))
            for part in received[route]
        ]


def direct_parts(head, width, received):
    return [
        (part, pl.BlockSpec((part.shape[0], width), lambda i, sp: (0, head))) for part in received
    ]


def gather_specs(key_heads, width, hidden, rim, weight, taps, base, parts):
    rows = weight.shape[0]
    inputs = [hidden, rim]
    specs = [hidden_spec(hidden, rows), hidden_spec(rim, rows)]
    jobs = []
    for head, received in enumerate(parts):
        jobs.append(len(inputs))
        inputs += [weight, taps]
        specs += [
            weight_spec(key_heads, rows, width, 0, head), tap_spec(key_heads, width, base, head)
        ]
        for part, spec in received:
            inputs.append(part)
            specs.append(spec)
    return inputs, specs, jobs


def activate(refs, job, number, scratch):
    held, taps = refs[job][...], refs[job + 1][...].astype(F32)
    count = refs[0].shape[0]
    for left, span in ((refs[0], slice(RIM, RIM + count)), (refs[1], slice(0, RIM))):
        part = plain(left[...], held)
        for source in range(job + 2, job + 2 + number):
            part = part + refs[source][span, :].astype(F32)
        scratch[span, :] = part
    total = None
    for tap in range(TAPS):
        first = RIM - (TAPS - 1) + tap
        term = taps[tap : tap + 1] * scratch[first : first + count, :]
        total = term if total is None else total + term
    return total / (1.0 + jnp.exp(-total))


def plain(a, b):
    return jnp.dot(a, b, preferred_element_type=F32)


def unit_rows(values):
    return values * lax.rsqrt(jnp.sum(values * values, axis=-1, keepdims=True) + EPS)


def iotas(size):
    return (
        lax.broadcasted_iota(jnp.int32, (size, size), 0),
        lax.broadcasted_iota(jnp.int32, (size, size), 1),
    )


def prepare(decay, beta, sp, after=()):
    heads, count = decay.shape
    outs = [
        jax.ShapeDtypeStruct((heads, count), F32),
        jax.ShapeDtypeStruct((count, heads), F32),
        jax.ShapeDtypeStruct((count, heads), F32),
    ]

    def body(sp_ref, decay_ref, beta_ref, row_ref, col_ref, rate_ref):
        rows, cols = iotas(count)
        row_ref[...] = dot_full(decay_ref[...], (rows <= cols).astype(F32))
        col_ref[...] = dot_full((cols <= rows).astype(F32), decay_ref[...], NT)
        rate_ref[...] = dot_full((rows == cols).astype(F32), beta_ref[...], NT)

    return call(body, sp, [decay, beta], [whole(decay), whole(beta)], outs, 1.2, after=after)


def inverses(systems):
    size = systems[0].shape[0]
    rows, cols = iotas(size)
    eye = (rows == cols).astype(F32)
    cut = [split(low) for low in systems]
    mask = ((rows >> 2) == (cols >> 2)).astype(F32).astype(BF16)
    near = [c[0] * mask for c in cut]
    square = [plain(n, n) for n in near]
    cube = [plain(n, s.astype(BF16)) for n, s in zip(near, square)]
    inv = [
        (eye - n.astype(F32) + s - c).astype(BF16) for n, s, c in zip(near, square, cube)
    ]
    shift = 2
    while (1 << shift) < size:
        inside = ((rows >> (shift + 1)) == (cols >> (shift + 1))) & (
            (rows >> shift) != (cols >> shift)
        )
        mask = inside.astype(F32).astype(BF16)
        middle = [plain(c[0] * mask, x).astype(BF16) for c, x in zip(cut, inv)]
        inv = [x - plain(x, m).astype(BF16) for x, m in zip(inv, middle)]
        shift += 1
    rest = [
        eye - x.astype(F32) - plain(packed_left(c), jnp.concatenate([x, x], axis=0))
        for c, x in zip(cut, inv)
    ]
    return [x.astype(F32) + plain(x, r.astype(BF16)) for x, r in zip(inv, rest)]


def key_phase(gathered, number, count, tables, sp, after=()):
    inputs, specs, jobs = gathered
    received = (len(inputs) - 2) // len(jobs) - 2
    at = len(inputs)
    inputs = inputs + tables
    specs = specs + [whole(table) for table in tables]
    half = count // 2
    heads = range(number // 2)
    outs = [
        jax.ShapeDtypeStruct((len(heads), count, HEAD), F32),
        jax.ShapeDtypeStruct((number, 3, half, 2 * half), BF16),
        jax.ShapeDtypeStruct((number, 2, HEAD, 2 * half), BF16),
        jax.ShapeDtypeStruct((number, HEAD, HEAD), F32),
    ]
    total = len(inputs)

    def body(sp_ref, *refs):
        key_ref, solve_ref, gather_ref, trans_ref, scratch = refs[total:]
        sums, sums_col, beta_col = (ref[...] for ref in refs[at : at + 3])
        rows, cols = iotas(half)
        keys, turned, systems, crosses = [], [], [], []
        for i, job in enumerate(jobs):
            key = unit_rows(activate(refs, job, received, scratch))
            keys.append(key)
            key_ref[i] = key
            turned.append(key.T)
            low, high = split(key[:half]), split(key[half:])
            low_left, high_left = packed_left(low), packed_left(high)
            low_right, high_right = packed_turned(low), packed_turned(high)
            alike = (
                fold(low_left, low_right, NT),
                fold(high_left, high_right, NT),
                fold(high_left, low_right, NT),
            )
            for r in (2 * i, 2 * i + 1):
                row, col, rate = sums[r : r + 1], sums_col[:, r : r + 1], beta_col[:, r : r + 1]
                for b, span in enumerate((slice(0, half), slice(half, count))):
                    fade = jnp.exp(jnp.minimum(col[span] - row[:, span], 0.0))
                    systems.append(jnp.where(cols < rows, rate[span] * fade * alike[b], 0.0))
                fade = jnp.exp(jnp.minimum(col[half:] - row[:, :half], 0.0))
                crosses.append(rate[half:] * fade * alike[2])
        solved = inverses(systems)
        left = [packed_left(split(x)) for x in solved]
        middle = [
            mul(cross, solved[2 * j]) for j, cross in enumerate(crosses)
        ]
        corner = [
            -fold(left[2 * j + 1], packed_right(split(m))) for j, m in enumerate(middle)
        ]
        keep = sp_ref[1].astype(F32)
        eye = (lax.broadcasted_iota(jnp.int32, (HEAD, HEAD), 0)
               == lax.broadcasted_iota(jnp.int32, (HEAD, HEAD), 1)).astype(F32)
        for j in range(number):
            key = keys[j // 2]
            row, col, rate = sums[j : j + 1], sums_col[:, j : j + 1], beta_col[:, j : j + 1]
            side = split(corner[j])
            for which, part in enumerate((left[2 * j], left[2 * j + 1], packed_left(side))):
                solve_ref[j, which] = part
            trailing = turned[j // 2] * jnp.exp(row[:, count - 1 :] - row)
            low, high = [packed_left(split(t)) for t in (trailing[:, :half], trailing[:, half:])]
            taken = (
                fold(low, packed_right(split(solved[2 * j]))) + fold(high, packed_right(side)),
                fold(high, packed_right(split(solved[2 * j + 1]))),
            )
            right = (rate * jnp.exp(col)) * key
            moved = None
            for part, span in zip(taken, (slice(0, half), slice(half, count))):
                part = packed_left(split(part))
                gather_ref[j, 0 if span.start == 0 else 1] = part
                once = right[span].astype(BF16)
                term = plain(part, jnp.concatenate([once, once], axis=0))
                moved = term if moved is None else moved + term
            gone = jnp.exp(row[:, count - 1 :])
            trans_ref[j] = keep * (gone * eye - moved)

    return call(
        body, sp, inputs, specs, outs, 5.0, [pltpu.VMEM((RIM + count, HEAD), F32)], after=after,
    )


def value_phase(gathered, number, count, tables, gathers, trans, sp, place, after=()):
    inputs, specs, jobs = gathered
    received = (len(inputs) - 2) // len(jobs) - 2
    at = len(inputs)
    inputs = inputs + tables + [gathers, trans]
    specs = specs + [whole(a) for a in inputs[at:]]
    half = count // 2
    outs = [
        jax.ShapeDtypeStruct((number, count, HEAD), F32),
        jax.ShapeDtypeStruct((2, number // 2, HEAD, HEAD), BF16),
        jax.ShapeDtypeStruct((2, number // 2, HEAD, HEAD), BF16),
    ]
    total = len(inputs)

    def body(sp_ref, *refs):
        write_ref, keep_ref, give_ref, scratch = refs[total:]
        beta_col = refs[at + 2][...]
        gather_ref, moved_ref = refs[at + 3 : at + 5]
        made = []
        for i, job in enumerate(jobs):
            values = activate(refs, job, received, scratch)
            for j in (2 * i, 2 * i + 1):
                right = beta_col[:, j : j + 1] * values[:, (j % 2) * HEAD : (j % 2 + 1) * HEAD]
                write_ref[j] = right
                low, high = [right[span].astype(BF16) for span in (slice(0, half), slice(half, count))]
                made.append(
                    plain(gather_ref[j, 0], jnp.concatenate([low, low], axis=0))
                    + plain(gather_ref[j, 1], jnp.concatenate([high, high], axis=0))
                )
        first = sp_ref[place] == 0
        for i in range(number // 2):
            k = i + number // 2
            for ref, mine in ((keep_ref, first), (give_ref, jnp.logical_not(first))):
                ref[0, i] = jnp.where(mine, moved_ref[i], moved_ref[k]).astype(BF16)
                ref[1, i] = jnp.where(mine, made[i], made[k]).astype(BF16)

    return call(
        body, sp, inputs, specs, outs, 0.05, [pltpu.VMEM((RIM + count, 2 * HEAD), F32)], after=after,
    )


def write_phase(right, keys, tables, solve, sp, after=()):
    number, count = right.shape[:2]
    half = count // 2
    inputs = [right, keys, *tables, solve]
    out = jax.ShapeDtypeStruct((number, count, 2 * HEAD), F32)

    def body(sp_ref, right_ref, key_ref, _, col_ref, rate_ref, solve_ref, out_ref):
        for j in range(number):
            col, rate = col_ref[:, j : j + 1], rate_ref[:, j : j + 1]
            both = jnp.concatenate([right_ref[j], (rate * jnp.exp(col)) * key_ref[j // 2]], axis=1)
            parts = []
            for span in (slice(0, half), slice(half, count)):
                high, low = split(both[span])
                parts.append((jnp.concatenate([high, high], axis=0), low))

            def solved(which, part):
                left = solve_ref[j, which]
                return plain(left, part[0]) + plain(left[:, :half], part[1])

            out_ref[j, :half] = solved(0, parts[0])
            out_ref[j, half:] = solved(2, parts[0]) + solved(1, parts[1])

    return call(body, sp, inputs, [whole(a) for a in inputs], [out], 0.05, after=after)[0]


def query_phase(gathered, number, count, tables, keys, writes, sp, after=()):
    inputs, specs, jobs = gathered
    received = (len(inputs) - 2) // len(jobs) - 2
    at = len(inputs)
    inputs = inputs + tables + [keys, writes]
    specs = specs + [whole(a) for a in inputs[at:]]
    half = count // 2
    outs = [
        jax.ShapeDtypeStruct((number, count, HEAD), F32),
        jax.ShapeDtypeStruct((number, count, HEAD), BF16),
    ]
    total = len(inputs)

    def body(sp_ref, *refs):
        inner_ref, query_ref, scratch = refs[total:]
        sums, sums_col = refs[at][...], refs[at + 1][...]
        rows, cols = iotas(half)
        low, high = slice(0, half), slice(half, count)
        for i, job in enumerate(jobs):
            key_ref, write_ref = refs[at + 3 : at + 5]
            query = unit_rows(activate(refs, job, received, scratch))
            key = key_ref[i]
            left = [packed_left(split(query[span])) for span in (low, high)]
            right = [packed_turned(split(key[span])) for span in (low, high)]
            alike = {
                (0, 0): fold(left[0], right[0], NT),
                (1, 1): fold(left[1], right[1], NT),
                (1, 0): fold(left[1], right[0], NT),
            }
            for j in (2 * i, 2 * i + 1):
                row, col = sums[j : j + 1], sums_col[:, j : j + 1]
                wrote = [split(write_ref[j, span]) for span in (low, high)]
                tall = [jnp.concatenate([w[0], w[0]], axis=0) for w in wrote]
                read = [None, None]
                for (t, s), product in alike.items():
                    fade = jnp.exp(
                        jnp.minimum(col[(low, high)[t]] - row[:, (low, high)[s]], 0.0)
                    )
                    attend = fade * product
                    if t == s:
                        attend = jnp.where(cols <= rows, attend, 0.0)
                    attend = split(attend)
                    part = jnp.dot(
                        packed_left(attend), tall[s], preferred_element_type=F32
                    ) + jnp.dot(attend[0], wrote[s][1], preferred_element_type=F32)
                    read[t] = part if read[t] is None else read[t] + part
                for t, span in enumerate((low, high)):
                    inner_ref[j, span] = read[t][:, :HEAD]
                    read_in = jnp.exp(col[span]) * query[span] - read[t][:, HEAD:]
                    query_ref[j, span] = read_in.astype(BF16)

    return call(
        body, sp, inputs, specs, outs, 3.7, [pltpu.VMEM((RIM + count, HEAD), F32)], after=after,
    )


def join_cores(mine, other, sp, place, after=()):
    half = mine.shape[1]
    outs = [
        jax.ShapeDtypeStruct((2, half, HEAD, HEAD), BF16),
        jax.ShapeDtypeStruct((half, HEAD, HEAD), BF16),
    ]

    def body(sp_ref, mine_ref, other_ref, both_ref, write_ref):
        first = sp_ref[place] == 0
        for i in range(half):
            held = [(mine_ref[k, i].astype(F32), other_ref[k, i].astype(F32)) for k in (0, 1)]
            early = [jnp.where(first, pair[0], pair[1]) for pair in held]
            late = [jnp.where(first, pair[1], pair[0]) for pair in held]
            left = late[0].astype(BF16)
            write = plain(left, early[1].astype(BF16)) + late[1]
            both_ref[0, i] = plain(left, early[0].astype(BF16)).astype(BF16)
            both_ref[1, i] = write.astype(BF16)
            write_ref[i] = write.astype(BF16)

    inputs = [mine, other]
    return call(body, sp, inputs, [whole(a) for a in inputs], outs, 0.05, after=after)


def pass_chip(joined, states, sp, after=()):
    half = states[0].shape[0]
    outs = [jax.ShapeDtypeStruct((half, HEAD, HEAD), BF16)] * 2
    inputs = [joined, *states]

    def body(sp_ref, joined_ref, *refs):
        for i in range(half):
            state = sum(ref[i].astype(F32) for ref in refs[:-2]).astype(BF16)
            stepped = plain(joined_ref[0, i], state)
            refs[-2][i] = (stepped + joined_ref[1, i].astype(F32)).astype(BF16)
            refs[-1][i] = state

    return call(body, sp, inputs, [whole(a) for a in inputs], outs, 0.05, after=after)


def shifted(value, steps):
    count = lax.axis_size("ctx")
    return lax.ppermute(value, "ctx", [(i, i + steps) for i in range(count - steps)])


def swapped(value):
    count = lax.axis_size("ctx")
    return lax.ppermute(value, "ctx", [(i, i ^ 1) for i in range(count)])


def enter_far(joined):
    chips = lax.axis_size("ctx") // 2
    joined = shifted(joined, 2)
    step = 1
    while step < chips:
        early = shifted(joined, 2 * step).astype(F32)
        late = joined.astype(F32)
        both = jnp.einsum("hij,xhjk->xhik", late[0], early, precision=lax.Precision.HIGHEST)
        joined = (both + late * jnp.array([0.0, 1.0], F32)[:, None, None, None]).astype(BF16)
        step *= 2
    return joined[1]


def finish(inner, query, mine, others, early, gain, sp, place):
    inputs = [inner, query, *early, gain, *mine, *others]
    number, count = inner.shape[:2]
    half = number // 2
    out = jax.ShapeDtypeStruct((count, number * HEAD), BF16)

    def body(sp_ref, inner_ref, query_ref, low_ref, high_ref, gain_ref, *refs):
        core = sp_ref[place]
        keep = sp_ref[1].astype(F32)
        for j in range(number):
            i, early_ref = j % half, (low_ref, high_ref)[j // half]
            own, far = [
                sum(ref[i].astype(F32) for ref in part)
                for part in (refs[: len(mine)], refs[len(mine) : 2 * len(mine)])
            ]
            state = jnp.where((core == 0) == (j < half), own, far)
            stepped = plain(early_ref[0, i], state.astype(BF16)) + early_ref[1, i].astype(F32)
            state = keep * jnp.where(core == 0, state, stepped)
            read = inner_ref[j] + plain(query_ref[j], state.astype(BF16))
            scale = lax.rsqrt(jnp.mean(read * read, axis=-1, keepdims=True) + EPS)
            cols = slice(j * HEAD, (j + 1) * HEAD)
            refs[-1][:, cols] = (read * scale * gain_ref[...]).astype(BF16)

    return call(body, sp, inputs, [whole(a) for a in inputs], [out], 2.7)[0]


def per_device(
    hidden,
    w_query,
    w_key,
    payload_projection_matrix,
    conv_weight,
    log_decay,
    beta_rate,
    norm_gain,
    head_order,
    block_starts,
):
    count = hidden.shape[0]
    ranks = lax.axis_size("head")
    chips = lax.axis_size("ctx") // 2
    total_heads = head_order.shape[0]
    key_heads = total_heads // ranks
    number = 2 * key_heads
    serve, spot = lax.axis_index("head"), lax.axis_index("ctx")
    keep = 1 - block_starts[0]
    place = 2 + total_heads
    w_value = payload_projection_matrix

    rows = w_key.shape[0]
    edge = lax.dynamic_slice(hidden, (count - RIM, serve * rows), (RIM, rows))
    rim = shifted(edge, 1) * keep.astype(BF16)
    hidden = lax.dynamic_slice(hidden, (0, serve * rows), (count, rows))
    sp = jnp.concatenate(
        [jnp.stack([serve, keep]), head_order, jnp.stack([spot % 2])]
    ).astype(jnp.int32)

    everyone = list(range(key_heads))
    halving = Halving(ranks, everyone)

    def gathered(width, weight, base, parts):
        return gather_specs(key_heads, width, hidden, rim, weight, conv_weight, base, parts)

    got_k = [[] for _ in halving.routes]
    part_k = halving.send(0, key_heads, HEAD, hidden, rim, w_key, got_k, sp)
    halving.exchange(0, part_k, got_k)
    tables = list(prepare(log_decay, beta_rate, sp, after=part_k[:1]))
    got_v = [[] for _ in halving.routes]
    part_v = halving.send(
        0, key_heads, 2 * HEAD, hidden, rim, w_value, got_v, sp, after=tables[:1]
    )
    halving.exchange(0, part_v, got_v)
    part_q = partial_sums(
        key_heads, ranks, everyone, HEAD, hidden, rim, w_query, sp, after=part_v[:1]
    )
    for stage in range(1, halving.stages):
        part_k = halving.send(
            stage, key_heads, HEAD, hidden, rim, w_key, got_k, sp, after=part_q[:1]
        )
        halving.exchange(stage, part_k, got_k)
    keys, solve, gathers, trans_a = key_phase(
        gathered(HEAD, w_key, total_heads, [halving.parts(h, HEAD, got_k) for h in everyone]),
        number, count, tables, sp, after=part_k[:1],
    )
    ordered = [trans_a]
    for stage in range(1, halving.stages):
        part_v = halving.send(
            stage, key_heads, 2 * HEAD, hidden, rim, w_value, got_v, sp, after=ordered
        )
        halving.exchange(stage, part_v, got_v)
        ordered = part_v[:1]
    part_q, _ = lax.optimization_barrier((part_q, ordered[0]))
    got_q = exchange(part_q)
    right, own, given = value_phase(
        gathered(
            2 * HEAD, w_value, total_heads,
            [halving.parts(h, 2 * HEAD, got_v) for h in everyone],
        ),
        number, count, tables, gathers, trans_a, sp, place, after=ordered,
    )
    taken = swapped(given)
    joined, joined_b = join_cores(own, taken, sp, place)
    states, last, writes = [], joined_b, None
    if chips <= 4:
        for chip in range(chips - 1):
            if chip:
                after = [] if writes is None else [writes]
                last, so_far = pass_chip(joined, states, sp, after)
                states = [so_far]
            hop = [(2 * chip + c, 2 * chip + 2 + c) for c in range(2)]
            states.append(lax.ppermute(last, "ctx", hop))
            if writes is None and chip + 1 >= min(2, chips - 1):
                writes = write_phase(right, keys, tables, solve, sp, after=[last])
    else:
        states = [enter_far(joined)]
    if writes is None:
        writes = write_phase(right, keys, tables, solve, sp, after=[last])
    inner, query = query_phase(
        gathered(HEAD, w_query, 0, [direct_parts(h, HEAD, got_q) for h in everyone]),
        number, count, tables, keys, writes, sp, after=[last],
    )
    own, _ = lax.optimization_barrier((own, joined))
    early = swapped(own)
    others = [swapped(state) for state in states[:-1]]
    final, _ = lax.optimization_barrier((states[-1], inner))
    return finish(
        inner, query, [*states[:-1], final], [*others, swapped(final)], (early, taken),
        norm_gain[None, :], sp, place,
    )


def solution(mesh):
    return jax.shard_map(
        per_device,
        mesh=mesh,
        in_specs=(
            P("ctx", None),
            P("head", None),
            P("head", None),
            P("head", None),
            P(),
            P("head", "ctx"),
            P("head", "ctx"),
            P(),
            P(),
            P("ctx"),
        ),
        out_specs=P("ctx", "head"),
        check_vma=False,
    )
```
